32 devices in a mesh: grp: 2 (over y), pencil: 4 (over z), depth: 2 (over x), mem: 2 (over core).
Axes of the slice: x: 2, y: 2, z: 4, core: 2. Of those that a mesh axis runs over, the one named last changes fastest.
Arguments:
- density: float32 [4, 2, 2048, 2048], P(('grp', 'mem'), 'depth', 'pencil'), parts along dimension 0, may hold values from -6 to 6
- background: float32 [8, 2], P(None, 'depth'), may hold values from -2 to 2
- member_ids: int32 [4], P(('grp', 'mem')), parts along dimension 0, may hold values from 0 to 7
- layer_kernel: int32 [2], P('depth'), may hold values from 0 to 3, as said below
- kernel_spectra: bfloat16 [4, 2, 2048, 2048], P('depth', None, None, 'pencil'), may hold values from -4 to 4
Outputs:
- gravity: float32 [4, 2048, 2048], P(('grp', 'mem'), ('pencil', 'depth')), parts along dimension 0
The draws below stay inside these ranges and needn't reach their ends.
There are 2 independent parts, one for each index of `grp`. The reference program is written for one: setup_inputs(seed, part) draws one part's arguments, and reference() takes and returns one part's arrays. A program takes and returns all parts, laid end to end along the dimension named above; an argument that names none is the same for every part. Nothing has to cross between parts.
Inputs may be any that keep to these rules, and one draw needn't show every extreme that they name: Layer l takes one of the 2 kernels of its depth band: layer_kernel[l] // 2 equals l.
All inputs are finite; a program needn't handle non-finite values.
Results may differ from the reference program's by a relative error of at most 0.0003.
Values sent between devices are 32-bit elements; how exact they have to be, the bound alone decides.
A program may use at most 128 MiB of HBM per device.

```python
import jax
import jax.numpy as jnp
from jax import lax

NX = 2048
NY = 2048
LAY_DEV = 1
K_DEV = 2
PROFILES = 8
LAYERS = 2
NK = 4
MEMBERS = 2


def draw_layer_kernel(key, part):
    key_offset = jax.random.fold_in(key, 17)
    positions = jnp.arange(LAYERS, dtype=jnp.int32)
    offsets = jax.random.randint(key_offset, (LAYERS,), 0, K_DEV).astype(jnp.int32)
    offsets = jnp.where(positions == 0, 0, offsets)
    offsets = jnp.where(positions == LAYERS - 1, K_DEV - 1, offsets)
    return (positions // LAY_DEV * K_DEV + offsets).astype(jnp.int32)


def levels(stream_key, extent, pieces, low, high):
    factor_of = 1.0
    for dim, parts in pieces:
        draws = jax.random.uniform(jax.random.fold_in(jax.random.fold_in(stream_key, 6), dim), (parts,), jnp.float32, low / len(pieces), high / len(pieces))
        factor_of = factor_of * jnp.repeat(jnp.exp(draws), extent[dim] // parts).reshape((-1,) + (1,) * (len(extent) - 1 - dim))
    return factor_of


def scatter_about(own_key, shape, scale, most, split=(), held_as=jnp.bfloat16):
    entries = scale * jax.random.normal(own_key, shape, jnp.float32)
    if split:
        entries = entries * levels(own_key, shape, split, -0.22, 0.18)
    return jnp.clip(entries, -most, most).astype(held_as)


def setup_inputs(seed: int = 0, part: int = 0) -> dict:
    splits = jax.random.split(jax.random.key(seed), 6)
    part_keys = jax.random.split(jax.random.fold_in(splits[5], part), 6)
    return {
        "density": scatter_about(part_keys[0], (MEMBERS, LAYERS, NX, NY), 1.0, 6.0, ((0, 2), (1, 2), (2, 4)), jnp.float32),
        "background": jnp.clip(jax.random.uniform(splits[1], (PROFILES, LAYERS), jnp.float32, -2.0, 2.0) * levels(splits[1], (PROFILES, LAYERS), ((1, 2),), -0.4, 0.0), -2.0, 2.0),
        "member_ids": jax.random.randint(part_keys[2], (MEMBERS,), 0, PROFILES).astype(jnp.int32),
        "layer_kernel": draw_layer_kernel(jax.random.fold_in(splits[5], 71), part),
        "kernel_spectra": scatter_about(splits[4], (NK, 2, NX, NY), LAYERS ** -0.5, 4.0, ((0, 2), (3, 4))),
    }


def storage_order(length):
    frequency = jnp.arange(length, dtype=jnp.int32)
    return (frequency % 16) * (length // 16) + frequency // 16


def reference(density, background, member_ids, layer_kernel, kernel_spectra):
    order_x = storage_order(NX)
    order_y = storage_order(NY)
    outputs = []
    for member in range(MEMBERS):
        offsets = background[member_ids[member]]
        total_real = jnp.zeros((NX, NY), jnp.float32)
        total_imag = jnp.zeros((NX, NY), jnp.float32)
        for layer_pos in range(LAYERS):
            contrast = density[member, layer_pos] - offsets[layer_pos]
            transformed = jnp.fft.fft2(contrast)
            trans_real = jnp.real(transformed)
            trans_imag = jnp.imag(transformed)
            stored = kernel_spectra[layer_kernel[layer_pos]].astype(jnp.float32)
            kern_real = stored[0][order_x][:, order_y]
            kern_imag = stored[1][order_x][:, order_y]
            total_real = total_real + trans_real * kern_real - trans_imag * kern_imag
            total_imag = total_imag + trans_real * kern_imag + trans_imag * kern_real
        gravity_field = jnp.fft.ifft2(lax.complex(total_real, total_imag))
        outputs.append(jnp.real(gravity_field))
    return jnp.stack(outputs)
```

```python
import functools
import math

import jax
import jax.numpy as jnp
import numpy as np
from jax import lax
from jax.experimental import pallas as pl
from jax.experimental.pallas import tpu as pltpu
from jax.sharding import PartitionSpec as P

RADIX = 16
INNER = 128
HALF = 64
LENGTH = RADIX * INNER
f32 = jnp.float32
bf16 = jnp.bfloat16


def halves(table):
    table = np.asarray(table, np.float32)
    high = table.astype(bf16)
    low = (table - high.astype(np.float32)).astype(bf16)
    return jnp.asarray(high), jnp.asarray(low)


def residue_rows(r):
    m = np.arange(INNER)[:, None]
    q = np.arange(HALF)[None, :]
    turn = np.exp(-2j * np.pi * (((RADIX * q + r) * m) % LENGTH) / LENGTH)
    re, im = turn.real.copy(), turn.imag.copy()
    if r == 0:
        im[:, 0] = (-1.0) ** m[:, 0]
    out = np.zeros((2 * INNER, 2 * HALF))
    if r == 0:
        out[:INNER, :HALF], out[:INNER, HALF:] = re, im
    elif r == 8:
        out[INNER:, :HALF], out[INNER:, HALF:] = re, im
    else:
        sign = 1.0 if r < 8 else -1.0
        out[:INNER, :HALF], out[:INNER, HALF:] = re, im
        out[INNER:, :HALF], out[INNER:, HALF:] = -sign * im, sign * re
    return out


def slot_of(r):
    return 0 if r in (0, 8) else min(r, RADIX - r)


def row_tables():
    tables = np.zeros((8, 512, 256))
    for t in range(8):
        for odd in range(2):
            block = residue_rows(2 * t + odd)
            rows = slice(256 * odd, 256 * odd + 256)
            tables[t, rows, HALF * odd : HALF * odd + HALF] = block[:, :HALF]
            tables[t, rows, 128 + HALF * odd : 128 + HALF * odd + HALF] = block[:, HALF:]
    return tables


def inverse_row_tables():
    tables = np.zeros((8, 512, 256))
    scale = 1.0 / (LENGTH * LENGTH)
    for s in range(8):
        for place, r in enumerate((s, 8 if s == 0 else RADIX - s)):
            block = residue_rows(r).T.copy() * scale
            weight = np.full((2 * HALF, 1), 2.0 if r in (0, 8) else 1.0)
            if r == 0:
                weight[0] = weight[HALF] = 1.0
            block *= weight
            odd = r % 2
            tables[s, 256 * place + HALF * odd : 256 * place + HALF * odd + HALF] += block[:HALF]
            tables[s, 256 * place + 128 + HALF * odd : 256 * place + 128 + HALF * odd + HALF] += block[HALF:]
    return tables


def column_tables():
    q = np.arange(INNER)[:, None]
    m = np.arange(INNER)[None, :]
    turn = np.exp(-2j * np.pi * ((q * m) % INNER) / INNER)
    table = np.block([[turn.real, -turn.imag], [turn.imag, turn.real]])
    angles = 2 * np.pi * np.arange(RADIX)[:, None] * np.arange(INNER)[None, :] / LENGTH
    turns = np.zeros((RADIX, INNER, INNER), np.float32)
    turns[..., 0] = np.cos(angles)
    turns[..., 1] = np.sin(angles)
    return table, turns


def split_value(value):
    high = value.astype(bf16)
    return high, (value - high.astype(f32)).astype(bf16)


def dot(a, b):
    return jnp.dot(a, b, preferred_element_type=f32)


def rotate(value, count, length, sign):
    re, im = value
    count %= length
    if count == 0:
        return value
    if 4 * count == length:
        return (im, -re) if sign < 0 else (-im, re)
    c = math.cos(2 * math.pi * count / length)
    s = sign * math.sin(2 * math.pi * count / length)
    if 8 * count == length:
        return ((re + im) * c, (im - re) * c) if sign < 0 else ((re - im) * c, (im + re) * c)
    return (re * c - im * s, re * s + im * c)


def plus(a, b):
    return (a[0] + b[0], a[1] + b[1])


def minus(a, b):
    return (a[0] - b[0], a[1] - b[1])


def transform(values, sign):
    length = len(values)
    if length == 1:
        return values
    even, odd = transform(values[0::2], sign), transform(values[1::2], sign)
    turned = [rotate(odd[k], k, length, sign) for k in range(length // 2)]
    return [plus(even[k], turned[k]) for k in range(length // 2)] + [
        minus(even[k], turned[k]) for k in range(length // 2)
    ]


def real_transform(values):
    length = len(values)
    if length == 2:
        return [(values[0] + values[1], None), (values[0] - values[1], None)]
    even, odd = real_transform(values[0::2]), real_transform(values[1::2])
    out = [None] * (length // 2 + 1)
    out[0] = (even[0][0] + odd[0][0], None)
    out[length // 2] = (even[0][0] - odd[0][0], None)
    quarter = length // 4
    for k in range(1, quarter):
        turned = rotate(odd[k], k, length, -1)
        out[k] = plus(even[k], turned)
        low = minus(even[k], turned)
        out[length // 2 - k] = (low[0], -low[1])
    out[quarter] = (even[quarter][0], -odd[quarter][0])
    return out


def real_inverse(values):
    half = len(values) - 1
    length = 2 * half
    if length == 2:
        return [values[0][0] + values[1][0], values[0][0] - values[1][0]]
    even, odd = [], []
    for k in range(half // 2 + 1):
        if k == 0:
            even.append((values[0][0] + values[half][0], None))
            odd.append((values[0][0] - values[half][0], None))
        elif k == half // 2:
            even.append((2.0 * values[k][0], None))
            odd.append((-2.0 * values[k][1], None))
        else:
            other = values[half - k]
            even.append((values[k][0] + other[0], values[k][1] - other[1]))
            odd.append(rotate((values[k][0] - other[0], values[k][1] + other[1]), k, length, 1))
    first, second = real_inverse(even), real_inverse(odd)
    return [x for pair in zip(first, second) for x in pair]


def rows_kernel(pencils, width, offset_ref, in_ref, high_ref, low_ref, *rest):
    outs, pieces = rest[:-1], rest[-1]
    rows = in_ref.shape[0]
    per = RADIX // pencils
    offset = offset_ref[0]

    def step(b, carry):
        at = pl.ds(pl.multiple_of(b * 8, 8), 8)
        values = [in_ref[at, n * INNER : (n + 1) * INNER] - offset for n in range(RADIX)]
        got = real_transform(values)
        pieces[0, at, :INNER] = got[0][0]
        pieces[0, at, INNER:] = got[8][0]
        for s in range(1, 8):
            pieces[s, at, :INNER] = got[s][0]
            pieces[s, at, INNER:] = got[s][1]
        return carry

    lax.fori_loop(0, rows // 8, step, 0)
    for t in range(8):
        total = None
        for odd in range(2):
            high, low = split_value(pieces[slot_of(2 * t + odd)])
            table_high = high_ref[t, 256 * odd : 256 * odd + 256]
            table_low = low_ref[t, 256 * odd : 256 * odd + 256]
            part = dot(high, table_high) + dot(low, table_high) + dot(high, table_low)
            total = part if total is None else total + part
        if width == 2:
            pencil, place = divmod(2 * t, per)
            for c in range(2):
                outs[place // 2][pencil, c] = total[:, c * 128 : (c + 1) * 128]
        else:
            for odd in range(2):
                pencil, place = divmod(2 * t + odd, per)
                for c in range(2):
                    begin = c * 128 + odd * HALF
                    outs[place][pencil, c] = total[:, begin : begin + HALF]


def swapped(zero, shape, axis):
    total = lax.broadcasted_iota(jnp.int32, shape, 0) + lax.broadcasted_iota(jnp.int32, shape, 1)
    wanted = jnp.where(zero, INNER, INNER - 1)
    also = jnp.where(zero, 0, INNER - 1)
    return jnp.where((total == wanted) | (total == also), 1.0, 0.0).astype(bf16)


def mirror_kernel(share, where_ref, *refs):
    ins, zero_ref, rest_refs = refs[:share], refs[share], refs[share + 1 :]
    per = ins[0].shape[2] // INNER
    plain = swapped(where_ref[1] < 0, (INNER, HALF), 1)
    edge = swapped(where_ref[2] == 0, (INNER, HALF), 1)
    for u in range(share):
        swap = swapped(where_ref[1] + u == 0, (INNER, INNER), 0)
        rows = [dot(swap, ins[u][c]).astype(bf16) for c in range(2)]
        for j in range(per):
            turn = edge if j == 0 else plain
            turned = [dot(rows[c][:, j * INNER : (j + 1) * INNER], turn) for c in range(2)]
            value = jnp.concatenate(turned, axis=1)
            if j == 0:
                zero_ref[0, u] = value
            else:
                rest_refs[0][per - 1 - j, u] = value


def columns_kernel(special, where_ref, in_ref, kern_ref, mirror_ref, edge_ref,
                   turns_ref, late_ref, table_ref, out_ref, pieces, waves):
    part_rows = in_ref.shape[2]
    depths, pencils, _, out_rows, lanes = out_ref.shape
    share = mirror_ref.shape[1]
    steps = RADIX // share
    mine = where_ref[0]
    now = pl.program_id(0)
    from_lane = lax.broadcasted_iota(jnp.int32, (kern_ref.shape[2], lanes), 0)
    to_lane = lax.broadcasted_iota(jnp.int32, (kern_ref.shape[2], lanes), 1)
    wanted = to_lane + jnp.where(to_lane < HALF, 0, HALF)
    pick = jnp.where(from_lane == wanted, 0.5, 0.0).astype(bf16)
    zero_swap = swapped(mine >= 0, (INNER, INNER), 0)
    plain_swap = swapped(mine < 0, (INNER, INNER), 0)

    def forward(b, carry):
        values = []
        for n in range(RADIX):
            source, begin = divmod(n * INNER, part_rows)
            at = pl.ds(pl.multiple_of(begin + b * 8, 8), 8)
            values.append((in_ref[source, 0, at, :], in_ref[source, 1, at, :]))
        at = pl.ds(pl.multiple_of(b * 8, 8), 8)
        also = pl.ds(pl.multiple_of(INNER + b * 8, 8), 8)
        for r, (re, im) in enumerate(transform(values, -1)):
            pieces[r, at, :] = re
            pieces[r, also, :] = im
        return carry

    @pl.when(now == 0)
    def _():
        lax.fori_loop(0, INNER // 8, forward, 0)

    def wave(r, u):
        re, im = pieces[r, :INNER], pieces[r, INNER:]
        c, s = turns_ref[u, :, 0:1], turns_ref[u, :, 1:2]
        high, low = split_value(jnp.concatenate([re * c + im * s, im * c - re * s], axis=0))
        return dot(table_ref[0], high) + dot(table_ref[0], low) + dot(table_ref[1], high)

    def finish(r, u, got):
        re, im = got[:INNER], got[INNER:]
        tiles = [mirror_ref[j, u] for j in range(mirror_ref.shape[0])]
        rows = slice(u * INNER, (u + 1) * INNER)
        parts = []
        for c in range(2):
            other = [tile[:, c * HALF : (c + 1) * HALF] for tile in tiles]
            other = jnp.concatenate(other, axis=1) if len(other) > 1 else other[0]
            own = dot(kern_ref[c, rows, :], pick)
            parts.append(own + 0.5 * other if c == 0 else own - 0.5 * other)
        kr, ki = parts
        if special:
            other = lax.rem(RADIX - r, RADIX)
            high, low = split_value(waves[other])
            swap = jnp.where(r == 0, zero_swap.astype(f32), plain_swap.astype(f32)).astype(bf16) if u == 0 else plain_swap
            ore = dot(swap, high[:INNER]) + dot(swap, low[:INNER])
            oim = -(dot(swap, high[INNER:]) + dot(swap, low[INNER:]))
            mask = (lax.broadcasted_iota(jnp.int32, (INNER, lanes), 1) == 0) & (where_ref[2] == 0)
            hr = jnp.where(mask, 0.5 * (kr - edge_ref[0, u]), 0.0)
            hi = jnp.where(mask, 0.5 * (ki - edge_ref[1, u]), 0.0)
            kr, ki = kr - hr, ki - hi
            sr = re * kr - im * ki + (ore * hr - oim * hi)
            si = re * ki + im * kr + (ore * hi + oim * hr)
        else:
            sr, si = re * kr - im * ki, re * ki + im * kr
        spectrum = jnp.concatenate([sr, si], axis=0)
        high, low = split_value(spectrum)
        got = dot(table_ref[2], high) + dot(table_ref[2], low) + dot(table_ref[3], high)
        re, im = got[:INNER], got[INNER:]
        c, s = late_ref[u, :, 0:1], late_ref[u, :, 1:2]
        pieces[r, :INNER] = re * c - im * s
        pieces[r, INNER:] = im * c + re * s

    if special:
        @pl.when(now < steps)
        def _():
            for u in range(share):
                waves[now * share + u] = wave(now * share + u, u)

        @pl.when(now >= steps)
        def _():
            for u in range(share):
                r = (now - steps) * share + u
                finish(r, u, waves[r])
    else:
        for u in range(share):
            r = now * share + u
            finish(r, u, wave(r, u))

    slots = [lax.rem(d - mine + depths, depths) for d in range(depths)]

    def backward(b, carry):
        at = pl.ds(pl.multiple_of(b * 8, 8), 8)
        also = pl.ds(pl.multiple_of(INNER + b * 8, 8), 8)
        values = [(pieces[r, at, :], pieces[r, also, :]) for r in range(RADIX)]
        for n, (re, im) in enumerate(transform(values, 1)):
            if out_rows % INNER == 0:
                part, begin = divmod(n * INNER, out_rows)
                pencil, depth = divmod(part, depths)
                depth = slots[depth]
                put = pl.ds(pl.multiple_of(begin + b * 8, 8), 8)
            else:
                x = n * INNER + b * 8
                pencil = x // (out_rows * depths)
                depth = lax.rem(x // out_rows - mine + depths, depths)
                put = pl.ds(pl.multiple_of(lax.rem(x, out_rows), 8), 8)
            out_ref[depth, pencil, 0, put, :] = re
            out_ref[depth, pencil, 1, put, :] = im
        return carry

    @pl.when(now == pl.num_programs(0) - 1)
    def _():
        lax.fori_loop(0, INNER // 8, backward, 0)


def fields_kernel(pencils, width, counts, *refs):
    ins, at = [], 0
    for count in counts:
        ins.append(refs[at : at + count])
        at += count
    high_ref, low_ref, out_ref, pieces = refs[at:]
    per = RADIX // pencils
    rows = out_ref.shape[1]

    def read(chunk, pencil, c):
        found = [ref[pencil, c] for ref in ins[chunk]]
        return jnp.concatenate(found, axis=0) if len(found) > 1 else found[0]

    def pair(t):
        if width == 2:
            pencil, place = divmod(2 * t, per)
            return jnp.concatenate([read(place // 2, pencil, c) for c in range(2)], axis=1)
        found = []
        for c in range(2):
            for odd in range(2):
                pencil, place = divmod(2 * t + odd, per)
                found.append(read(place, pencil, c))
        return jnp.concatenate(found, axis=1)

    for s in range(8):
        total = None
        for place, r in enumerate((s, 8 if s == 0 else RADIX - s)):
            high, low = split_value(pair(r // 2))
            table_high = high_ref[s, 256 * place : 256 * place + 256]
            table_low = low_ref[s, 256 * place : 256 * place + 256]
            part = dot(high, table_high) + dot(low, table_high) + dot(high, table_low)
            total = part if total is None else total + part
        pieces[s] = total

    def step(b, carry):
        at = pl.ds(pl.multiple_of(b * 8, 8), 8)
        values = [(pieces[0, at, :INNER], None)]
        for s in range(1, 8):
            values.append((pieces[s, at, :INNER], pieces[s, at, INNER:]))
        values.append((pieces[0, at, INNER:], None))
        for n, value in enumerate(real_inverse(values)):
            out_ref[0, at, n * INNER : (n + 1) * INNER] = value
        return carry

    lax.fori_loop(0, rows // 8, step, 0)


def slot_at(r):
    return jnp.where(r == 8, 0, jnp.minimum(r, RADIX - r))


def shift_rows_kernel(pencils, offset_ref, where_ref, in_ref, high_ref, low_ref, *rest):
    outs, pieces = rest[:-1], rest[-1]
    rows = in_ref.shape[0]
    chunks = RADIX // pencils // 2
    offset = offset_ref[0]
    mine = where_ref[0]

    def step(b, carry):
        at = pl.ds(pl.multiple_of(b * 8, 8), 8)
        values = [in_ref[at, n * INNER : (n + 1) * INNER] - offset for n in range(RADIX)]
        got = real_transform(values)
        pieces[0, at, :INNER] = got[0][0]
        pieces[0, at, INNER:] = got[8][0]
        for s in range(1, 8):
            pieces[s, at, :INNER] = got[s][0]
            pieces[s, at, INNER:] = got[s][1]
        return carry

    lax.fori_loop(0, rows // 8, step, 0)
    for shift in range(pencils):
        for chunk in range(chunks):
            t = lax.rem(mine + shift, pencils) * chunks + chunk
            total = None
            for odd in range(2):
                high, low = split_value(pieces[slot_at(2 * t + odd)])
                table_high = high_ref[t, 256 * odd : 256 * odd + 256]
                table_low = low_ref[t, 256 * odd : 256 * odd + 256]
                part = dot(high, table_high) + dot(low, table_high) + dot(high, table_low)
                total = part if total is None else total + part
            for c in range(2):
                outs[chunk * pencils + shift][c] = total[:, c * 128 : (c + 1) * 128]


def shift_columns_kernel(special, pencils, depths, where_ref, *refs):
    ins, refs = refs[:pencils], refs[pencils:]
    phase_ref, kern_ref, mirror_ref, edge_ref, turns_ref, late_ref, table_ref = refs[:7]
    outs, (pieces, waves) = refs[7:-2], refs[-2:]
    part_rows = ins[0].shape[1]
    out_rows, lanes = outs[0].shape[1:]
    share = mirror_ref.shape[1]
    steps = RADIX // share
    mine = where_ref[0]
    now = pl.program_id(0)
    from_lane = lax.broadcasted_iota(jnp.int32, (kern_ref.shape[2], lanes), 0)
    to_lane = lax.broadcasted_iota(jnp.int32, (kern_ref.shape[2], lanes), 1)
    wanted = to_lane + jnp.where(to_lane < HALF, 0, HALF)
    pick = jnp.where(from_lane == wanted, 0.5, 0.0).astype(bf16)
    zero_swap = swapped(mine >= 0, (INNER, INNER), 0)
    plain_swap = swapped(mine < 0, (INNER, INNER), 0)

    def forward(b, carry):
        values = []
        for n in range(RADIX):
            source, begin = divmod(n * INNER, part_rows)
            at = pl.ds(pl.multiple_of(begin + b * 8, 8), 8)
            values.append((ins[source][0, at, :], ins[source][1, at, :]))
        at = pl.ds(pl.multiple_of(b * 8, 8), 8)
        also = pl.ds(pl.multiple_of(INNER + b * 8, 8), 8)
        for r, (re, im) in enumerate(transform(values, -1)):
            pieces[r, at, :] = re
            pieces[r, also, :] = im
        return carry

    @pl.when(now == 0)
    def _():
        lax.fori_loop(0, INNER // 8, forward, 0)

    def turn(ref, r, u):
        c, s = ref[u, :, 0:1], ref[u, :, 1:2]
        pc, ps = phase_ref[r, 0], phase_ref[r, 1]
        return c * pc - s * ps, s * pc + c * ps

    def wave(r, u):
        re, im = pieces[r, :INNER], pieces[r, INNER:]
        c, s = turn(turns_ref, r, u)
        high, low = split_value(jnp.concatenate([re * c + im * s, im * c - re * s], axis=0))
        return dot(table_ref[0], high) + dot(table_ref[0], low) + dot(table_ref[1], high)

    def finish(r, u, got):
        re, im = got[:INNER], got[INNER:]
        tiles = [mirror_ref[j, u] for j in range(mirror_ref.shape[0])]
        rows = slice(u * INNER, (u + 1) * INNER)
        parts = []
        for c in range(2):
            other = [tile[:, c * HALF : (c + 1) * HALF] for tile in tiles]
            other = jnp.concatenate(other, axis=1)
            own = dot(kern_ref[c, rows, :], pick)
            parts.append(own + 0.5 * other if c == 0 else own - 0.5 * other)
        kr, ki = parts
        if special:
            other = lax.rem(RADIX - r, RADIX)
            high, low = split_value(waves[other])
            swap = jnp.where(r == 0, zero_swap.astype(f32), plain_swap.astype(f32)).astype(bf16) if u == 0 else plain_swap
            ore = dot(swap, high[:INNER]) + dot(swap, low[:INNER])
            oim = -(dot(swap, high[INNER:]) + dot(swap, low[INNER:]))
            mask = (lax.broadcasted_iota(jnp.int32, (INNER, lanes), 1) == 0) & (where_ref[2] == 0)
            hr = jnp.where(mask, 0.5 * (kr - edge_ref[0, u]), 0.0)
            hi = jnp.where(mask, 0.5 * (ki - edge_ref[1, u]), 0.0)
            kr, ki = kr - hr, ki - hi
            sr = re * kr - im * ki + (ore * hr - oim * hi)
            si = re * ki + im * kr + (ore * hi + oim * hr)
        else:
            sr, si = re * kr - im * ki, re * ki + im * kr
        spectrum = jnp.concatenate([sr, si], axis=0)
        high, low = split_value(spectrum)
        got = dot(table_ref[2], high) + dot(table_ref[2], low) + dot(table_ref[3], high)
        re, im = got[:INNER], got[INNER:]
        c, s = turn(late_ref, r, u)
        pieces[r, :INNER] = re * c - im * s
        pieces[r, INNER:] = im * c + re * s

    if special:
        @pl.when(now < steps)
        def _():
            for u in range(share):
                waves[now * share + u] = wave(now * share + u, u)

        @pl.when(now >= steps)
        def _():
            for u in range(share):
                r = (now - steps) * share + u
                finish(r, u, waves[r])
    else:
        for u in range(share):
            r = now * share + u
            finish(r, u, wave(r, u))

    def backward(owner, b, carry):
        at = pl.ds(pl.multiple_of(b * 8, 8), 8)
        also = pl.ds(pl.multiple_of(INNER + b * 8, 8), 8)
        values = [(pieces[r, at, :], pieces[r, also, :]) for r in range(RADIX)]
        for n, (re, im) in enumerate(transform(values, 1)):
            part, begin = divmod(n * INNER, out_rows)
            shift, depth = divmod(part, depths)
            put = pl.ds(pl.multiple_of(begin + b * 8, 8), 8)
            out_ref = outs[(depth - owner) % depths * pencils + shift]
            out_ref[0, put, :] = re
            out_ref[1, put, :] = im
        return carry

    for owner in range(depths):
        @pl.when((now == pl.num_programs(0) - 1) & (mine == owner))
        def _(owner=owner):
            lax.fori_loop(0, INNER // 8, functools.partial(backward, owner), 0)


def shift_fields_kernel(pencils, chunks, where_ref, *refs):
    ins, at = [], 0
    for chunk in range(chunks):
        for shift in range(pencils):
            count = 2 if shift == 0 else 1
            ins.append((chunk, shift, refs[at : at + count]))
            at += count
    high_ref, low_ref, out_ref, pieces = refs[at:]
    rows = out_ref.shape[1]
    mine = where_ref[0]
    pieces[...] = jnp.zeros_like(pieces)
    for chunk, shift, found in ins:
        t = lax.rem(mine + pencils - shift, pencils) * chunks + chunk
        value = [found[0][c] if len(found) == 1 else found[0][c] + found[1][c] for c in range(2)]
        high, low = split_value(jnp.concatenate(value, axis=1))
        for odd in range(2):
            r = 2 * t + odd
            slot = slot_at(r)
            pieces[slot] += dot(high, high_ref[r]) + dot(low, high_ref[r]) + dot(high, low_ref[r])

    def step(b, carry):
        at = pl.ds(pl.multiple_of(b * 8, 8), 8)
        values = [(pieces[0, at, :INNER], None)]
        for s in range(1, 8):
            values.append((pieces[s, at, :INNER], pieces[s, at, INNER:]))
        values.append((pieces[0, at, INNER:], None))
        for n, value in enumerate(real_inverse(values)):
            out_ref[0, at, n * INNER : (n + 1) * INNER] = value
        return carry

    lax.fori_loop(0, rows // 8, step, 0)


def params(**more):
    return pltpu.CompilerParams(vmem_limit_bytes=48 * 1024 * 1024, **more)


def wide_body(density, background, member_ids, layer_kernel, kernel_spectra):
    pencils = lax.axis_size("pencil")
    depths = lax.axis_size("depth")
    sharers = lax.axis_size("grp") * lax.axis_size("mem")
    pencil = lax.axis_index("pencil")
    per = RADIX // pencils
    width = min(per, 2)
    chunks = per // width
    lanes = width * HALF
    part_rows = density.shape[2]
    out_rows = part_rows // depths
    vmem = pl.BlockSpec(memory_space=pltpu.VMEM)
    smem = pl.BlockSpec(memory_space=pltpu.SMEM)

    kern_count = kernel_spectra.shape[0]
    local = layer_kernel[0] - lax.axis_index("depth") * kern_count
    share = RADIX // sharers
    first = lax.axis_index(("grp", "mem")) * share
    groups = [1] if per == 1 else [1, per - 1]
    moved = pl.pallas_call(
        functools.partial(mirror_kernel, share),
        grid_spec=pltpu.PrefetchScalarGridSpec(
            num_scalar_prefetch=1,
            grid=(1,),
            in_specs=[
                pl.BlockSpec(
                    (None, 2, INNER, per * INNER),
                    lambda i, w, u=u: (w[0], 0, lax.rem(RADIX - w[1] - u, RADIX), 0),
                )
                for u in range(share)
            ],
            out_specs=[pl.BlockSpec((g, share, INNER, INNER), lambda i, w: (0, 0, 0, 0)) for g in groups],
        ),
        out_shape=[jax.ShapeDtypeStruct((g, share, INNER, INNER), f32) for g in groups],
        compiler_params=params(),
        cost_estimate=pl.CostEstimate(flops=1 << 20, bytes_accessed=2 << 20, transcendentals=0),
    )(jnp.stack([local, first, pencil]), *[kernel_spectra] * share)
    mirrored = lax.ppermute(moved[0], "pencil", [(p, (pencils - p) % pencils) for p in range(pencils)])
    if per > 1:
        rest = lax.ppermute(moved[1], "pencil", [(p, pencils - 1 - p) for p in range(pencils)])

    offset = lax.dynamic_index_in_dim(background[:, 0], member_ids[0], 0, keepdims=True)
    row_high, row_low = halves(row_tables())
    block = min(part_rows, 128)
    sent = pl.pallas_call(
        functools.partial(rows_kernel, pencils, width),
        grid=(part_rows // block,),
        in_specs=[
            smem,
            pl.BlockSpec((None, None, block, LENGTH), lambda i: (0, 0, i, 0)),
            pl.BlockSpec((8, 512, 256), lambda i: (0, 0, 0)),
            pl.BlockSpec((8, 512, 256), lambda i: (0, 0, 0)),
        ],
        out_specs=[pl.BlockSpec((pencils, 2, block, lanes), lambda i: (0, 0, i, 0))] * chunks,
        out_shape=[jax.ShapeDtypeStruct((pencils, 2, part_rows, lanes), f32)] * chunks,
        scratch_shapes=[pltpu.VMEM((8, block, 256), f32)],
        compiler_params=params(),
        cost_estimate=pl.CostEstimate(flops=6 * part_rows * 2 * LENGTH * 512, bytes_accessed=12 << 20, transcendentals=0),
    )(offset, density, row_high, row_low)
    arrived = [lax.all_to_all(part, "pencil", 0, 0, tiled=True) for part in sent]

    sign = jnp.array([0.5, -0.5], f32)
    edge = lax.dynamic_slice(kernel_spectra, (local, 0, 0, HALF), (1, 2, LENGTH, 1))
    edge = edge.reshape(2, RADIX, INNER).astype(f32)
    flipped = jnp.concatenate([edge[:, :1], edge[:, :0:-1]], axis=1)[..., ::-1]
    flipped = jnp.concatenate([jnp.roll(flipped[:, :1], 1, axis=2), flipped[:, 1:]], axis=1)
    edge = 0.5 * edge + sign.reshape(2, 1, 1) * flipped
    edge = jnp.where(lax.broadcasted_iota(jnp.int32, (lanes,), 0) == 0, edge[..., None], 0.0)

    if per > 1:
        mirrored = jnp.concatenate([mirrored, rest], axis=0)
    mirrored, edge, _ = lax.optimization_barrier((mirrored, edge, sent[0]))
    mirrored = lax.all_gather(mirrored, ("grp", "mem"), axis=0)

    column, column_turns = column_tables()
    column_turns = jnp.asarray(column_turns)
    tables = jnp.stack(halves(column) + halves(column.T))
    two = depths == 2
    mine = lax.axis_index("depth") if two else jnp.int32(0)
    where = jnp.stack([mine, local, pencil])
    fields = []
    before = None
    for k in range(chunks):
        special = k == 0
        steps = sharers

        def early(i, special=special):
            return jnp.minimum(i, steps - 1) if special else i

        def late(i, special=special):
            return jnp.maximum(i - steps, 0) if special else i

        here = arrived[k]
        if before is not None:
            here, before = lax.optimization_barrier((here, before))
            fields.append(lax.all_to_all(before, "pencil", 0, 0, tiled=True))
        edge_block = (2, share, INNER, lanes) if special else (2, 1, 8, lanes)
        out = pl.pallas_call(
            functools.partial(columns_kernel, special),
            grid_spec=pltpu.PrefetchScalarGridSpec(
                num_scalar_prefetch=1,
                grid=(2 * steps if special else steps,),
                in_specs=[
                    pl.BlockSpec((pencils, 2, part_rows, lanes), lambda i, w: (0, 0, 0, 0)),
                    pl.BlockSpec(
                        (None, 2, share * INNER, width * INNER), lambda i, w, k=k, late=late: (w[1], 0, late(i), k)
                    ),
                    pl.BlockSpec(
                        (None, width, share, INNER, INNER), lambda i, w, k=k, late=late: (late(i), k, 0, 0, 0)
                    ),
                    pl.BlockSpec(
                        edge_block,
                        (lambda i, w, late=late: (0, late(i), 0, 0)) if special else (lambda i, w: (0, 0, 0, 0)),
                    ),
                ]
                + [pl.BlockSpec((share, INNER, INNER), lambda i, w, early=early: (early(i), 0, 0))]
                + [pl.BlockSpec((share, INNER, INNER), lambda i, w, late=late: (late(i), 0, 0))]
                + [pl.BlockSpec((4, 256, 256), lambda i, w: (0, 0, 0))],
                out_specs=pl.BlockSpec((depths, pencils, 2, out_rows, lanes), lambda i, w: (0, 0, 0, 0, 0)),
                scratch_shapes=[
                    pltpu.VMEM((RADIX, 256, lanes), f32),
                    pltpu.VMEM((RADIX if special else 1, 256, lanes), f32),
                ],
            ),
            out_shape=jax.ShapeDtypeStruct((depths, pencils, 2, out_rows, lanes), f32),
            compiler_params=params(),
            cost_estimate=pl.CostEstimate(
                flops=12 * RADIX * 256 * 256 * lanes, bytes_accessed=16 << 20, transcendentals=0
            ),
        )(where, here, kernel_spectra, mirrored, edge, column_turns, column_turns, tables)
        if two:
            before = out[0] + lax.ppermute(out[1], "depth", [(0, 1), (1, 0)])
        else:
            before = lax.psum_scatter(out, "depth", scatter_dimension=0, tiled=False)
    fields.append(lax.all_to_all(before, "pencil", 0, 0, tiled=True))

    back_high, back_low = halves(inverse_row_tables())
    return pl.pallas_call(
        functools.partial(fields_kernel, pencils, width, [1] * chunks),
        in_specs=[vmem] * (len(fields) + 2),
        out_specs=vmem,
        out_shape=jax.ShapeDtypeStruct((1, out_rows, LENGTH), f32),
        scratch_shapes=[pltpu.VMEM((8, out_rows, 256), f32)],
        compiler_params=params(),
        cost_estimate=pl.CostEstimate(flops=6 * out_rows * 2 * LENGTH * 512, bytes_accessed=8 << 20, transcendentals=0),
    )(*fields, back_high, back_low)


def shift_body(density, background, member_ids, layer_kernel, kernel_spectra):
    pencils = lax.axis_size("pencil")
    depths = lax.axis_size("depth")
    sharers = lax.axis_size("grp") * lax.axis_size("mem")
    pencil = lax.axis_index("pencil")
    per = RADIX // pencils
    chunks = per // 2
    lanes = 2 * HALF
    part_rows = density.shape[2]
    out_rows = part_rows // depths
    vmem = pl.BlockSpec(memory_space=pltpu.VMEM)
    smem = pl.BlockSpec(memory_space=pltpu.SMEM)

    def shifted(value, shift):
        return lax.ppermute(value, "pencil", [(p, (p + shift) % pencils) for p in range(pencils)])

    kern_count = kernel_spectra.shape[0]
    local = layer_kernel[0] - lax.axis_index("depth") * kern_count
    share = RADIX // sharers
    first = lax.axis_index(("grp", "mem")) * share
    moved = pl.pallas_call(
        functools.partial(mirror_kernel, share),
        grid_spec=pltpu.PrefetchScalarGridSpec(
            num_scalar_prefetch=1,
            grid=(1,),
            in_specs=[
                pl.BlockSpec(
                    (None, 2, INNER, per * INNER),
                    lambda i, w, u=u: (w[0], 0, lax.rem(RADIX - w[1] - u, RADIX), 0),
                )
                for u in range(share)
            ],
            out_specs=[pl.BlockSpec((g, share, INNER, INNER), lambda i, w: (0, 0, 0, 0)) for g in (1, per - 1)],
        ),
        out_shape=[jax.ShapeDtypeStruct((g, share, INNER, INNER), f32) for g in (1, per - 1)],
        compiler_params=params(),
        cost_estimate=pl.CostEstimate(flops=1 << 20, bytes_accessed=2 << 20, transcendentals=0),
    )(jnp.stack([local, first, pencil]), *[kernel_spectra] * share)
    mirrored = lax.ppermute(moved[0], "pencil", [(p, (pencils - p) % pencils) for p in range(pencils)])
    rest = lax.ppermute(moved[1], "pencil", [(p, pencils - 1 - p) for p in range(pencils)])

    offset = lax.dynamic_index_in_dim(background[:, 0], member_ids[0], 0, keepdims=True)
    row_high, row_low = halves(row_tables())
    block = min(part_rows, 128)
    place = pencil.reshape(1)
    sent = pl.pallas_call(
        functools.partial(shift_rows_kernel, pencils),
        grid=(part_rows // block,),
        in_specs=[
            smem,
            smem,
            pl.BlockSpec((None, None, block, LENGTH), lambda i: (0, 0, i, 0)),
            pl.BlockSpec((8, 512, 256), lambda i: (0, 0, 0)),
            pl.BlockSpec((8, 512, 256), lambda i: (0, 0, 0)),
        ],
        out_specs=[pl.BlockSpec((2, block, lanes), lambda i: (0, i, 0))] * (chunks * pencils),
        out_shape=[jax.ShapeDtypeStruct((2, part_rows, lanes), f32)] * (chunks * pencils),
        scratch_shapes=[pltpu.VMEM((8, block, 256), f32)],
        compiler_params=params(),
        cost_estimate=pl.CostEstimate(flops=6 * part_rows * 2 * LENGTH * 512, bytes_accessed=12 << 20, transcendentals=0),
    )(offset, place, density, row_high, row_low)

    sign = jnp.array([0.5, -0.5], f32)
    edge = lax.dynamic_slice(kernel_spectra, (local, 0, 0, HALF), (1, 2, LENGTH, 1))
    edge = edge.reshape(2, RADIX, INNER).astype(f32)
    flipped = jnp.concatenate([edge[:, :1], edge[:, :0:-1]], axis=1)[..., ::-1]
    flipped = jnp.concatenate([jnp.roll(flipped[:, :1], 1, axis=2), flipped[:, 1:]], axis=1)
    edge = 0.5 * edge + sign.reshape(2, 1, 1) * flipped
    edge = jnp.where(lax.broadcasted_iota(jnp.int32, (lanes,), 0) == 0, edge[..., None], 0.0)

    arrived = []
    for k in range(chunks):
        here = [sent[k * pencils]]
        for shift in range(1, pencils):
            value = sent[k * pencils + shift]
            if k > 0:
                value, arrived[k - 1][shift] = lax.optimization_barrier((value, arrived[k - 1][shift]))
            here.append(shifted(value, shift))
        arrived.append(here)

    mirrored = jnp.concatenate([mirrored, rest], axis=0)
    mirrored, edge, _ = lax.optimization_barrier((mirrored, edge, sent[0]))
    mirrored = lax.all_gather(mirrored, ("grp", "mem"), axis=0)

    column, column_turns = column_tables()
    column_turns = jnp.asarray(column_turns)
    tables = jnp.stack(halves(column) + halves(column.T))
    angles = 2 * np.pi * np.arange(pencils)[:, None] * np.arange(RADIX)[None, :] / pencils
    phases = np.stack([np.cos(angles), np.sin(angles)], axis=-1).round(15)
    phase = lax.dynamic_index_in_dim(jnp.asarray(phases, f32), pencil, 0, keepdims=False)
    where = jnp.stack([lax.axis_index("depth"), local, pencil])
    steps = sharers
    order = [2, 1, 3, 0] if pencils == 4 else list(range(1, pencils)) + [0]
    fields = []
    waiting = None
    for k in range(chunks):
        special = k == 0

        def early(i, special=special):
            return jnp.minimum(i, steps - 1) if special else i

        def late(i, special=special):
            return jnp.maximum(i - steps, 0) if special else i

        here = [arrived[k][-j % pencils] for j in range(pencils)]
        if waiting is not None:
            here, waiting = lax.optimization_barrier((here, waiting))
            fields.append([waiting[0]] + [shifted(waiting[j], j) for j in range(1, pencils)])
        edge_block = (2, share, INNER, lanes) if special else (2, 1, 8, lanes)
        piece = jax.ShapeDtypeStruct((2, out_rows, lanes), f32)
        out = pl.pallas_call(
            functools.partial(shift_columns_kernel, special, pencils, depths),
            grid_spec=pltpu.PrefetchScalarGridSpec(
                num_scalar_prefetch=1,
                grid=(2 * steps if special else steps,),
                in_specs=[pl.BlockSpec((2, part_rows, lanes), lambda i, w: (0, 0, 0))] * pencils
                + [
                    smem,
                    pl.BlockSpec((None, 2, share * INNER, 2 * INNER), lambda i, w, k=k, late=late: (w[1], 0, late(i), k)),
                    pl.BlockSpec((None, 2, share, INNER, INNER), lambda i, w, k=k, late=late: (late(i), k, 0, 0, 0)),
                    pl.BlockSpec(
                        edge_block,
                        (lambda i, w, late=late: (0, late(i), 0, 0)) if special else (lambda i, w: (0, 0, 0, 0)),
                    ),
                    pl.BlockSpec((share, INNER, INNER), lambda i, w, early=early: (early(i), 0, 0)),
                    pl.BlockSpec((share, INNER, INNER), lambda i, w, late=late: (late(i), 0, 0)),
                    pl.BlockSpec((4, 256, 256), lambda i, w: (0, 0, 0)),
                ],
                out_specs=[pl.BlockSpec((2, out_rows, lanes), lambda i, w: (0, 0, 0))] * (depths * pencils),
                scratch_shapes=[
                    pltpu.VMEM((RADIX, 256, lanes), f32),
                    pltpu.VMEM((RADIX if special else 1, 256, lanes), f32),
                ],
            ),
            out_shape=[piece] * (depths * pencils),
            compiler_params=params(),
            cost_estimate=pl.CostEstimate(
                flops=12 * RADIX * 256 * 256 * lanes, bytes_accessed=16 << 20, transcendentals=0
            ),
        )(where, *here, phase, kernel_spectra, mirrored, edge, column_turns, column_turns, tables)
        keep, give = out[:pencils], out[pencils:]
        waiting = [None] * pencils
        for j in order:
            got = lax.ppermute(give[j], "depth", [(0, 1), (1, 0)])
            waiting[j] = (keep[j], got) if j == 0 else keep[j] + got
    fields.append([waiting[0]] + [shifted(waiting[j], j) for j in range(1, pencils)])
    fields = [ref for chunk in fields for ref in (*chunk[0], *chunk[1:])]

    back_high, back_low = halves(inverse_row_tables().reshape(8, 2, 256, 256)[
        [0 if r == 8 else min(r, RADIX - r) for r in range(RADIX)], [int(r >= 8) for r in range(RADIX)]
    ])
    return pl.pallas_call(
        functools.partial(shift_fields_kernel, pencils, chunks),
        in_specs=[smem] + [vmem] * (len(fields) + 2),
        out_specs=vmem,
        out_shape=jax.ShapeDtypeStruct((1, out_rows, LENGTH), f32),
        scratch_shapes=[pltpu.VMEM((8, out_rows, 256), f32)],
        compiler_params=params(),
        cost_estimate=pl.CostEstimate(flops=6 * out_rows * 2 * LENGTH * 512, bytes_accessed=8 << 20, transcendentals=0),
    )(place, *fields, back_high, back_low)


def body(density, background, member_ids, layer_kernel, kernel_spectra):
    pencils, depths = lax.axis_size("pencil"), lax.axis_size("depth")
    narrow = pencils < RADIX and depths == 2 and density.shape[2] // depths % INNER == 0
    plan = shift_body if narrow else wide_body
    return plan(density, background, member_ids, layer_kernel, kernel_spectra)


def solution(mesh):
    placed = (
        P(("grp", "mem"), "depth", "pencil", None),
        P(None, "depth"),
        P(("grp", "mem")),
        P("depth"),
        P("depth", None, None, "pencil"),
    )
    return jax.shard_map(
        body,
        mesh=mesh,
        in_specs=placed,
        out_specs=P(("grp", "mem"), ("pencil", "depth"), None),
        check_vma=False,
    )
```

```python
import functools
import math

import jax
import jax.numpy as jnp
import numpy as np
from jax import lax
from jax.experimental import pallas as pl
from jax.experimental.pallas import tpu as pltpu
from jax.sharding import PartitionSpec as P

RADIX = 16
INNER = 128
HALF = 64
LENGTH = RADIX * INNER
f32 = jnp.float32
bf16 = jnp.bfloat16


def halves(table):
    table = np.asarray(table, np.float32)
    high = table.astype(bf16)
    low = (table - high.astype(np.float32)).astype(bf16)
    return jnp.asarray(high), jnp.asarray(low)


def residue_rows(r):
    m = np.arange(INNER)[:, None]
    q = np.arange(HALF)[None, :]
    turn = np.exp(-2j * np.pi * (((RADIX * q + r) * m) % LENGTH) / LENGTH)
    re, im = turn.real.copy(), turn.imag.copy()
    if r == 0:
        im[:, 0] = (-1.0) ** m[:, 0]
    out = np.zeros((2 * INNER, 2 * HALF))
    if r == 0:
        out[:INNER, :HALF], out[:INNER, HALF:] = re, im
    elif r == 8:
        out[INNER:, :HALF], out[INNER:, HALF:] = re, im
    else:
        sign = 1.0 if r < 8 else -1.0
        out[:INNER, :HALF], out[:INNER, HALF:] = re, im
        out[INNER:, :HALF], out[INNER:, HALF:] = -sign * im, sign * re
    return out


def slot_of(r):
    return 0 if r in (0, 8) else min(r, RADIX - r)


def row_tables():
    tables = np.zeros((8, 512, 256))
    for t in range(8):
        for odd in range(2):
            block = residue_rows(2 * t + odd)
            rows = slice(256 * odd, 256 * odd + 256)
            tables[t, rows, HALF * odd : HALF * odd + HALF] = block[:, :HALF]
            tables[t, rows, 128 + HALF * odd : 128 + HALF * odd + HALF] = block[:, HALF:]
    return tables


def inverse_row_tables():
    tables = np.zeros((8, 512, 256))
    scale = 1.0 / (LENGTH * LENGTH)
    for s in range(8):
        for place, r in enumerate((s, 8 if s == 0 else RADIX - s)):
            block = residue_rows(r).T.copy() * scale
            weight = np.full((2 * HALF, 1), 2.0 if r in (0, 8) else 1.0)
            if r == 0:
                weight[0] = weight[HALF] = 1.0
            block *= weight
            odd = r % 2
            tables[s, 256 * place + HALF * odd : 256 * place + HALF * odd + HALF] += block[:HALF]
            tables[s, 256 * place + 128 + HALF * odd : 256 * place + 128 + HALF * odd + HALF] += block[HALF:]
    return tables


def column_tables():
    q = np.arange(INNER)[:, None]
    m = np.arange(INNER)[None, :]
    turn = np.exp(-2j * np.pi * ((q * m) % INNER) / INNER)
    table = np.block([[turn.real, -turn.imag], [turn.imag, turn.real]])
    angles = 2 * np.pi * np.arange(RADIX)[:, None] * np.arange(INNER)[None, :] / LENGTH
    turns = np.zeros((RADIX, INNER, INNER), np.float32)
    turns[..., 0] = np.cos(angles)
    turns[..., 1] = np.sin(angles)
    return table, turns


def split_value(value):
    high = value.astype(bf16)
    return high, (value - high.astype(f32)).astype(bf16)


def dot(a, b):
    return jnp.dot(a, b, preferred_element_type=f32)


def rotate(value, count, length, sign):
    re, im = value
    count %= length
    if count == 0:
        return value
    if 4 * count == length:
        return (im, -re) if sign < 0 else (-im, re)
    c = math.cos(2 * math.pi * count / length)
    s = sign * math.sin(2 * math.pi * count / length)
    if 8 * count == length:
        return ((re + im) * c, (im - re) * c) if sign < 0 else ((re - im) * c, (im + re) * c)
    return (re * c - im * s, re * s + im * c)


def plus(a, b):
    return (a[0] + b[0], a[1] + b[1])


def minus(a, b):
    return (a[0] - b[0], a[1] - b[1])


def transform(values, sign):
    length = len(values)
    if length == 1:
        return values
    even, odd = transform(values[0::2], sign), transform(values[1::2], sign)
    turned = [rotate(odd[k], k, length, sign) for k in range(length // 2)]
    return [plus(even[k], turned[k]) for k in range(length // 2)] + [
        minus(even[k], turned[k]) for k in range(length // 2)
    ]


def real_transform(values):
    length = len(values)
    if length == 2:
        return [(values[0] + values[1], None), (values[0] - values[1], None)]
    even, odd = real_transform(values[0::2]), real_transform(values[1::2])
    out = [None] * (length // 2 + 1)
    out[0] = (even[0][0] + odd[0][0], None)
    out[length // 2] = (even[0][0] - odd[0][0], None)
    quarter = length // 4
    for k in range(1, quarter):
        turned = rotate(odd[k], k, length, -1)
        out[k] = plus(even[k], turned)
        low = minus(even[k], turned)
        out[length // 2 - k] = (low[0], -low[1])
    out[quarter] = (even[quarter][0], -odd[quarter][0])
    return out


def real_inverse(values):
    half = len(values) - 1
    length = 2 * half
    if length == 2:
        return [values[0][0] + values[1][0], values[0][0] - values[1][0]]
    even, odd = [], []
    for k in range(half // 2 + 1):
        if k == 0:
            even.append((values[0][0] + values[half][0], None))
            odd.append((values[0][0] - values[half][0], None))
        elif k == half // 2:
            even.append((2.0 * values[k][0], None))
            odd.append((-2.0 * values[k][1], None))
        else:
            other = values[half - k]
            even.append((values[k][0] + other[0], values[k][1] - other[1]))
            odd.append(rotate((values[k][0] - other[0], values[k][1] + other[1]), k, length, 1))
    first, second = real_inverse(even), real_inverse(odd)
    return [x for pair in zip(first, second) for x in pair]


def rows_kernel(pencils, width, offset_ref, in_ref, high_ref, low_ref, *rest):
    outs, pieces = rest[:-1], rest[-1]
    rows = in_ref.shape[0]
    per = RADIX // pencils
    offset = offset_ref[0]

    def step(b, carry):
        at = pl.ds(pl.multiple_of(b * 8, 8), 8)
        values = [in_ref[at, n * INNER : (n + 1) * INNER] - offset for n in range(RADIX)]
        got = real_transform(values)
        pieces[0, at, :INNER] = got[0][0]
        pieces[0, at, INNER:] = got[8][0]
        for s in range(1, 8):
            pieces[s, at, :INNER] = got[s][0]
            pieces[s, at, INNER:] = got[s][1]
        return carry

    lax.fori_loop(0, rows // 8, step, 0)
    for t in range(8):
        total = None
        for odd in range(2):
            high, low = split_value(pieces[slot_of(2 * t + odd)])
            table_high = high_ref[t, 256 * odd : 256 * odd + 256]
            table_low = low_ref[t, 256 * odd : 256 * odd + 256]
            part = dot(high, table_high) + dot(low, table_high) + dot(high, table_low)
            total = part if total is None else total + part
        if width == 2:
            pencil, place = divmod(2 * t, per)
            for c in range(2):
                outs[place // 2][pencil, c] = total[:, c * 128 : (c + 1) * 128]
        else:
            for odd in range(2):
                pencil, place = divmod(2 * t + odd, per)
                for c in range(2):
                    begin = c * 128 + odd * HALF
                    outs[place][pencil, c] = total[:, begin : begin + HALF]


def swapped(zero, shape, axis):
    total = lax.broadcasted_iota(jnp.int32, shape, 0) + lax.broadcasted_iota(jnp.int32, shape, 1)
    wanted = jnp.where(zero, INNER, INNER - 1)
    also = jnp.where(zero, 0, INNER - 1)
    return jnp.where((total == wanted) | (total == also), 1.0, 0.0).astype(bf16)


def mirror_kernel(share, where_ref, *refs):
    ins, zero_ref, rest_refs = refs[:share], refs[share], refs[share + 1 :]
    per = ins[0].shape[2] // INNER
    plain = swapped(where_ref[1] < 0, (INNER, HALF), 1)
    edge = swapped(where_ref[2] == 0, (INNER, HALF), 1)
    for u in range(share):
        swap = swapped(where_ref[1] + u == 0, (INNER, INNER), 0)
        rows = [dot(swap, ins[u][c]).astype(bf16) for c in range(2)]
        for j in range(per):
            turn = edge if j == 0 else plain
            turned = [dot(rows[c][:, j * INNER : (j + 1) * INNER], turn) for c in range(2)]
            value = jnp.concatenate(turned, axis=1)
            if j == 0:
                zero_ref[0, u] = value
            else:
                rest_refs[0][per - 1 - j, u] = value


def columns_kernel(special, where_ref, in_ref, kern_ref, mirror_ref, edge_ref,
                   turns_ref, late_ref, table_ref, out_ref, pieces, waves):
    part_rows = in_ref.shape[2]
    depths, pencils, _, out_rows, lanes = out_ref.shape
    share = mirror_ref.shape[1]
    steps = RADIX // share
    mine = where_ref[0]
    now = pl.program_id(0)
    from_lane = lax.broadcasted_iota(jnp.int32, (kern_ref.shape[2], lanes), 0)
    to_lane = lax.broadcasted_iota(jnp.int32, (kern_ref.shape[2], lanes), 1)
    wanted = to_lane + jnp.where(to_lane < HALF, 0, HALF)
    pick = jnp.where(from_lane == wanted, 0.5, 0.0).astype(bf16)
    zero_swap = swapped(mine >= 0, (INNER, INNER), 0)
    plain_swap = swapped(mine < 0, (INNER, INNER), 0)

    def forward(b, carry):
        values = []
        for n in range(RADIX):
            source, begin = divmod(n * INNER, part_rows)
            at = pl.ds(pl.multiple_of(begin + b * 8, 8), 8)
            values.append((in_ref[source, 0, at, :], in_ref[source, 1, at, :]))
        at = pl.ds(pl.multiple_of(b * 8, 8), 8)
        also = pl.ds(pl.multiple_of(INNER + b * 8, 8), 8)
        for r, (re, im) in enumerate(transform(values, -1)):
            pieces[r, at, :] = re
            pieces[r, also, :] = im
        return carry

    @pl.when(now == 0)
    def _():
        lax.fori_loop(0, INNER // 8, forward, 0)

    def wave(r, u):
        re, im = pieces[r, :INNER], pieces[r, INNER:]
        c, s = turns_ref[u, :, 0:1], turns_ref[u, :, 1:2]
        high, low = split_value(jnp.concatenate([re * c + im * s, im * c - re * s], axis=0))
        return dot(table_ref[0], high) + dot(table_ref[0], low) + dot(table_ref[1], high)

    def finish(r, u, got):
        re, im = got[:INNER], got[INNER:]
        tiles = [mirror_ref[j, u] for j in range(mirror_ref.shape[0])]
        rows = slice(u * INNER, (u + 1) * INNER)
        parts = []
        for c in range(2):
            other = [tile[:, c * HALF : (c + 1) * HALF] for tile in tiles]
            other = jnp.concatenate(other, axis=1) if len(other) > 1 else other[0]
            own = dot(kern_ref[c, rows, :], pick)
            parts.append(own + 0.5 * other if c == 0 else own - 0.5 * other)
        kr, ki = parts
        if special:
            other = lax.rem(RADIX - r, RADIX)
            high, low = split_value(waves[other])
            swap = jnp.where(r == 0, zero_swap.astype(f32), plain_swap.astype(f32)).astype(bf16) if u == 0 else plain_swap
            ore = dot(swap, high[:INNER]) + dot(swap, low[:INNER])
            oim = -(dot(swap, high[INNER:]) + dot(swap, low[INNER:]))
            mask = (lax.broadcasted_iota(jnp.int32, (INNER, lanes), 1) == 0) & (where_ref[2] == 0)
            hr = jnp.where(mask, 0.5 * (kr - edge_ref[0, u]), 0.0)
            hi = jnp.where(mask, 0.5 * (ki - edge_ref[1, u]), 0.0)
            kr, ki = kr - hr, ki - hi
            sr = re * kr - im * ki + (ore * hr - oim * hi)
            si = re * ki + im * kr + (ore * hi + oim * hr)
        else:
            sr, si = re * kr - im * ki, re * ki + im * kr
        spectrum = jnp.concatenate([sr, si], axis=0)
        high, low = split_value(spectrum)
        got = dot(table_ref[2], high) + dot(table_ref[2], low) + dot(table_ref[3], high)
        re, im = got[:INNER], got[INNER:]
        c, s = late_ref[u, :, 0:1], late_ref[u, :, 1:2]
        pieces[r, :INNER] = re * c - im * s
        pieces[r, INNER:] = im * c + re * s

    if special:
        @pl.when(now < steps)
        def _():
            for u in range(share):
                waves[now * share + u] = wave(now * share + u, u)

        @pl.when(now >= steps)
        def _():
            for u in range(share):
                r = (now - steps) * share + u
                finish(r, u, waves[r])
    else:
        for u in range(share):
            r = now * share + u
            finish(r, u, wave(r, u))

    slots = [lax.rem(d - mine + depths, depths) for d in range(depths)]

    def backward(b, carry):
        at = pl.ds(pl.multiple_of(b * 8, 8), 8)
        also = pl.ds(pl.multiple_of(INNER + b * 8, 8), 8)
        values = [(pieces[r, at, :], pieces[r, also, :]) for r in range(RADIX)]
        for n, (re, im) in enumerate(transform(values, 1)):
            if out_rows % INNER == 0:
                part, begin = divmod(n * INNER, out_rows)
                pencil, depth = divmod(part, depths)
                depth = slots[depth]
                put = pl.ds(pl.multiple_of(begin + b * 8, 8), 8)
            else:
                x = n * INNER + b * 8
                pencil = x // (out_rows * depths)
                depth = lax.rem(x // out_rows - mine + depths, depths)
                put = pl.ds(pl.multiple_of(lax.rem(x, out_rows), 8), 8)
            out_ref[depth, pencil, 0, put, :] = re
            out_ref[depth, pencil, 1, put, :] = im
        return carry

    @pl.when(now == pl.num_programs(0) - 1)
    def _():
        lax.fori_loop(0, INNER // 8, backward, 0)


def fields_kernel(pencils, width, counts, *refs):
    ins, at = [], 0
    for count in counts:
        ins.append(refs[at : at + count])
        at += count
    high_ref, low_ref, out_ref, pieces = refs[at:]
    per = RADIX // pencils
    rows = out_ref.shape[1]

    def read(chunk, pencil, c):
        found = [ref[pencil, c] for ref in ins[chunk]]
        return jnp.concatenate(found, axis=0) if len(found) > 1 else found[0]

    def pair(t):
        if width == 2:
            pencil, place = divmod(2 * t, per)
            return jnp.concatenate([read(place // 2, pencil, c) for c in range(2)], axis=1)
        found = []
        for c in range(2):
            for odd in range(2):
                pencil, place = divmod(2 * t + odd, per)
                found.append(read(place, pencil, c))
        return jnp.concatenate(found, axis=1)

    for s in range(8):
        total = None
        for place, r in enumerate((s, 8 if s == 0 else RADIX - s)):
            high, low = split_value(pair(r // 2))
            table_high = high_ref[s, 256 * place : 256 * place + 256]
            table_low = low_ref[s, 256 * place : 256 * place + 256]
            part = dot(high, table_high) + dot(low, table_high) + dot(high, table_low)
            total = part if total is None else total + part
        pieces[s] = total

    def step(b, carry):
        at = pl.ds(pl.multiple_of(b * 8, 8), 8)
        values = [(pieces[0, at, :INNER], None)]
        for s in range(1, 8):
            values.append((pieces[s, at, :INNER], pieces[s, at, INNER:]))
        values.append((pieces[0, at, INNER:], None))
        for n, value in enumerate(real_inverse(values)):
            out_ref[0, at, n * INNER : (n + 1) * INNER] = value
        return carry

    lax.fori_loop(0, rows // 8, step, 0)


def slot_at(r):
    return jnp.where(r == 8, 0, jnp.minimum(r, RADIX - r))


BLOCKS = 4


def fused_kernel(pencils, depths, offset_ref, local_ref, phase_ref, density_ref, kern_ref, row_high_ref, row_low_ref,
                 back_high_ref, back_low_ref, table_ref, turns_ref, out_ref,
                 dens, source, kern, row_high, row_low, back_high, back_low, tables, turns,
                 pieces, sending, landing, moved, gathered, spectra, waves, keep, other_keep, fields,
                 local_sem, b_sem, g_sem, a_send_sem, a_recv_sem, x_sem, c_sem):
    per = RADIX // pencils
    chunks = per // 2
    lanes = 2 * HALF
    part_rows = dens.shape[0]
    block = part_rows // BLOCKS
    out_rows = part_rows // depths
    share = moved.shape[1]
    me = lax.axis_index("pencil")
    deep = lax.axis_index("depth")
    grp, mem = lax.axis_index("grp"), lax.axis_index("mem")
    sharer = grp * 2 + mem
    first = sharer * share
    local = local_ref[0]

    def remote(src, dst, send, recv, **where):
        return pltpu.make_async_remote_copy(
            src_ref=src, dst_ref=dst, send_sem=send, recv_sem=recv,
            device_id=where, device_id_type=pl.DeviceIdType.MESH,
        )

    def toward(shift):
        return lax.rem(me + shift, pencils)

    loads = []

    def load(src, dst):
        copy = pltpu.make_async_copy(src, dst, local_sem.at[len(loads)])
        copy.start()
        loads.append(copy)
        return copy

    source_loads = [
        load(kern_ref.at[:, :, pl.ds(pl.multiple_of(lax.rem(RADIX - first - u, RADIX) * INNER, INNER), INNER)], source.at[u])
        for u in range(share)
    ]
    dens_loads = [load(density_ref.at[0, 0, pl.ds(i * block, block)], dens.at[pl.ds(i * block, block)]) for i in range(BLOCKS)]
    row_loads = [load(row_high_ref, row_high), load(row_low_ref, row_low)]
    late_loads = [load(table_ref, tables), load(turns_ref, turns), load(kern_ref, kern),
                  load(back_high_ref, back_high), load(back_low_ref, back_low)]

    barrier = pltpu.get_barrier_semaphore()
    peers = [{"pencil": toward(shift)} for shift in range(1, pencils)]
    peers += [{"depth": 1 - deep}, {"grp": 1 - grp}, {"mem": 1 - mem}]
    for peer in peers:
        pl.semaphore_signal(barrier, inc=1, device_id=peer, device_id_type=pl.DeviceIdType.MESH)

    for copy in source_loads:
        copy.wait()
    plain = swapped(me < 0, (INNER, HALF), 1)
    edge = swapped(me == 0, (INNER, HALF), 1)
    for u in range(share):
        swap = swapped(first + u == 0, (INNER, INNER), 0)
        rows = [dot(swap, source[u, local, c]).astype(bf16) for c in range(2)]
        for j in range(per):
            turn = edge if j == 0 else plain
            turned = [dot(rows[c][:, j * INNER : (j + 1) * INNER], turn) for c in range(2)]
            moved[(per - j) % per, u] = jnp.concatenate(turned, axis=1)

    pl.semaphore_wait(barrier, len(peers))
    rest = remote(moved.at[pl.ds(1, per - 1)], gathered.at[sharer, pl.ds(1, per - 1)], b_sem.at[0], b_sem.at[1],
                  pencil=pencils - 1 - me)
    rest.start()
    partner = lax.rem(pencils - me, pencils)
    zero = remote(moved.at[0], gathered.at[sharer, 0], b_sem.at[2], b_sem.at[3], pencil=partner)
    stay = pltpu.make_async_copy(moved.at[0], gathered.at[sharer, 0], b_sem.at[4])

    @pl.when(partner != me)
    def _():
        zero.start()

    @pl.when(partner == me)
    def _():
        stay.start()

    for copy in row_loads:
        copy.wait()
    offset = offset_ref[0]

    def a_copy(chunk, shift, i):
        at = pl.ds(i * block, block)
        return remote(sending.at[chunk, shift, :, at], landing.at[chunk, shift - 1, :, at],
                      a_send_sem.at[chunk, shift - 1, i], a_recv_sem.at[chunk, shift - 1, i], pencil=toward(shift))

    for i in range(BLOCKS):
        dens_loads[i].wait()

        def step(b, carry, i=i):
            at = pl.ds(pl.multiple_of(b * 8, 8), 8)
            here = pl.ds(pl.multiple_of(i * block + b * 8, 8), 8)
            got = real_transform([dens[here, n * INNER : (n + 1) * INNER] - offset for n in range(RADIX)])
            pieces[0, at, :INNER] = got[0][0]
            pieces[0, at, INNER:] = got[8][0]
            for s in range(1, 8):
                pieces[s, at, :INNER] = got[s][0]
                pieces[s, at, INNER:] = got[s][1]
            return carry

        lax.fori_loop(0, block // 8, step, 0)

        def part(index, carry, i=i):
            shift, chunk = index // chunks, lax.rem(index, chunks)
            t = lax.rem(me + shift, pencils) * chunks + chunk
            total = None
            for odd in range(2):
                high, low = split_value(pieces[slot_at(2 * t + odd)])
                table_high = row_high[t, 256 * odd : 256 * odd + 256]
                table_low = row_low[t, 256 * odd : 256 * odd + 256]
                term = dot(high, table_high) + dot(low, table_high) + dot(high, table_low)
                total = term if total is None else total + term
            for c in range(2):
                sending[chunk, shift, c, i * block : (i + 1) * block] = total[:, c * 128 : (c + 1) * 128]
            return carry

        lax.fori_loop(0, pencils * chunks, part, 0)
        for shift in SHIFTS:
            a_copy(0, shift, i).start()

    def start_a(chunk):
        for shift in SHIFTS:
            for i in range(BLOCKS):
                a_copy(chunk, shift, i).start()

    def wait_a(chunk):
        for shift in SHIFTS:
            for i in range(BLOCKS):
                a_copy(chunk, shift, i).wait_recv()

    for copy in late_loads:
        copy.wait()

    rest.wait_recv()

    @pl.when(partner != me)
    def _():
        zero.wait_recv()
        zero.wait_send()

    @pl.when(partner == me)
    def _():
        stay.wait()

    own = gathered.at[sharer]
    far = (1 - grp) * 2 + mem
    across = remote(own, own, g_sem.at[0], g_sem.at[1], grp=1 - grp)
    across.start()
    beside = remote(own, own, g_sem.at[2], g_sem.at[3], mem=1 - mem)
    beside.start()
    if not PACED:
        start_a(1)
    across.wait_recv()
    passed = remote(gathered.at[far], gathered.at[far], g_sem.at[4], g_sem.at[5], mem=1 - mem)
    passed.start()
    beside.wait_recv()
    passed.wait_recv()

    from_lane = lax.broadcasted_iota(jnp.int32, (2 * INNER, lanes), 0)
    to_lane = lax.broadcasted_iota(jnp.int32, (2 * INNER, lanes), 1)
    pick = jnp.where(from_lane == to_lane + jnp.where(to_lane < HALF, 0, HALF), 0.5, 0.0).astype(bf16)
    from_lane, to_lane = from_lane[:INNER], to_lane[:INNER]
    pick_edge = jnp.where((from_lane == HALF) & (to_lane == 0), 0.5, 0.0).astype(bf16)
    mask = (to_lane == 0) & (me == 0)

    def turned(r):
        c, s = turns[r, :, 0:1], turns[r, :, 1:2]
        pc, ps = phase_ref[me, r, 0], phase_ref[me, r, 1]
        return c * pc - s * ps, s * pc + c * ps

    def wave(r):
        re, im = spectra[r, :INNER], spectra[r, INNER:]
        c, s = turned(r)
        high, low = split_value(jnp.concatenate([re * c + im * s, im * c - re * s], axis=0))
        return dot(tables[0], high) + dot(tables[0], low) + dot(tables[1], high)

    def finish(chunk, r, got):
        re, im = got[:INNER], got[INNER:]
        rows = pl.ds(pl.multiple_of(r * INNER, INNER), INNER)
        holder, u = r // share, lax.rem(r, share)
        parts = []
        for c in range(2):
            other = [gathered[holder, 2 * chunk + j, u, :, c * HALF : (c + 1) * HALF] for j in range(2)]
            other = jnp.concatenate(other, axis=1)
            mine = dot(kern[local, c, rows, 2 * chunk * INNER : 2 * (chunk + 1) * INNER], pick)
            parts.append(mine + 0.5 * other if c == 0 else mine - 0.5 * other)
        kr, ki = parts
        if chunk == 0:
            other = lax.rem(RADIX - r, RADIX)
            other_rows = pl.ds(pl.multiple_of(other * INNER, INNER), INNER)
            swap = swapped(r == 0, (INNER, INNER), 0)
            edges = []
            for c in range(2):
                mine = dot(kern[local, c, rows, :INNER], pick_edge)
                flipped = dot(swap, kern[local, c, other_rows, :INNER]).astype(bf16)
                flipped = dot(flipped, pick_edge)
                edges.append(mine + flipped if c == 0 else mine - flipped)
            high, low = split_value(waves[other])
            ore = dot(swap, high[:INNER]) + dot(swap, low[:INNER])
            oim = -(dot(swap, high[INNER:]) + dot(swap, low[INNER:]))
            hr = jnp.where(mask, 0.5 * (kr - edges[0]), 0.0)
            hi = jnp.where(mask, 0.5 * (ki - edges[1]), 0.0)
            kr, ki = kr - hr, ki - hi
            sr = re * kr - im * ki + (ore * hr - oim * hi)
            si = re * ki + im * kr + (ore * hi + oim * hr)
        else:
            sr, si = re * kr - im * ki, re * ki + im * kr
        high, low = split_value(jnp.concatenate([sr, si], axis=0))
        got = dot(tables[2], high) + dot(tables[2], low) + dot(tables[3], high)
        re, im = got[:INNER], got[INNER:]
        c, s = turned(r)
        spectra[r, :INNER] = re * c - im * s
        spectra[r, INNER:] = im * c + re * s

    def columns(chunk):
        def forward(b, carry):
            values = []
            for n in range(RADIX):
                j, begin = divmod(n * INNER, part_rows)
                at = pl.ds(pl.multiple_of(begin + b * 8, 8), 8)
                ref = sending.at[chunk, 0] if j == 0 else landing.at[chunk, pencils - j - 1]
                values.append((ref[0, at, :], ref[1, at, :]))
            at = pl.ds(pl.multiple_of(b * 8, 8), 8)
            also = pl.ds(pl.multiple_of(INNER + b * 8, 8), 8)
            for r, (re, im) in enumerate(transform(values, -1)):
                spectra[r, at, :] = re
                spectra[r, also, :] = im
            return carry

        lax.fori_loop(0, INNER // 8, forward, 0)

        def early(i, carry):
            for u in range(UNROLL):
                waves[i * UNROLL + u] = wave(i * UNROLL + u)
            return carry

        def late(i, carry):
            for u in range(UNROLL):
                r = i * UNROLL + u
                finish(chunk, r, waves[r] if chunk == 0 else wave(r))
            return carry

        if chunk == 0:
            lax.fori_loop(0, RADIX // UNROLL, early, 0)
        lax.fori_loop(0, RADIX // UNROLL, late, 0)

        def backward(b, carry):
            at = pl.ds(pl.multiple_of(b * 8, 8), 8)
            also = pl.ds(pl.multiple_of(INNER + b * 8, 8), 8)
            values = [(spectra[r, at, :], spectra[r, also, :]) for r in range(RADIX)]
            for n, (re, im) in enumerate(transform(values, 1)):
                shift_depth, begin = divmod(n * INNER, out_rows)
                shift, depth = divmod(shift_depth, depths)
                put = pl.ds(pl.multiple_of(begin + b * 8, 8), 8)
                slot = jnp.where(deep == depth, 0, 1)
                keep[chunk, slot, shift, 0, put, :] = re
                keep[chunk, slot, shift, 1, put, :] = im
            return carry

        lax.fori_loop(0, INNER // 8, backward, 0)

    def x_copy(chunk, j):
        return remote(keep.at[chunk, 1, j], other_keep.at[chunk, j], x_sem.at[0, chunk, j], x_sem.at[1, chunk, j],
                      depth=1 - deep)

    def c_copy(chunk, j):
        return remote(keep.at[chunk, 0, j], fields.at[chunk, j - 1], c_sem.at[0, chunk, j - 1], c_sem.at[1, chunk, j - 1],
                      pencil=toward(j))

    def summed(chunk, j):
        x_copy(chunk, j).wait_recv()
        keep[chunk, 0, j] += other_keep[chunk, j]

    def gather_field(chunk, shift):
        t = lax.rem(me + pencils - shift, pencils) * chunks + chunk
        ref = keep.at[chunk, 0, 0] if shift == 0 else fields.at[chunk, shift - 1]
        high, low = split_value(jnp.concatenate([ref[0], ref[1]], axis=1))
        for odd in range(2):
            r = 2 * t + odd
            out_ref[slot_at(r)] += dot(high, back_high[r]) + dot(low, back_high[r]) + dot(high, back_low[r])

    out_ref[...] = jnp.zeros_like(out_ref)
    wait_a(0)
    if PACED:
        start_a(1)
    columns(0)
    for j in ORDER:
        x_copy(0, j).start()
    for j in ORDER:
        summed(0, j)
    wait_a(1)
    for j in ORDER:
        if j:
            c_copy(0, j).start()
    columns(1)
    for j in ORDER:
        x_copy(1, j).start()
    gather_field(0, 0)
    for j in ORDER:
        summed(1, j)
        if j:
            c_copy(1, j).start()
    gather_field(1, 0)
    for chunk in range(chunks):
        for j in ORDER:
            if j:
                c_copy(chunk, j).wait_recv()
                gather_field(chunk, j)

    rest.wait_send()
    across.wait_send()
    beside.wait_send()
    passed.wait_send()
    for chunk in range(chunks):
        for shift in SHIFTS:
            for i in range(BLOCKS):
                a_copy(chunk, shift, i).wait_send()
        for j in ORDER:
            x_copy(chunk, j).wait_send()
            if j:
                c_copy(chunk, j).wait_send()


def last_kernel(pieces, out_ref):
    def step(b, carry):
        at = pl.ds(pl.multiple_of(b * 8, 8), 8)
        values = [(pieces[0, at, :INNER], None)]
        for s in range(1, 8):
            values.append((pieces[s, at, :INNER], pieces[s, at, INNER:]))
        values.append((pieces[0, at, INNER:], None))
        for n, value in enumerate(real_inverse(values)):
            out_ref[0, at, n * INNER : (n + 1) * INNER] = value
        return carry

    lax.fori_loop(0, out_ref.shape[1] // 8, step, 0)


SHIFTS = (2, 1, 3)
ORDER = (2, 1, 3, 0)
UNROLL = 4
PACED = True


def params(**more):
    return pltpu.CompilerParams(vmem_limit_bytes=48 * 1024 * 1024, **more)


def wide_body(density, background, member_ids, layer_kernel, kernel_spectra):
    pencils = lax.axis_size("pencil")
    depths = lax.axis_size("depth")
    sharers = lax.axis_size("grp") * lax.axis_size("mem")
    pencil = lax.axis_index("pencil")
    per = RADIX // pencils
    width = min(per, 2)
    chunks = per // width
    lanes = width * HALF
    part_rows = density.shape[2]
    out_rows = part_rows // depths
    vmem = pl.BlockSpec(memory_space=pltpu.VMEM)
    smem = pl.BlockSpec(memory_space=pltpu.SMEM)

    kern_count = kernel_spectra.shape[0]
    local = layer_kernel[0] - lax.axis_index("depth") * kern_count
    share = RADIX // sharers
    first = lax.axis_index(("grp", "mem")) * share
    groups = [1] if per == 1 else [1, per - 1]
    moved = pl.pallas_call(
        functools.partial(mirror_kernel, share),
        grid_spec=pltpu.PrefetchScalarGridSpec(
            num_scalar_prefetch=1,
            grid=(1,),
            in_specs=[
                pl.BlockSpec(
                    (None, 2, INNER, per * INNER),
                    lambda i, w, u=u: (w[0], 0, lax.rem(RADIX - w[1] - u, RADIX), 0),
                )
                for u in range(share)
            ],
            out_specs=[pl.BlockSpec((g, share, INNER, INNER), lambda i, w: (0, 0, 0, 0)) for g in groups],
        ),
        out_shape=[jax.ShapeDtypeStruct((g, share, INNER, INNER), f32) for g in groups],
        compiler_params=params(),
        cost_estimate=pl.CostEstimate(flops=1 << 20, bytes_accessed=2 << 20, transcendentals=0),
    )(jnp.stack([local, first, pencil]), *[kernel_spectra] * share)
    mirrored = lax.ppermute(moved[0], "pencil", [(p, (pencils - p) % pencils) for p in range(pencils)])
    if per > 1:
        rest = lax.ppermute(moved[1], "pencil", [(p, pencils - 1 - p) for p in range(pencils)])

    offset = lax.dynamic_index_in_dim(background[:, 0], member_ids[0], 0, keepdims=True)
    row_high, row_low = halves(row_tables())
    block = min(part_rows, 128)
    sent = pl.pallas_call(
        functools.partial(rows_kernel, pencils, width),
        grid=(part_rows // block,),
        in_specs=[
            smem,
            pl.BlockSpec((None, None, block, LENGTH), lambda i: (0, 0, i, 0)),
            pl.BlockSpec((8, 512, 256), lambda i: (0, 0, 0)),
            pl.BlockSpec((8, 512, 256), lambda i: (0, 0, 0)),
        ],
        out_specs=[pl.BlockSpec((pencils, 2, block, lanes), lambda i: (0, 0, i, 0))] * chunks,
        out_shape=[jax.ShapeDtypeStruct((pencils, 2, part_rows, lanes), f32)] * chunks,
        scratch_shapes=[pltpu.VMEM((8, block, 256), f32)],
        compiler_params=params(),
        cost_estimate=pl.CostEstimate(flops=6 * part_rows * 2 * LENGTH * 512, bytes_accessed=12 << 20, transcendentals=0),
    )(offset, density, row_high, row_low)
    arrived = [lax.all_to_all(part, "pencil", 0, 0, tiled=True) for part in sent]

    sign = jnp.array([0.5, -0.5], f32)
    edge = lax.dynamic_slice(kernel_spectra, (local, 0, 0, HALF), (1, 2, LENGTH, 1))
    edge = edge.reshape(2, RADIX, INNER).astype(f32)
    flipped = jnp.concatenate([edge[:, :1], edge[:, :0:-1]], axis=1)[..., ::-1]
    flipped = jnp.concatenate([jnp.roll(flipped[:, :1], 1, axis=2), flipped[:, 1:]], axis=1)
    edge = 0.5 * edge + sign.reshape(2, 1, 1) * flipped
    edge = jnp.where(lax.broadcasted_iota(jnp.int32, (lanes,), 0) == 0, edge[..., None], 0.0)

    if per > 1:
        mirrored = jnp.concatenate([mirrored, rest], axis=0)
    mirrored, edge, _ = lax.optimization_barrier((mirrored, edge, sent[0]))
    mirrored = lax.all_gather(mirrored, ("grp", "mem"), axis=0)

    column, column_turns = column_tables()
    column_turns = jnp.asarray(column_turns)
    tables = jnp.stack(halves(column) + halves(column.T))
    two = depths == 2
    mine = lax.axis_index("depth") if two else jnp.int32(0)
    where = jnp.stack([mine, local, pencil])
    fields = []
    before = None
    for k in range(chunks):
        special = k == 0
        steps = sharers

        def early(i, special=special):
            return jnp.minimum(i, steps - 1) if special else i

        def late(i, special=special):
            return jnp.maximum(i - steps, 0) if special else i

        here = arrived[k]
        if before is not None:
            here, before = lax.optimization_barrier((here, before))
            fields.append(lax.all_to_all(before, "pencil", 0, 0, tiled=True))
        edge_block = (2, share, INNER, lanes) if special else (2, 1, 8, lanes)
        out = pl.pallas_call(
            functools.partial(columns_kernel, special),
            grid_spec=pltpu.PrefetchScalarGridSpec(
                num_scalar_prefetch=1,
                grid=(2 * steps if special else steps,),
                in_specs=[
                    pl.BlockSpec((pencils, 2, part_rows, lanes), lambda i, w: (0, 0, 0, 0)),
                    pl.BlockSpec(
                        (None, 2, share * INNER, width * INNER), lambda i, w, k=k, late=late: (w[1], 0, late(i), k)
                    ),
                    pl.BlockSpec(
                        (None, width, share, INNER, INNER), lambda i, w, k=k, late=late: (late(i), k, 0, 0, 0)
                    ),
                    pl.BlockSpec(
                        edge_block,
                        (lambda i, w, late=late: (0, late(i), 0, 0)) if special else (lambda i, w: (0, 0, 0, 0)),
                    ),
                ]
                + [pl.BlockSpec((share, INNER, INNER), lambda i, w, early=early: (early(i), 0, 0))]
                + [pl.BlockSpec((share, INNER, INNER), lambda i, w, late=late: (late(i), 0, 0))]
                + [pl.BlockSpec((4, 256, 256), lambda i, w: (0, 0, 0))],
                out_specs=pl.BlockSpec((depths, pencils, 2, out_rows, lanes), lambda i, w: (0, 0, 0, 0, 0)),
                scratch_shapes=[
                    pltpu.VMEM((RADIX, 256, lanes), f32),
                    pltpu.VMEM((RADIX if special else 1, 256, lanes), f32),
                ],
            ),
            out_shape=jax.ShapeDtypeStruct((depths, pencils, 2, out_rows, lanes), f32),
            compiler_params=params(),
            cost_estimate=pl.CostEstimate(
                flops=12 * RADIX * 256 * 256 * lanes, bytes_accessed=16 << 20, transcendentals=0
            ),
        )(where, here, kernel_spectra, mirrored, edge, column_turns, column_turns, tables)
        if two:
            before = out[0] + lax.ppermute(out[1], "depth", [(0, 1), (1, 0)])
        else:
            before = lax.psum_scatter(out, "depth", scatter_dimension=0, tiled=False)
    fields.append(lax.all_to_all(before, "pencil", 0, 0, tiled=True))

    back_high, back_low = halves(inverse_row_tables())
    return pl.pallas_call(
        functools.partial(fields_kernel, pencils, width, [1] * chunks),
        in_specs=[vmem] * (len(fields) + 2),
        out_specs=vmem,
        out_shape=jax.ShapeDtypeStruct((1, out_rows, LENGTH), f32),
        scratch_shapes=[pltpu.VMEM((8, out_rows, 256), f32)],
        compiler_params=params(),
        cost_estimate=pl.CostEstimate(flops=6 * out_rows * 2 * LENGTH * 512, bytes_accessed=8 << 20, transcendentals=0),
    )(*fields, back_high, back_low)


def fused_body(density, background, member_ids, layer_kernel, kernel_spectra):
    pencils = lax.axis_size("pencil")
    depths = lax.axis_size("depth")
    sharers = lax.axis_size("grp") * lax.axis_size("mem")
    per = RADIX // pencils
    chunks = per // 2
    lanes = 2 * HALF
    part_rows = density.shape[2]
    out_rows = part_rows // depths
    share = RADIX // sharers
    smem = pl.BlockSpec(memory_space=pltpu.SMEM)
    anywhere = pl.BlockSpec(memory_space=pl.ANY)
    vmem = pl.BlockSpec(memory_space=pltpu.VMEM)

    offset = lax.dynamic_index_in_dim(background[:, 0], member_ids[0], 0, keepdims=True)
    local = layer_kernel - lax.axis_index("depth") * kernel_spectra.shape[0]
    angles = 2 * np.pi * np.arange(pencils)[:, None] * np.arange(RADIX)[None, :] / pencils
    phases = jnp.asarray(np.stack([np.cos(angles), np.sin(angles)], axis=-1).round(15), f32)
    row_high, row_low = halves(row_tables())
    where = [0 if r == 8 else min(r, RADIX - r) for r in range(RADIX)], [int(r >= 8) for r in range(RADIX)]
    back_high, back_low = halves(inverse_row_tables().reshape(8, 2, 256, 256)[where])
    column, turns = column_tables()
    tables = jnp.stack(halves(column) + halves(column.T))
    turns = jnp.asarray(turns)
    dma = pltpu.SemaphoreType.DMA
    pieces = pl.pallas_call(
        functools.partial(fused_kernel, pencils, depths),
        in_specs=[smem] * 3 + [anywhere] * 8,
        out_specs=vmem,
        out_shape=jax.ShapeDtypeStruct((8, out_rows, 256), f32),
        scratch_shapes=[
            pltpu.VMEM((part_rows, LENGTH), f32),
            pltpu.VMEM((share, kernel_spectra.shape[0], 2, INNER, per * INNER), bf16),
            pltpu.VMEM(kernel_spectra.shape, bf16),
            pltpu.VMEM(row_high.shape, bf16),
            pltpu.VMEM(row_low.shape, bf16),
            pltpu.VMEM(back_high.shape, bf16),
            pltpu.VMEM(back_low.shape, bf16),
            pltpu.VMEM(tables.shape, bf16),
            pltpu.VMEM(turns.shape, f32),
            pltpu.VMEM((8, part_rows // BLOCKS, 256), f32),
            pltpu.VMEM((chunks, pencils, 2, part_rows, lanes), f32),
            pltpu.VMEM((chunks, pencils - 1, 2, part_rows, lanes), f32),
            pltpu.VMEM((per, share, INNER, INNER), f32),
            pltpu.VMEM((sharers, per, share, INNER, INNER), f32),
            pltpu.VMEM((RADIX, 256, lanes), f32),
            pltpu.VMEM((RADIX, 256, lanes), f32),
            pltpu.VMEM((chunks, 2, pencils, 2, out_rows, lanes), f32),
            pltpu.VMEM((chunks, pencils, 2, out_rows, lanes), f32),
            pltpu.VMEM((chunks, pencils - 1, 2, out_rows, lanes), f32),
            dma((share + BLOCKS + 7,)),
            dma((5,)),
            dma((6,)),
            dma((chunks, pencils - 1, BLOCKS)),
            dma((chunks, pencils - 1, BLOCKS)),
            dma((2, chunks, pencils)),
            dma((2, chunks, pencils - 1)),
        ],
        compiler_params=pltpu.CompilerParams(
            vmem_limit_bytes=60 * 1024 * 1024, collective_id=0, has_side_effects=True
        ),
    )(offset, local, phases, density, kernel_spectra, row_high, row_low, back_high, back_low, tables, turns)
    return pl.pallas_call(
        last_kernel,
        in_specs=[vmem],
        out_specs=vmem,
        out_shape=jax.ShapeDtypeStruct((1, out_rows, LENGTH), f32),
        compiler_params=params(),
    )(pieces)


def body(density, background, member_ids, layer_kernel, kernel_spectra):
    sizes = tuple(lax.axis_size(name) for name in ("grp", "pencil", "depth", "mem"))
    plan = fused_body if sizes == (2, 4, 2, 2) else wide_body
    return plan(density, background, member_ids, layer_kernel, kernel_spectra)


def solution(mesh):
    placed = (
        P(("grp", "mem"), "depth", "pencil", None),
        P(None, "depth"),
        P(("grp", "mem")),
        P("depth"),
        P("depth", None, None, "pencil"),
    )
    return jax.shard_map(
        body,
        mesh=mesh,
        in_specs=placed,
        out_specs=P(("grp", "mem"), ("pencil", "depth"), None),
        check_vma=False,
    )
```

```python
import functools
import math

import jax
import jax.numpy as jnp
import numpy as np
from jax import lax
from jax.experimental import pallas as pl
from jax.experimental.pallas import tpu as pltpu
from jax.sharding import PartitionSpec as P

RADIX = 16
INNER = 128
HALF = 64
LENGTH = RADIX * INNER
f32 = jnp.float32
bf16 = jnp.bfloat16


def halves(table):
    table = np.asarray(table, np.float32)
    high = table.astype(bf16)
    low = (table - high.astype(np.float32)).astype(bf16)
    return jnp.asarray(high), jnp.asarray(low)


def residue_rows(r):
    m = np.arange(INNER)[:, None]
    q = np.arange(HALF)[None, :]
    turn = np.exp(-2j * np.pi * (((RADIX * q + r) * m) % LENGTH) / LENGTH)
    re, im = turn.real.copy(), turn.imag.copy()
    if r == 0:
        im[:, 0] = (-1.0) ** m[:, 0]
    out = np.zeros((2 * INNER, 2 * HALF))
    if r == 0:
        out[:INNER, :HALF], out[:INNER, HALF:] = re, im
    elif r == 8:
        out[INNER:, :HALF], out[INNER:, HALF:] = re, im
    else:
        sign = 1.0 if r < 8 else -1.0
        out[:INNER, :HALF], out[:INNER, HALF:] = re, im
        out[INNER:, :HALF], out[INNER:, HALF:] = -sign * im, sign * re
    return out


def slot_of(r):
    return 0 if r in (0, 8) else min(r, RADIX - r)


def row_tables():
    tables = np.zeros((8, 512, 256))
    for t in range(8):
        for odd in range(2):
            block = residue_rows(2 * t + odd)
            rows = slice(256 * odd, 256 * odd + 256)
            tables[t, rows, HALF * odd : HALF * odd + HALF] = block[:, :HALF]
            tables[t, rows, 128 + HALF * odd : 128 + HALF * odd + HALF] = block[:, HALF:]
    return tables


def inverse_row_tables():
    tables = np.zeros((8, 512, 256))
    scale = 1.0 / (LENGTH * LENGTH)
    for s in range(8):
        for place, r in enumerate((s, 8 if s == 0 else RADIX - s)):
            block = residue_rows(r).T.copy() * scale
            weight = np.full((2 * HALF, 1), 2.0 if r in (0, 8) else 1.0)
            if r == 0:
                weight[0] = weight[HALF] = 1.0
            block *= weight
            odd = r % 2
            tables[s, 256 * place + HALF * odd : 256 * place + HALF * odd + HALF] += block[:HALF]
            tables[s, 256 * place + 128 + HALF * odd : 256 * place + 128 + HALF * odd + HALF] += block[HALF:]
    return tables


def column_tables():
    q = np.arange(INNER)[:, None]
    m = np.arange(INNER)[None, :]
    turn = np.exp(-2j * np.pi * ((q * m) % INNER) / INNER)
    table = np.block([[turn.real, -turn.imag], [turn.imag, turn.real]])
    angles = 2 * np.pi * np.arange(RADIX)[:, None] * np.arange(INNER)[None, :] / LENGTH
    turns = np.zeros((RADIX, INNER, INNER), np.float32)
    turns[..., 0] = np.cos(angles)
    turns[..., 1] = np.sin(angles)
    return table, turns


def split_value(value):
    high = value.astype(bf16)
    return high, (value - high.astype(f32)).astype(bf16)


def dot(a, b):
    return jnp.dot(a, b, preferred_element_type=f32)


def rotate(value, count, length, sign):
    re, im = value
    count %= length
    if count == 0:
        return value
    if 4 * count == length:
        return (im, -re) if sign < 0 else (-im, re)
    c = math.cos(2 * math.pi * count / length)
    s = sign * math.sin(2 * math.pi * count / length)
    if 8 * count == length:
        return ((re + im) * c, (im - re) * c) if sign < 0 else ((re - im) * c, (im + re) * c)
    return (re * c - im * s, re * s + im * c)


def plus(a, b):
    return (a[0] + b[0], a[1] + b[1])


def minus(a, b):
    return (a[0] - b[0], a[1] - b[1])


def transform(values, sign):
    length = len(values)
    if length == 1:
        return values
    even, odd = transform(values[0::2], sign), transform(values[1::2], sign)
    turned = [rotate(odd[k], k, length, sign) for k in range(length // 2)]
    return [plus(even[k], turned[k]) for k in range(length // 2)] + [
        minus(even[k], turned[k]) for k in range(length // 2)
    ]


def real_transform(values):
    length = len(values)
    if length == 2:
        return [(values[0] + values[1], None), (values[0] - values[1], None)]
    even, odd = real_transform(values[0::2]), real_transform(values[1::2])
    out = [None] * (length // 2 + 1)
    out[0] = (even[0][0] + odd[0][0], None)
    out[length // 2] = (even[0][0] - odd[0][0], None)
    quarter = length // 4
    for k in range(1, quarter):
        turned = rotate(odd[k], k, length, -1)
        out[k] = plus(even[k], turned)
        low = minus(even[k], turned)
        out[length // 2 - k] = (low[0], -low[1])
    out[quarter] = (even[quarter][0], -odd[quarter][0])
    return out


def real_inverse(values):
    half = len(values) - 1
    length = 2 * half
    if length == 2:
        return [values[0][0] + values[1][0], values[0][0] - values[1][0]]
    even, odd = [], []
    for k in range(half // 2 + 1):
        if k == 0:
            even.append((values[0][0] + values[half][0], None))
            odd.append((values[0][0] - values[half][0], None))
        elif k == half // 2:
            even.append((2.0 * values[k][0], None))
            odd.append((-2.0 * values[k][1], None))
        else:
            other = values[half - k]
            even.append((values[k][0] + other[0], values[k][1] - other[1]))
            odd.append(rotate((values[k][0] - other[0], values[k][1] + other[1]), k, length, 1))
    first, second = real_inverse(even), real_inverse(odd)
    return [x for pair in zip(first, second) for x in pair]


def rows_kernel(pencils, width, offset_ref, in_ref, high_ref, low_ref, *rest):
    outs, pieces = rest[:-1], rest[-1]
    rows = in_ref.shape[0]
    per = RADIX // pencils
    offset = offset_ref[0]

    def step(b, carry):
        at = pl.ds(pl.multiple_of(b * 8, 8), 8)
        values = [in_ref[at, n * INNER : (n + 1) * INNER] - offset for n in range(RADIX)]
        got = real_transform(values)
        pieces[0, at, :INNER] = got[0][0]
        pieces[0, at, INNER:] = got[8][0]
        for s in range(1, 8):
            pieces[s, at, :INNER] = got[s][0]
            pieces[s, at, INNER:] = got[s][1]
        return carry

    lax.fori_loop(0, rows // 8, step, 0)
    for t in range(8):
        total = None
        for odd in range(2):
            high, low = split_value(pieces[slot_of(2 * t + odd)])
            table_high = high_ref[t, 256 * odd : 256 * odd + 256]
            table_low = low_ref[t, 256 * odd : 256 * odd + 256]
            part = dot(high, table_high) + dot(low, table_high) + dot(high, table_low)
            total = part if total is None else total + part
        if width == 2:
            pencil, place = divmod(2 * t, per)
            for c in range(2):
                outs[place // 2][pencil, c] = total[:, c * 128 : (c + 1) * 128]
        else:
            for odd in range(2):
                pencil, place = divmod(2 * t + odd, per)
                for c in range(2):
                    begin = c * 128 + odd * HALF
                    outs[place][pencil, c] = total[:, begin : begin + HALF]


def swapped(zero, shape, axis):
    total = lax.broadcasted_iota(jnp.int32, shape, 0) + lax.broadcasted_iota(jnp.int32, shape, 1)
    wanted = jnp.where(zero, INNER, INNER - 1)
    also = jnp.where(zero, 0, INNER - 1)
    return jnp.where((total == wanted) | (total == also), 1.0, 0.0).astype(bf16)


def mirror_kernel(share, where_ref, *refs):
    ins, zero_ref, rest_refs = refs[:share], refs[share], refs[share + 1 :]
    per = ins[0].shape[2] // INNER
    plain = swapped(where_ref[1] < 0, (INNER, HALF), 1)
    edge = swapped(where_ref[2] == 0, (INNER, HALF), 1)
    for u in range(share):
        swap = swapped(where_ref[1] + u == 0, (INNER, INNER), 0)
        rows = [dot(swap, ins[u][c]).astype(bf16) for c in range(2)]
        for j in range(per):
            turn = edge if j == 0 else plain
            turned = [dot(rows[c][:, j * INNER : (j + 1) * INNER], turn) for c in range(2)]
            value = jnp.concatenate(turned, axis=1)
            if j == 0:
                zero_ref[0, u] = value
            else:
                rest_refs[0][per - 1 - j, u] = value


def columns_kernel(special, where_ref, in_ref, kern_ref, mirror_ref, edge_ref,
                   turns_ref, late_ref, table_ref, out_ref, pieces, waves):
    part_rows = in_ref.shape[2]
    depths, pencils, _, out_rows, lanes = out_ref.shape
    share = mirror_ref.shape[1]
    steps = RADIX // share
    mine = where_ref[0]
    now = pl.program_id(0)
    from_lane = lax.broadcasted_iota(jnp.int32, (kern_ref.shape[2], lanes), 0)
    to_lane = lax.broadcasted_iota(jnp.int32, (kern_ref.shape[2], lanes), 1)
    wanted = to_lane + jnp.where(to_lane < HALF, 0, HALF)
    pick = jnp.where(from_lane == wanted, 0.5, 0.0).astype(bf16)
    zero_swap = swapped(mine >= 0, (INNER, INNER), 0)
    plain_swap = swapped(mine < 0, (INNER, INNER), 0)

    def forward(b, carry):
        values = []
        for n in range(RADIX):
            source, begin = divmod(n * INNER, part_rows)
            at = pl.ds(pl.multiple_of(begin + b * 8, 8), 8)
            values.append((in_ref[source, 0, at, :], in_ref[source, 1, at, :]))
        at = pl.ds(pl.multiple_of(b * 8, 8), 8)
        also = pl.ds(pl.multiple_of(INNER + b * 8, 8), 8)
        for r, (re, im) in enumerate(transform(values, -1)):
            pieces[r, at, :] = re
            pieces[r, also, :] = im
        return carry

    @pl.when(now == 0)
    def _():
        lax.fori_loop(0, INNER // 8, forward, 0)

    def wave(r, u):
        re, im = pieces[r, :INNER], pieces[r, INNER:]
        c, s = turns_ref[u, :, 0:1], turns_ref[u, :, 1:2]
        high, low = split_value(jnp.concatenate([re * c + im * s, im * c - re * s], axis=0))
        return dot(table_ref[0], high) + dot(table_ref[0], low) + dot(table_ref[1], high)

    def finish(r, u, got):
        re, im = got[:INNER], got[INNER:]
        tiles = [mirror_ref[j, u] for j in range(mirror_ref.shape[0])]
        rows = slice(u * INNER, (u + 1) * INNER)
        parts = []
        for c in range(2):
            other = [tile[:, c * HALF : (c + 1) * HALF] for tile in tiles]
            other = jnp.concatenate(other, axis=1) if len(other) > 1 else other[0]
            own = dot(kern_ref[c, rows, :], pick)
            parts.append(own + 0.5 * other if c == 0 else own - 0.5 * other)
        kr, ki = parts
        if special:
            other = lax.rem(RADIX - r, RADIX)
            high, low = split_value(waves[other])
            swap = jnp.where(r == 0, zero_swap.astype(f32), plain_swap.astype(f32)).astype(bf16) if u == 0 else plain_swap
            ore = dot(swap, high[:INNER]) + dot(swap, low[:INNER])
            oim = -(dot(swap, high[INNER:]) + dot(swap, low[INNER:]))
            mask = (lax.broadcasted_iota(jnp.int32, (INNER, lanes), 1) == 0) & (where_ref[2] == 0)
            hr = jnp.where(mask, 0.5 * (kr - edge_ref[0, u]), 0.0)
            hi = jnp.where(mask, 0.5 * (ki - edge_ref[1, u]), 0.0)
            kr, ki = kr - hr, ki - hi
            sr = re * kr - im * ki + (ore * hr - oim * hi)
            si = re * ki + im * kr + (ore * hi + oim * hr)
        else:
            sr, si = re * kr - im * ki, re * ki + im * kr
        spectrum = jnp.concatenate([sr, si], axis=0)
        high, low = split_value(spectrum)
        got = dot(table_ref[2], high) + dot(table_ref[2], low) + dot(table_ref[3], high)
        re, im = got[:INNER], got[INNER:]
        c, s = late_ref[u, :, 0:1], late_ref[u, :, 1:2]
        pieces[r, :INNER] = re * c - im * s
        pieces[r, INNER:] = im * c + re * s

    if special:
        @pl.when(now < steps)
        def _():
            for u in range(share):
                waves[now * share + u] = wave(now * share + u, u)

        @pl.when(now >= steps)
        def _():
            for u in range(share):
                r = (now - steps) * share + u
                finish(r, u, waves[r])
    else:
        for u in range(share):
            r = now * share + u
            finish(r, u, wave(r, u))

    slots = [lax.rem(d - mine + depths, depths) for d in range(depths)]

    def backward(b, carry):
        at = pl.ds(pl.multiple_of(b * 8, 8), 8)
        also = pl.ds(pl.multiple_of(INNER + b * 8, 8), 8)
        values = [(pieces[r, at, :], pieces[r, also, :]) for r in range(RADIX)]
        for n, (re, im) in enumerate(transform(values, 1)):
            if out_rows % INNER == 0:
                part, begin = divmod(n * INNER, out_rows)
                pencil, depth = divmod(part, depths)
                depth = slots[depth]
                put = pl.ds(pl.multiple_of(begin + b * 8, 8), 8)
            else:
                x = n * INNER + b * 8
                pencil = x // (out_rows * depths)
                depth = lax.rem(x // out_rows - mine + depths, depths)
                put = pl.ds(pl.multiple_of(lax.rem(x, out_rows), 8), 8)
            out_ref[depth, pencil, 0, put, :] = re
            out_ref[depth, pencil, 1, put, :] = im
        return carry

    @pl.when(now == pl.num_programs(0) - 1)
    def _():
        lax.fori_loop(0, INNER // 8, backward, 0)


def fields_kernel(pencils, width, counts, *refs):
    ins, at = [], 0
    for count in counts:
        ins.append(refs[at : at + count])
        at += count
    high_ref, low_ref, out_ref, pieces = refs[at:]
    per = RADIX // pencils
    rows = out_ref.shape[1]

    def read(chunk, pencil, c):
        found = [ref[pencil, c] for ref in ins[chunk]]
        return jnp.concatenate(found, axis=0) if len(found) > 1 else found[0]

    def pair(t):
        if width == 2:
            pencil, place = divmod(2 * t, per)
            return jnp.concatenate([read(place // 2, pencil, c) for c in range(2)], axis=1)
        found = []
        for c in range(2):
            for odd in range(2):
                pencil, place = divmod(2 * t + odd, per)
                found.append(read(place, pencil, c))
        return jnp.concatenate(found, axis=1)

    for s in range(8):
        total = None
        for place, r in enumerate((s, 8 if s == 0 else RADIX - s)):
            high, low = split_value(pair(r // 2))
            table_high = high_ref[s, 256 * place : 256 * place + 256]
            table_low = low_ref[s, 256 * place : 256 * place + 256]
            part = dot(high, table_high) + dot(low, table_high) + dot(high, table_low)
            total = part if total is None else total + part
        pieces[s] = total

    def step(b, carry):
        at = pl.ds(pl.multiple_of(b * 8, 8), 8)
        values = [(pieces[0, at, :INNER], None)]
        for s in range(1, 8):
            values.append((pieces[s, at, :INNER], pieces[s, at, INNER:]))
        values.append((pieces[0, at, INNER:], None))
        for n, value in enumerate(real_inverse(values)):
            out_ref[0, at, n * INNER : (n + 1) * INNER] = value
        return carry

    lax.fori_loop(0, rows // 8, step, 0)


def slot_at(r):
    return jnp.where(r == 8, 0, jnp.minimum(r, RADIX - r))


BLOCKS = 4


def fused_kernel(pencils, depths, background_ref, member_ref, layer_ref, phase_ref, density_ref, kern_ref, row_high_ref, row_low_ref,
                 back_high_ref, back_low_ref, table_ref, turns_ref, out_ref,
                 dens, sources, kern, row_high, row_low, back_high, back_low, tables, turns,
                 pieces, sending, landing, moved, gathered, spectra, waves, keep, other_keep, fields, half,
                 local_sem, b_sem, g_sem, a_send_sem, a_recv_sem, x_sem, c_sem):
    per = RADIX // pencils
    chunks = per // 2
    lanes = 2 * HALF
    part_rows = dens.shape[0]
    block = part_rows // BLOCKS
    out_rows = part_rows // depths
    share = moved.shape[1]
    me = lax.axis_index("pencil")
    deep = lax.axis_index("depth")
    grp, mem = lax.axis_index("grp"), lax.axis_index("mem")
    sharer = grp * 2 + mem
    first = sharer * share
    local = jnp.clip(layer_ref[0] - deep * kern.shape[0], 0, kern.shape[0] - 1)

    def remote(src, dst, send, recv, **where):
        return pltpu.make_async_remote_copy(
            src_ref=src, dst_ref=dst, send_sem=send, recv_sem=recv,
            device_id=where, device_id_type=pl.DeviceIdType.MESH,
        )

    def toward(shift):
        return lax.rem(me + shift, pencils)

    loads = []

    def load(src, dst):
        copy = pltpu.make_async_copy(src, dst, local_sem.at[len(loads)])
        copy.start()
        loads.append(copy)
        return copy

    source_loads = [
        load(kern_ref.at[:, :, pl.ds(pl.multiple_of(lax.rem(RADIX - first - u, RADIX) * INNER, INNER), INNER)], sources[u])
        for u in range(share)
    ]
    barrier = pltpu.get_barrier_semaphore()
    peers = [{"pencil": toward(shift)} for shift in range(1, pencils)]
    peers += [{"depth": 1 - deep}, {"grp": 1 - grp}, {"mem": 1 - mem}]
    for peer in peers:
        pl.semaphore_signal(barrier, inc=1, device_id=peer, device_id_type=pl.DeviceIdType.MESH)

    row_loads = [load(row_high_ref, row_high), load(row_low_ref, row_low)]
    dens_loads = [load(density_ref.at[0, 0, pl.ds(i * block, block)], dens.at[pl.ds(i * block, block)]) for i in range(BLOCKS)]
    partner = lax.rem(pencils - me, pencils)

    def rest(u):
        at = pl.ds(1, per - 1)
        return remote(moved.at[at, u], gathered.at[sharer, at, u], b_sem.at[0, u], b_sem.at[1, u], pencil=pencils - 1 - me)

    def zero(u):
        return remote(moved.at[0, u], gathered.at[sharer, 0, u], b_sem.at[2, u], b_sem.at[3, u], pencil=partner)

    def stay(u):
        return pltpu.make_async_copy(moved.at[0, u], gathered.at[sharer, 0, u], b_sem.at[4, u])

    plain = swapped(me < 0, (INNER, HALF), 1)
    edge = swapped(me == 0, (INNER, HALF), 1)
    for u in range(share):
        source_loads[u].wait()
        swap = swapped(first + u == 0, (INNER, INNER), 0)
        rows = [dot(swap, sources[u][local, c]).astype(bf16) for c in range(2)]
        for j in range(per):
            turn = edge if j == 0 else plain
            turned = [dot(rows[c][:, j * INNER : (j + 1) * INNER], turn) for c in range(2)]
            moved[(per - j) % per, u] = jnp.concatenate(turned, axis=1)

        if u == 0:
            pl.semaphore_wait(barrier, len(peers))
        rest(u).start()

        @pl.when(partner != me)
        def _(u=u):
            zero(u).start()

        @pl.when(partner == me)
        def _(u=u):
            stay(u).start()

    late_loads = [load(table_ref, tables), load(turns_ref, turns), load(kern_ref, kern),
                  load(back_high_ref, back_high), load(back_low_ref, back_low)]

    for copy in row_loads:
        copy.wait()
    offset = background_ref[member_ref[0]]

    def a_copy(chunk, shift, i):
        at = pl.ds(i * block, block)
        return remote(sending.at[chunk, shift, :, at], landing.at[chunk, shift - 1, :, at],
                      a_send_sem.at[chunk, shift - 1, i], a_recv_sem.at[chunk, shift - 1, i], pencil=toward(shift))

    for i in range(BLOCKS):
        dens_loads[i].wait()

        def step(b, carry, i=i):
            at = pl.ds(pl.multiple_of(b * 8, 8), 8)
            here = pl.ds(pl.multiple_of(i * block + b * 8, 8), 8)
            got = real_transform([dens[here, n * INNER : (n + 1) * INNER] - offset for n in range(RADIX)])
            pieces[0, at, :INNER] = got[0][0]
            pieces[0, at, INNER:] = got[8][0]
            for s in range(1, 8):
                pieces[s, at, :INNER] = got[s][0]
                pieces[s, at, INNER:] = got[s][1]
            return carry

        lax.fori_loop(0, block // 8, step, 0)

        def part(index, carry, i=i):
            shift, chunk = index // chunks, lax.rem(index, chunks)
            t = lax.rem(me + shift, pencils) * chunks + chunk
            total = None
            for odd in range(2):
                high, low = split_value(pieces[slot_at(2 * t + odd)])
                table_high = row_high[t, 256 * odd : 256 * odd + 256]
                table_low = row_low[t, 256 * odd : 256 * odd + 256]
                term = dot(high, table_high) + dot(low, table_high) + dot(high, table_low)
                total = term if total is None else total + term
            for c in range(2):
                sending[chunk, shift, c, i * block : (i + 1) * block] = total[:, c * 128 : (c + 1) * 128]
            return carry

        lax.fori_loop(0, pencils * chunks, part, 0)
        for shift in SHIFTS:
            a_copy(0, shift, i).start()

    def start_a(chunk):
        for i in range(BLOCKS):
            for shift in SHIFTS:
                a_copy(chunk, shift, i).start()

    def wait_a(chunk, blocks):
        for i in blocks:
            for shift in SHIFTS:
                a_copy(chunk, shift, i).wait_recv()

    for copy in late_loads:
        copy.wait()

    for u in range(share):
        rest(u).wait_recv()

        @pl.when(partner != me)
        def _(u=u):
            zero(u).wait_recv()
            zero(u).wait_send()

        @pl.when(partner == me)
        def _(u=u):
            stay(u).wait()

    own = gathered.at[sharer]
    far = (1 - grp) * 2 + mem
    across = remote(own, own, g_sem.at[0], g_sem.at[1], grp=1 - grp)
    across.start()
    beside = remote(own, own, g_sem.at[2], g_sem.at[3], mem=1 - mem)
    beside.start()
    wait_a(0, range(AHEAD))
    start_a(1)
    across.wait_recv()
    passed = remote(gathered.at[far], gathered.at[far], g_sem.at[4], g_sem.at[5], mem=1 - mem)
    passed.start()
    beside.wait_recv()
    passed.wait_recv()

    from_lane = lax.broadcasted_iota(jnp.int32, (2 * INNER, lanes), 0)
    to_lane = lax.broadcasted_iota(jnp.int32, (2 * INNER, lanes), 1)
    pick = jnp.where(from_lane == to_lane + jnp.where(to_lane < HALF, 0, HALF), 0.5, 0.0).astype(bf16)
    from_lane, to_lane = from_lane[:INNER], to_lane[:INNER]
    pick_edge = jnp.where((from_lane == HALF) & (to_lane == 0), 0.5, 0.0).astype(bf16)
    mask = (to_lane == 0) & (me == 0)

    def turned(r):
        c, s = turns[r, :, 0:1], turns[r, :, 1:2]
        pc, ps = phase_ref[me, r, 0], phase_ref[me, r, 1]
        return c * pc - s * ps, s * pc + c * ps

    def wave(r):
        re, im = spectra[r, :INNER], spectra[r, INNER:]
        c, s = turned(r)
        high, low = split_value(jnp.concatenate([re * c + im * s, im * c - re * s], axis=0))
        return dot(tables[0], high) + dot(tables[0], low) + dot(tables[1], high)

    def finish(chunk, r, got):
        re, im = got[:INNER], got[INNER:]
        rows = pl.ds(pl.multiple_of(r * INNER, INNER), INNER)
        holder, u = r // share, lax.rem(r, share)
        parts = []
        for c in range(2):
            other = [gathered[holder, 2 * chunk + j, u, :, c * HALF : (c + 1) * HALF] for j in range(2)]
            other = jnp.concatenate(other, axis=1)
            mine = dot(kern[local, c, rows, 2 * chunk * INNER : 2 * (chunk + 1) * INNER], pick)
            parts.append(mine + 0.5 * other if c == 0 else mine - 0.5 * other)
        kr, ki = parts
        if chunk == 0:
            other = lax.rem(RADIX - r, RADIX)
            other_rows = pl.ds(pl.multiple_of(other * INNER, INNER), INNER)
            swap = swapped(r == 0, (INNER, INNER), 0)
            edges = []
            for c in range(2):
                mine = dot(kern[local, c, rows, :INNER], pick_edge)
                flipped = dot(swap, kern[local, c, other_rows, :INNER]).astype(bf16)
                flipped = dot(flipped, pick_edge)
                edges.append(mine + flipped if c == 0 else mine - flipped)
            high, low = split_value(waves[other])
            ore = dot(swap, high[:INNER]) + dot(swap, low[:INNER])
            oim = -(dot(swap, high[INNER:]) + dot(swap, low[INNER:]))
            hr = jnp.where(mask, 0.5 * (kr - edges[0]), 0.0)
            hi = jnp.where(mask, 0.5 * (ki - edges[1]), 0.0)
            kr, ki = kr - hr, ki - hi
            sr = re * kr - im * ki + (ore * hr - oim * hi)
            si = re * ki + im * kr + (ore * hi + oim * hr)
        else:
            sr, si = re * kr - im * ki, re * ki + im * kr
        high, low = split_value(jnp.concatenate([sr, si], axis=0))
        got = dot(tables[2], high) + dot(tables[2], low) + dot(tables[3], high)
        re, im = got[:INNER], got[INNER:]
        c, s = turned(r)
        spectra[r, :INNER] = re * c - im * s
        spectra[r, INNER:] = im * c + re * s

    def columns(chunk):
        def forward(b, carry):
            values = []
            for n in range(RADIX):
                j, begin = divmod(n * INNER, part_rows)
                at = pl.ds(pl.multiple_of(begin + b * 8, 8), 8)
                ref = sending.at[chunk, 0] if j == 0 else landing.at[chunk, pencils - j - 1]
                values.append((ref[0, at, :], ref[1, at, :]))
            at = pl.ds(pl.multiple_of(b * 8, 8), 8)
            also = pl.ds(pl.multiple_of(INNER + b * 8, 8), 8)
            for r, (re, im) in enumerate(transform(values, -1)):
                spectra[r, at, :] = re
                spectra[r, also, :] = im
            return carry

        lax.fori_loop(0, INNER // 8, forward, 0)

        def early(i, carry):
            for u in range(UNROLL):
                waves[i * UNROLL + u] = wave(i * UNROLL + u)
            return carry

        def late(i, carry):
            for u in range(UNROLL):
                r = i * UNROLL + u
                finish(chunk, r, waves[r] if chunk == 0 else wave(r))
            return carry

        if chunk == 0:
            lax.fori_loop(0, RADIX // UNROLL, early, 0)
        lax.fori_loop(0, RADIX // UNROLL, late, 0)

        def backward(b, carry):
            at = pl.ds(pl.multiple_of(b * 8, 8), 8)
            also = pl.ds(pl.multiple_of(INNER + b * 8, 8), 8)
            values = [(spectra[r, at, :], spectra[r, also, :]) for r in range(RADIX)]
            for n, (re, im) in enumerate(transform(values, 1)):
                shift_depth, begin = divmod(n * INNER, out_rows)
                shift, depth = divmod(shift_depth, depths)
                put = pl.ds(pl.multiple_of(begin + b * 8, 8), 8)
                slot = jnp.where(deep == depth, 0, 1)
                keep[chunk, slot, shift, 0, put, :] = re
                keep[chunk, slot, shift, 1, put, :] = im
            return carry

        lax.fori_loop(0, INNER // 8, backward, 0)

    def x_copy(chunk, j):
        return remote(keep.at[chunk, 1, j], other_keep.at[chunk, j], x_sem.at[0, chunk, j], x_sem.at[1, chunk, j],
                      depth=1 - deep)

    out_block = out_rows // PARTS

    def c_copy(chunk, j, i):
        at = pl.ds(i * out_block, out_block)
        return remote(keep.at[chunk, 0, j, :, at], fields.at[chunk, j - 1, :, at],
                      c_sem.at[0, chunk, j - 1, i], c_sem.at[1, chunk, j - 1, i], pencil=toward(j))

    def start_c(chunk, j):
        if j:
            for i in range(PARTS):
                c_copy(chunk, j, i).start()

    def summed(chunk, j):
        x_copy(chunk, j).wait_recv()
        keep[chunk, 0, j] += other_keep[chunk, j]

    def gather_field(chunk, shift, i):
        t = lax.rem(me + pencils - shift, pencils) * chunks + chunk
        at = pl.ds(i * out_block, out_block)
        ref = keep.at[chunk, 0, 0] if shift == 0 else fields.at[chunk, shift - 1]
        high, low = split_value(jnp.concatenate([ref[0, at], ref[1, at]], axis=1))
        for odd in range(2):
            r = 2 * t + odd
            half[slot_at(r), at] += dot(high, back_high[r]) + dot(low, back_high[r]) + dot(high, back_low[r])

    def last(b, carry):
        at = pl.ds(pl.multiple_of(b * 8, 8), 8)
        values = [(half[0, at, :INNER], None)]
        for s in range(1, 8):
            values.append((half[s, at, :INNER], half[s, at, INNER:]))
        values.append((half[0, at, INNER:], None))
        for n, value in enumerate(real_inverse(values)):
            out_ref[0, at, n * INNER : (n + 1) * INNER] = value
        return carry

    half[...] = jnp.zeros_like(half)
    wait_a(0, range(AHEAD, BLOCKS))
    columns(0)
    for j in ORDER:
        x_copy(0, j).start()
    for j in ORDER:
        summed(0, j)
    wait_a(1, range(BEFORE))
    for j in ORDER:
        start_c(0, j)
    wait_a(1, range(BEFORE, BLOCKS))
    columns(1)
    for j in ORDER:
        x_copy(1, j).start()
    for i in range(PARTS):
        gather_field(0, 0, i)
    for j in ORDER:
        summed(1, j)
        start_c(1, j)
    for i in range(PARTS):
        gather_field(1, 0, i)
    for j in ORDER:
        if j:
            for i in range(PARTS):
                c_copy(0, j, i).wait_recv()
                gather_field(0, j, i)
    for i in range(PARTS):
        for j in ORDER:
            if j:
                c_copy(1, j, i).wait_recv()
                gather_field(1, j, i)
        lax.fori_loop(i * out_block // 8, (i + 1) * out_block // 8, last, 0)

    for u in range(share):
        rest(u).wait_send()
    across.wait_send()
    beside.wait_send()
    passed.wait_send()
    for chunk in range(chunks):
        for shift in SHIFTS:
            for i in range(BLOCKS):
                a_copy(chunk, shift, i).wait_send()
        for j in ORDER:
            x_copy(chunk, j).wait_send()
            if j:
                for i in range(PARTS):
                    c_copy(chunk, j, i).wait_send()


SHIFTS = (2, 1, 3)
ORDER = (2, 1, 3, 0)
UNROLL = 4
AHEAD = 3
BEFORE = 4
PARTS = 2


def params(**more):
    return pltpu.CompilerParams(vmem_limit_bytes=48 * 1024 * 1024, **more)


def wide_body(density, background, member_ids, layer_kernel, kernel_spectra):
    pencils = lax.axis_size("pencil")
    depths = lax.axis_size("depth")
    sharers = lax.axis_size("grp") * lax.axis_size("mem")
    pencil = lax.axis_index("pencil")
    per = RADIX // pencils
    width = min(per, 2)
    chunks = per // width
    lanes = width * HALF
    part_rows = density.shape[2]
    out_rows = part_rows // depths
    vmem = pl.BlockSpec(memory_space=pltpu.VMEM)
    smem = pl.BlockSpec(memory_space=pltpu.SMEM)

    kern_count = kernel_spectra.shape[0]
    local = layer_kernel[0] - lax.axis_index("depth") * kern_count
    share = RADIX // sharers
    first = lax.axis_index(("grp", "mem")) * share
    groups = [1] if per == 1 else [1, per - 1]
    moved = pl.pallas_call(
        functools.partial(mirror_kernel, share),
        grid_spec=pltpu.PrefetchScalarGridSpec(
            num_scalar_prefetch=1,
            grid=(1,),
            in_specs=[
                pl.BlockSpec(
                    (None, 2, INNER, per * INNER),
                    lambda i, w, u=u: (w[0], 0, lax.rem(RADIX - w[1] - u, RADIX), 0),
                )
                for u in range(share)
            ],
            out_specs=[pl.BlockSpec((g, share, INNER, INNER), lambda i, w: (0, 0, 0, 0)) for g in groups],
        ),
        out_shape=[jax.ShapeDtypeStruct((g, share, INNER, INNER), f32) for g in groups],
        compiler_params=params(),
        cost_estimate=pl.CostEstimate(flops=1 << 20, bytes_accessed=2 << 20, transcendentals=0),
    )(jnp.stack([local, first, pencil]), *[kernel_spectra] * share)
    mirrored = lax.ppermute(moved[0], "pencil", [(p, (pencils - p) % pencils) for p in range(pencils)])
    if per > 1:
        rest = lax.ppermute(moved[1], "pencil", [(p, pencils - 1 - p) for p in range(pencils)])

    offset = lax.dynamic_index_in_dim(background[:, 0], member_ids[0], 0, keepdims=True)
    row_high, row_low = halves(row_tables())
    block = min(part_rows, 128)
    sent = pl.pallas_call(
        functools.partial(rows_kernel, pencils, width),
        grid=(part_rows // block,),
        in_specs=[
            smem,
            pl.BlockSpec((None, None, block, LENGTH), lambda i: (0, 0, i, 0)),
            pl.BlockSpec((8, 512, 256), lambda i: (0, 0, 0)),
            pl.BlockSpec((8, 512, 256), lambda i: (0, 0, 0)),
        ],
        out_specs=[pl.BlockSpec((pencils, 2, block, lanes), lambda i: (0, 0, i, 0))] * chunks,
        out_shape=[jax.ShapeDtypeStruct((pencils, 2, part_rows, lanes), f32)] * chunks,
        scratch_shapes=[pltpu.VMEM((8, block, 256), f32)],
        compiler_params=params(),
        cost_estimate=pl.CostEstimate(flops=6 * part_rows * 2 * LENGTH * 512, bytes_accessed=12 << 20, transcendentals=0),
    )(offset, density, row_high, row_low)
    arrived = [lax.all_to_all(part, "pencil", 0, 0, tiled=True) for part in sent]

    sign = jnp.array([0.5, -0.5], f32)
    edge = lax.dynamic_slice(kernel_spectra, (local, 0, 0, HALF), (1, 2, LENGTH, 1))
    edge = edge.reshape(2, RADIX, INNER).astype(f32)
    flipped = jnp.concatenate([edge[:, :1], edge[:, :0:-1]], axis=1)[..., ::-1]
    flipped = jnp.concatenate([jnp.roll(flipped[:, :1], 1, axis=2), flipped[:, 1:]], axis=1)
    edge = 0.5 * edge + sign.reshape(2, 1, 1) * flipped
    edge = jnp.where(lax.broadcasted_iota(jnp.int32, (lanes,), 0) == 0, edge[..., None], 0.0)

    if per > 1:
        mirrored = jnp.concatenate([mirrored, rest], axis=0)
    mirrored, edge, _ = lax.optimization_barrier((mirrored, edge, sent[0]))
    mirrored = lax.all_gather(mirrored, ("grp", "mem"), axis=0)

    column, column_turns = column_tables()
    column_turns = jnp.asarray(column_turns)
    tables = jnp.stack(halves(column) + halves(column.T))
    two = depths == 2
    mine = lax.axis_index("depth") if two else jnp.int32(0)
    where = jnp.stack([mine, local, pencil])
    fields = []
    before = None
    for k in range(chunks):
        special = k == 0
        steps = sharers

        def early(i, special=special):
            return jnp.minimum(i, steps - 1) if special else i

        def late(i, special=special):
            return jnp.maximum(i - steps, 0) if special else i

        here = arrived[k]
        if before is not None:
            here, before = lax.optimization_barrier((here, before))
            fields.append(lax.all_to_all(before, "pencil", 0, 0, tiled=True))
        edge_block = (2, share, INNER, lanes) if special else (2, 1, 8, lanes)
        out = pl.pallas_call(
            functools.partial(columns_kernel, special),
            grid_spec=pltpu.PrefetchScalarGridSpec(
                num_scalar_prefetch=1,
                grid=(2 * steps if special else steps,),
                in_specs=[
                    pl.BlockSpec((pencils, 2, part_rows, lanes), lambda i, w: (0, 0, 0, 0)),
                    pl.BlockSpec(
                        (None, 2, share * INNER, width * INNER), lambda i, w, k=k, late=late: (w[1], 0, late(i), k)
                    ),
                    pl.BlockSpec(
                        (None, width, share, INNER, INNER), lambda i, w, k=k, late=late: (late(i), k, 0, 0, 0)
                    ),
                    pl.BlockSpec(
                        edge_block,
                        (lambda i, w, late=late: (0, late(i), 0, 0)) if special else (lambda i, w: (0, 0, 0, 0)),
                    ),
                ]
                + [pl.BlockSpec((share, INNER, INNER), lambda i, w, early=early: (early(i), 0, 0))]
                + [pl.BlockSpec((share, INNER, INNER), lambda i, w, late=late: (late(i), 0, 0))]
                + [pl.BlockSpec((4, 256, 256), lambda i, w: (0, 0, 0))],
                out_specs=pl.BlockSpec((depths, pencils, 2, out_rows, lanes), lambda i, w: (0, 0, 0, 0, 0)),
                scratch_shapes=[
                    pltpu.VMEM((RADIX, 256, lanes), f32),
                    pltpu.VMEM((RADIX if special else 1, 256, lanes), f32),
                ],
            ),
            out_shape=jax.ShapeDtypeStruct((depths, pencils, 2, out_rows, lanes), f32),
            compiler_params=params(),
            cost_estimate=pl.CostEstimate(
                flops=12 * RADIX * 256 * 256 * lanes, bytes_accessed=16 << 20, transcendentals=0
            ),
        )(where, here, kernel_spectra, mirrored, edge, column_turns, column_turns, tables)
        if two:
            before = out[0] + lax.ppermute(out[1], "depth", [(0, 1), (1, 0)])
        else:
            before = lax.psum_scatter(out, "depth", scatter_dimension=0, tiled=False)
    fields.append(lax.all_to_all(before, "pencil", 0, 0, tiled=True))

    back_high, back_low = halves(inverse_row_tables())
    return pl.pallas_call(
        functools.partial(fields_kernel, pencils, width, [1] * chunks),
        in_specs=[vmem] * (len(fields) + 2),
        out_specs=vmem,
        out_shape=jax.ShapeDtypeStruct((1, out_rows, LENGTH), f32),
        scratch_shapes=[pltpu.VMEM((8, out_rows, 256), f32)],
        compiler_params=params(),
        cost_estimate=pl.CostEstimate(flops=6 * out_rows * 2 * LENGTH * 512, bytes_accessed=8 << 20, transcendentals=0),
    )(*fields, back_high, back_low)


def fused_body(density, background, member_ids, layer_kernel, kernel_spectra):
    pencils = lax.axis_size("pencil")
    depths = lax.axis_size("depth")
    sharers = lax.axis_size("grp") * lax.axis_size("mem")
    per = RADIX // pencils
    chunks = per // 2
    lanes = 2 * HALF
    part_rows = density.shape[2]
    out_rows = part_rows // depths
    share = RADIX // sharers
    smem = pl.BlockSpec(memory_space=pltpu.SMEM)
    anywhere = pl.BlockSpec(memory_space=pl.ANY)
    vmem = pl.BlockSpec(memory_space=pltpu.VMEM)

    angles = 2 * np.pi * np.arange(pencils)[:, None] * np.arange(RADIX)[None, :] / pencils
    phases = jnp.asarray(np.stack([np.cos(angles), np.sin(angles)], axis=-1).round(15), f32)
    row_high, row_low = halves(row_tables())
    where = [0 if r == 8 else min(r, RADIX - r) for r in range(RADIX)], [int(r >= 8) for r in range(RADIX)]
    back_high, back_low = halves(inverse_row_tables().reshape(8, 2, 256, 256)[where])
    column, turns = column_tables()
    tables = jnp.stack(halves(column) + halves(column.T))
    turns = jnp.asarray(turns)
    dma = pltpu.SemaphoreType.DMA
    return pl.pallas_call(
        functools.partial(fused_kernel, pencils, depths),
        in_specs=[smem] * 4 + [anywhere] * 8,
        out_specs=vmem,
        out_shape=jax.ShapeDtypeStruct((1, out_rows, LENGTH), f32),
        scratch_shapes=[
            pltpu.VMEM((part_rows, LENGTH), f32),
            [pltpu.VMEM((kernel_spectra.shape[0], 2, INNER, per * INNER), bf16)] * share,
            pltpu.VMEM(kernel_spectra.shape, bf16),
            pltpu.VMEM(row_high.shape, bf16),
            pltpu.VMEM(row_low.shape, bf16),
            pltpu.VMEM(back_high.shape, bf16),
            pltpu.VMEM(back_low.shape, bf16),
            pltpu.VMEM(tables.shape, bf16),
            pltpu.VMEM(turns.shape, f32),
            pltpu.VMEM((8, part_rows // BLOCKS, 256), f32),
            pltpu.VMEM((chunks, pencils, 2, part_rows, lanes), f32),
            pltpu.VMEM((chunks, pencils - 1, 2, part_rows, lanes), f32),
            pltpu.VMEM((per, share, INNER, INNER), f32),
            pltpu.VMEM((sharers, per, share, INNER, INNER), f32),
            pltpu.VMEM((RADIX, 256, lanes), f32),
            pltpu.VMEM((RADIX, 256, lanes), f32),
            pltpu.VMEM((chunks, 2, pencils, 2, out_rows, lanes), f32),
            pltpu.VMEM((chunks, pencils, 2, out_rows, lanes), f32),
            pltpu.VMEM((chunks, pencils - 1, 2, out_rows, lanes), f32),
            pltpu.VMEM((8, out_rows, 256), f32),
            dma((share + BLOCKS + 7,)),
            dma((5, share)),
            dma((6,)),
            dma((chunks, pencils - 1, BLOCKS)),
            dma((chunks, pencils - 1, BLOCKS)),
            dma((2, chunks, pencils)),
            dma((2, chunks, pencils - 1, PARTS)),
        ],
        compiler_params=pltpu.CompilerParams(
            vmem_limit_bytes=60 * 1024 * 1024, collective_id=0, has_side_effects=True
        ),
    )(background.reshape(-1), member_ids, layer_kernel, phases, density, kernel_spectra, row_high, row_low, back_high, back_low, tables, turns)


def body(density, background, member_ids, layer_kernel, kernel_spectra):
    sizes = tuple(lax.axis_size(name) for name in ("grp", "pencil", "depth", "mem"))
    plan = fused_body if sizes == (2, 4, 2, 2) else wide_body
    return plan(density, background, member_ids, layer_kernel, kernel_spectra)


def solution(mesh):
    placed = (
        P(("grp", "mem"), "depth", "pencil", None),
        P(None, "depth"),
        P(("grp", "mem")),
        P("depth"),
        P("depth", None, None, "pencil"),
    )
    return jax.shard_map(
        body,
        mesh=mesh,
        in_specs=placed,
        out_specs=P(("grp", "mem"), ("pencil", "depth"), None),
        check_vma=False,
    )
```

```python
import functools
import math

import jax
import jax.numpy as jnp
import numpy as np
from jax import lax
from jax.experimental import pallas as pl
from jax.experimental.pallas import tpu as pltpu
from jax.sharding import PartitionSpec as P

RADIX = 16
INNER = 128
HALF = 64
LENGTH = RADIX * INNER
f32 = jnp.float32
bf16 = jnp.bfloat16


def halves(table):
    table = np.asarray(table, np.float32)
    high = table.astype(bf16)
    low = (table - high.astype(np.float32)).astype(bf16)
    return jnp.asarray(high), jnp.asarray(low)


def residue_rows(r):
    m = np.arange(INNER)[:, None]
    q = np.arange(HALF)[None, :]
    turn = np.exp(-2j * np.pi * (((RADIX * q + r) * m) % LENGTH) / LENGTH)
    re, im = turn.real.copy(), turn.imag.copy()
    if r == 0:
        im[:, 0] = (-1.0) ** m[:, 0]
    out = np.zeros((2 * INNER, 2 * HALF))
    if r == 0:
        out[:INNER, :HALF], out[:INNER, HALF:] = re, im
    elif r == 8:
        out[INNER:, :HALF], out[INNER:, HALF:] = re, im
    else:
        sign = 1.0 if r < 8 else -1.0
        out[:INNER, :HALF], out[:INNER, HALF:] = re, im
        out[INNER:, :HALF], out[INNER:, HALF:] = -sign * im, sign * re
    return out


def slot_of(r):
    return 0 if r in (0, 8) else min(r, RADIX - r)


def row_tables():
    tables = np.zeros((8, 512, 256))
    for t in range(8):
        for odd in range(2):
            block = residue_rows(2 * t + odd)
            rows = slice(256 * odd, 256 * odd + 256)
            tables[t, rows, HALF * odd : HALF * odd + HALF] = block[:, :HALF]
            tables[t, rows, 128 + HALF * odd : 128 + HALF * odd + HALF] = block[:, HALF:]
    return tables


def inverse_row_tables():
    tables = np.zeros((8, 512, 256))
    scale = 1.0 / (LENGTH * LENGTH)
    for s in range(8):
        for place, r in enumerate((s, 8 if s == 0 else RADIX - s)):
            block = residue_rows(r).T.copy() * scale
            weight = np.full((2 * HALF, 1), 2.0 if r in (0, 8) else 1.0)
            if r == 0:
                weight[0] = weight[HALF] = 1.0
            block *= weight
            odd = r % 2
            tables[s, 256 * place + HALF * odd : 256 * place + HALF * odd + HALF] += block[:HALF]
            tables[s, 256 * place + 128 + HALF * odd : 256 * place + 128 + HALF * odd + HALF] += block[HALF:]
    return tables


def column_tables():
    q = np.arange(INNER)[:, None]
    m = np.arange(INNER)[None, :]
    turn = np.exp(-2j * np.pi * ((q * m) % INNER) / INNER)
    table = np.block([[turn.real, -turn.imag], [turn.imag, turn.real]])
    angles = 2 * np.pi * np.arange(RADIX)[:, None] * np.arange(INNER)[None, :] / LENGTH
    turns = np.zeros((RADIX, INNER, INNER), np.float32)
    turns[..., 0] = np.cos(angles)
    turns[..., 1] = np.sin(angles)
    return table, turns


def split_value(value):
    high = value.astype(bf16)
    return high, (value - high.astype(f32)).astype(bf16)


def dot(a, b):
    return jnp.dot(a, b, preferred_element_type=f32)


def rotate(value, count, length, sign):
    re, im = value
    count %= length
    if count == 0:
        return value
    if 4 * count == length:
        return (im, -re) if sign < 0 else (-im, re)
    c = math.cos(2 * math.pi * count / length)
    s = sign * math.sin(2 * math.pi * count / length)
    if 8 * count == length:
        return ((re + im) * c, (im - re) * c) if sign < 0 else ((re - im) * c, (im + re) * c)
    return (re * c - im * s, re * s + im * c)


def plus(a, b):
    return (a[0] + b[0], a[1] + b[1])


def minus(a, b):
    return (a[0] - b[0], a[1] - b[1])


def transform(values, sign):
    length = len(values)
    if length == 1:
        return values
    even, odd = transform(values[0::2], sign), transform(values[1::2], sign)
    turned = [rotate(odd[k], k, length, sign) for k in range(length // 2)]
    return [plus(even[k], turned[k]) for k in range(length // 2)] + [
        minus(even[k], turned[k]) for k in range(length // 2)
    ]


def real_transform(values):
    length = len(values)
    if length == 2:
        return [(values[0] + values[1], None), (values[0] - values[1], None)]
    even, odd = real_transform(values[0::2]), real_transform(values[1::2])
    out = [None] * (length // 2 + 1)
    out[0] = (even[0][0] + odd[0][0], None)
    out[length // 2] = (even[0][0] - odd[0][0], None)
    quarter = length // 4
    for k in range(1, quarter):
        turned = rotate(odd[k], k, length, -1)
        out[k] = plus(even[k], turned)
        low = minus(even[k], turned)
        out[length // 2 - k] = (low[0], -low[1])
    out[quarter] = (even[quarter][0], -odd[quarter][0])
    return out


def real_inverse(values):
    half = len(values) - 1
    length = 2 * half
    if length == 2:
        return [values[0][0] + values[1][0], values[0][0] - values[1][0]]
    even, odd = [], []
    for k in range(half // 2 + 1):
        if k == 0:
            even.append((values[0][0] + values[half][0], None))
            odd.append((values[0][0] - values[half][0], None))
        elif k == half // 2:
            even.append((2.0 * values[k][0], None))
            odd.append((-2.0 * values[k][1], None))
        else:
            other = values[half - k]
            even.append((values[k][0] + other[0], values[k][1] - other[1]))
            odd.append(rotate((values[k][0] - other[0], values[k][1] + other[1]), k, length, 1))
    first, second = real_inverse(even), real_inverse(odd)
    return [x for pair in zip(first, second) for x in pair]


def rows_kernel(pencils, width, offset_ref, in_ref, high_ref, low_ref, *rest):
    outs, pieces = rest[:-1], rest[-1]
    rows = in_ref.shape[0]
    per = RADIX // pencils
    offset = offset_ref[0]

    def step(b, carry):
        at = pl.ds(pl.multiple_of(b * 8, 8), 8)
        values = [in_ref[at, n * INNER : (n + 1) * INNER] - offset for n in range(RADIX)]
        got = real_transform(values)
        pieces[0, at, :INNER] = got[0][0]
        pieces[0, at, INNER:] = got[8][0]
        for s in range(1, 8):
            pieces[s, at, :INNER] = got[s][0]
            pieces[s, at, INNER:] = got[s][1]
        return carry

    lax.fori_loop(0, rows // 8, step, 0)
    for t in range(8):
        total = None
        for odd in range(2):
            high, low = split_value(pieces[slot_of(2 * t + odd)])
            table_high = high_ref[t, 256 * odd : 256 * odd + 256]
            table_low = low_ref[t, 256 * odd : 256 * odd + 256]
            part = dot(high, table_high) + dot(low, table_high) + dot(high, table_low)
            total = part if total is None else total + part
        if width == 2:
            pencil, place = divmod(2 * t, per)
            for c in range(2):
                outs[place // 2][pencil, c] = total[:, c * 128 : (c + 1) * 128]
        else:
            for odd in range(2):
                pencil, place = divmod(2 * t + odd, per)
                for c in range(2):
                    begin = c * 128 + odd * HALF
                    outs[place][pencil, c] = total[:, begin : begin + HALF]


def swapped(zero, shape, axis):
    total = lax.broadcasted_iota(jnp.int32, shape, 0) + lax.broadcasted_iota(jnp.int32, shape, 1)
    wanted = jnp.where(zero, INNER, INNER - 1)
    also = jnp.where(zero, 0, INNER - 1)
    return jnp.where((total == wanted) | (total == also), 1.0, 0.0).astype(bf16)


def mirror_kernel(share, where_ref, *refs):
    ins, zero_ref, rest_refs = refs[:share], refs[share], refs[share + 1 :]
    per = ins[0].shape[2] // INNER
    plain = swapped(where_ref[1] < 0, (INNER, HALF), 1)
    edge = swapped(where_ref[2] == 0, (INNER, HALF), 1)
    for u in range(share):
        swap = swapped(where_ref[1] + u == 0, (INNER, INNER), 0)
        rows = [dot(swap, ins[u][c]).astype(bf16) for c in range(2)]
        for j in range(per):
            turn = edge if j == 0 else plain
            turned = [dot(rows[c][:, j * INNER : (j + 1) * INNER], turn) for c in range(2)]
            value = jnp.concatenate(turned, axis=1)
            if j == 0:
                zero_ref[0, u] = value
            else:
                rest_refs[0][per - 1 - j, u] = value


def columns_kernel(special, where_ref, in_ref, kern_ref, mirror_ref, edge_ref,
                   turns_ref, late_ref, table_ref, out_ref, pieces, waves):
    part_rows = in_ref.shape[2]
    depths, pencils, _, out_rows, lanes = out_ref.shape
    share = mirror_ref.shape[1]
    steps = RADIX // share
    mine = where_ref[0]
    now = pl.program_id(0)
    from_lane = lax.broadcasted_iota(jnp.int32, (kern_ref.shape[2], lanes), 0)
    to_lane = lax.broadcasted_iota(jnp.int32, (kern_ref.shape[2], lanes), 1)
    wanted = to_lane + jnp.where(to_lane < HALF, 0, HALF)
    pick = jnp.where(from_lane == wanted, 0.5, 0.0).astype(bf16)
    zero_swap = swapped(mine >= 0, (INNER, INNER), 0)
    plain_swap = swapped(mine < 0, (INNER, INNER), 0)

    def forward(b, carry):
        values = []
        for n in range(RADIX):
            source, begin = divmod(n * INNER, part_rows)
            at = pl.ds(pl.multiple_of(begin + b * 8, 8), 8)
            values.append((in_ref[source, 0, at, :], in_ref[source, 1, at, :]))
        at = pl.ds(pl.multiple_of(b * 8, 8), 8)
        also = pl.ds(pl.multiple_of(INNER + b * 8, 8), 8)
        for r, (re, im) in enumerate(transform(values, -1)):
            pieces[r, at, :] = re
            pieces[r, also, :] = im
        return carry

    @pl.when(now == 0)
    def _():
        lax.fori_loop(0, INNER // 8, forward, 0)

    def wave(r, u):
        re, im = pieces[r, :INNER], pieces[r, INNER:]
        c, s = turns_ref[u, :, 0:1], turns_ref[u, :, 1:2]
        high, low = split_value(jnp.concatenate([re * c + im * s, im * c - re * s], axis=0))
        return dot(table_ref[0], high) + dot(table_ref[0], low) + dot(table_ref[1], high)

    def finish(r, u, got):
        re, im = got[:INNER], got[INNER:]
        tiles = [mirror_ref[j, u] for j in range(mirror_ref.shape[0])]
        rows = slice(u * INNER, (u + 1) * INNER)
        parts = []
        for c in range(2):
            other = [tile[:, c * HALF : (c + 1) * HALF] for tile in tiles]
            other = jnp.concatenate(other, axis=1) if len(other) > 1 else other[0]
            own = dot(kern_ref[c, rows, :], pick)
            parts.append(own + 0.5 * other if c == 0 else own - 0.5 * other)
        kr, ki = parts
        if special:
            other = lax.rem(RADIX - r, RADIX)
            high, low = split_value(waves[other])
            swap = jnp.where(r == 0, zero_swap.astype(f32), plain_swap.astype(f32)).astype(bf16) if u == 0 else plain_swap
            ore = dot(swap, high[:INNER]) + dot(swap, low[:INNER])
            oim = -(dot(swap, high[INNER:]) + dot(swap, low[INNER:]))
            mask = (lax.broadcasted_iota(jnp.int32, (INNER, lanes), 1) == 0) & (where_ref[2] == 0)
            hr = jnp.where(mask, 0.5 * (kr - edge_ref[0, u]), 0.0)
            hi = jnp.where(mask, 0.5 * (ki - edge_ref[1, u]), 0.0)
            kr, ki = kr - hr, ki - hi
            sr = re * kr - im * ki + (ore * hr - oim * hi)
            si = re * ki + im * kr + (ore * hi + oim * hr)
        else:
            sr, si = re * kr - im * ki, re * ki + im * kr
        spectrum = jnp.concatenate([sr, si], axis=0)
        high, low = split_value(spectrum)
        got = dot(table_ref[2], high) + dot(table_ref[2], low) + dot(table_ref[3], high)
        re, im = got[:INNER], got[INNER:]
        c, s = late_ref[u, :, 0:1], late_ref[u, :, 1:2]
        pieces[r, :INNER] = re * c - im * s
        pieces[r, INNER:] = im * c + re * s

    if special:
        @pl.when(now < steps)
        def _():
            for u in range(share):
                waves[now * share + u] = wave(now * share + u, u)

        @pl.when(now >= steps)
        def _():
            for u in range(share):
                r = (now - steps) * share + u
                finish(r, u, waves[r])
    else:
        for u in range(share):
            r = now * share + u
            finish(r, u, wave(r, u))

    slots = [lax.rem(d - mine + depths, depths) for d in range(depths)]

    def backward(b, carry):
        at = pl.ds(pl.multiple_of(b * 8, 8), 8)
        also = pl.ds(pl.multiple_of(INNER + b * 8, 8), 8)
        values = [(pieces[r, at, :], pieces[r, also, :]) for r in range(RADIX)]
        for n, (re, im) in enumerate(transform(values, 1)):
            if out_rows % INNER == 0:
                part, begin = divmod(n * INNER, out_rows)
                pencil, depth = divmod(part, depths)
                depth = slots[depth]
                put = pl.ds(pl.multiple_of(begin + b * 8, 8), 8)
            else:
                x = n * INNER + b * 8
                pencil = x // (out_rows * depths)
                depth = lax.rem(x // out_rows - mine + depths, depths)
                put = pl.ds(pl.multiple_of(lax.rem(x, out_rows), 8), 8)
            out_ref[depth, pencil, 0, put, :] = re
            out_ref[depth, pencil, 1, put, :] = im
        return carry

    @pl.when(now == pl.num_programs(0) - 1)
    def _():
        lax.fori_loop(0, INNER // 8, backward, 0)


def fields_kernel(pencils, width, counts, *refs):
    ins, at = [], 0
    for count in counts:
        ins.append(refs[at : at + count])
        at += count
    high_ref, low_ref, out_ref, pieces = refs[at:]
    per = RADIX // pencils
    rows = out_ref.shape[1]

    def read(chunk, pencil, c):
        found = [ref[pencil, c] for ref in ins[chunk]]
        return jnp.concatenate(found, axis=0) if len(found) > 1 else found[0]

    def pair(t):
        if width == 2:
            pencil, place = divmod(2 * t, per)
            return jnp.concatenate([read(place // 2, pencil, c) for c in range(2)], axis=1)
        found = []
        for c in range(2):
            for odd in range(2):
                pencil, place = divmod(2 * t + odd, per)
                found.append(read(place, pencil, c))
        return jnp.concatenate(found, axis=1)

    for s in range(8):
        total = None
        for place, r in enumerate((s, 8 if s == 0 else RADIX - s)):
            high, low = split_value(pair(r // 2))
            table_high = high_ref[s, 256 * place : 256 * place + 256]
            table_low = low_ref[s, 256 * place : 256 * place + 256]
            part = dot(high, table_high) + dot(low, table_high) + dot(high, table_low)
            total = part if total is None else total + part
        pieces[s] = total

    def step(b, carry):
        at = pl.ds(pl.multiple_of(b * 8, 8), 8)
        values = [(pieces[0, at, :INNER], None)]
        for s in range(1, 8):
            values.append((pieces[s, at, :INNER], pieces[s, at, INNER:]))
        values.append((pieces[0, at, INNER:], None))
        for n, value in enumerate(real_inverse(values)):
            out_ref[0, at, n * INNER : (n + 1) * INNER] = value
        return carry

    lax.fori_loop(0, rows // 8, step, 0)


def slot_at(r):
    return jnp.where(r == 8, 0, jnp.minimum(r, RADIX - r))


BLOCKS = 4


def fused_kernel(pencils, depths, background_ref, member_ref, layer_ref, phase_ref, density_ref, kern_ref, row_high_ref, row_low_ref,
                 back_high_ref, back_low_ref, table_ref, turns_ref, out_ref,
                 dens, sources, kern, row_high, row_low, back_high, back_low, tables, turns,
                 pieces, sending, landing, moved, gathered, spectra, waves, keep, other_keep, fields, half,
                 local_sem, b_sem, g_sem, a_send_sem, a_recv_sem, x_sem, c_sem):
    per = RADIX // pencils
    chunks = per // 2
    lanes = 2 * HALF
    part_rows = dens.shape[0]
    block = part_rows // BLOCKS
    out_rows = part_rows // depths
    share = moved.shape[0]
    me = lax.axis_index("pencil")
    deep = lax.axis_index("depth")
    grp, mem = lax.axis_index("grp"), lax.axis_index("mem")
    sharer = grp * 2 + mem
    first = sharer * share
    local = jnp.clip(layer_ref[0] - deep * kern.shape[0], 0, kern.shape[0] - 1)

    def remote(src, dst, send, recv, **where):
        return pltpu.make_async_remote_copy(
            src_ref=src, dst_ref=dst, send_sem=send, recv_sem=recv,
            device_id=where, device_id_type=pl.DeviceIdType.MESH,
        )

    def toward(shift):
        return lax.rem(me + shift, pencils)

    loads = []

    def load(src, dst):
        copy = pltpu.make_async_copy(src, dst, local_sem.at[len(loads)])
        copy.start()
        loads.append(copy)
        return copy

    source_loads = [
        load(kern_ref.at[:, :, pl.ds(pl.multiple_of(lax.rem(RADIX - first - u, RADIX) * INNER, INNER), INNER)], sources[u])
        for u in range(share)
    ]
    barrier = pltpu.get_barrier_semaphore()
    peers = [{"pencil": toward(shift)} for shift in range(1, pencils)]
    peers += [{"depth": 1 - deep}, {"grp": 1 - grp}, {"mem": 1 - mem}]
    for peer in peers:
        pl.semaphore_signal(barrier, inc=1, device_id=peer, device_id_type=pl.DeviceIdType.MESH)

    row_loads = [load(row_high_ref, row_high), load(row_low_ref, row_low)]
    dens_loads = [load(density_ref.at[0, 0, pl.ds(i * block, block)], dens.at[pl.ds(i * block, block)]) for i in range(BLOCKS)]
    partner = lax.rem(pencils - me, pencils)

    def rest(u):
        at = pl.ds(1, per - 1)
        return remote(moved.at[u, at], gathered.at[sharer, u, at], b_sem.at[0, u], b_sem.at[1, u], pencil=pencils - 1 - me)

    def zero(u):
        return remote(moved.at[u, 0], gathered.at[sharer, u, 0], b_sem.at[2, u], b_sem.at[3, u], pencil=partner)

    def stay(u):
        return pltpu.make_async_copy(moved.at[u, 0], gathered.at[sharer, u, 0], b_sem.at[4, u])

    plain = swapped(me < 0, (INNER, HALF), 1)
    edge = swapped(me == 0, (INNER, HALF), 1)
    for u in range(share):
        source_loads[u].wait()
        swap = swapped(first + u == 0, (INNER, INNER), 0)
        rows = [dot(swap, sources[u][local, c]).astype(bf16) for c in range(2)]
        for j in range(per):
            turn = edge if j == 0 else plain
            turned = [dot(rows[c][:, j * INNER : (j + 1) * INNER], turn) for c in range(2)]
            moved[u, (per - j) % per] = jnp.concatenate(turned, axis=1)

        if u == 0:
            pl.semaphore_wait(barrier, len(peers))
        rest(u).start()

        @pl.when(partner != me)
        def _(u=u):
            zero(u).start()

        @pl.when(partner == me)
        def _(u=u):
            stay(u).start()

    late_loads = [load(table_ref, tables), load(turns_ref, turns), load(kern_ref, kern),
                  load(back_high_ref, back_high), load(back_low_ref, back_low)]

    for copy in row_loads:
        copy.wait()
    offset = background_ref[member_ref[0]]

    def a_copy(chunk, shift, i):
        return remote(sending.at[chunk, shift, i], landing.at[chunk, shift - 1, i],
                      a_send_sem.at[chunk, shift - 1, i], a_recv_sem.at[chunk, shift - 1, i], pencil=toward(shift))

    for i in range(BLOCKS):
        dens_loads[i].wait()

        def step(b, carry, i=i):
            at = pl.ds(pl.multiple_of(b * 8, 8), 8)
            here = pl.ds(pl.multiple_of(i * block + b * 8, 8), 8)
            got = real_transform([dens[here, n * INNER : (n + 1) * INNER] - offset for n in range(RADIX)])
            pieces[0, at, :INNER] = got[0][0]
            pieces[0, at, INNER:] = got[8][0]
            for s in range(1, 8):
                pieces[s, at, :INNER] = got[s][0]
                pieces[s, at, INNER:] = got[s][1]
            return carry

        lax.fori_loop(0, block // 8, step, 0)

        def part(index, carry, i=i):
            shift, chunk = index // chunks, lax.rem(index, chunks)
            t = lax.rem(me + shift, pencils) * chunks + chunk
            total = None
            for odd in range(2):
                high, low = split_value(pieces[slot_at(2 * t + odd)])
                table_high = row_high[t, 256 * odd : 256 * odd + 256]
                table_low = row_low[t, 256 * odd : 256 * odd + 256]
                term = dot(high, table_high) + dot(low, table_high) + dot(high, table_low)
                total = term if total is None else total + term
            for c in range(2):
                sending[chunk, shift, i, c] = total[:, c * 128 : (c + 1) * 128]
            return carry

        lax.fori_loop(0, pencils * chunks, part, 0)
        for shift in SHIFTS:
            a_copy(0, shift, i).start()

    def start_a(chunk):
        for i in range(BLOCKS):
            for shift in SHIFTS:
                a_copy(chunk, shift, i).start()

    arrivals = [(i, shift) for i in range(BLOCKS) for shift in SHIFTS]

    def wait_a(chunk, which):
        for i, shift in which:
            a_copy(chunk, shift, i).wait_recv()

    for copy in late_loads:
        copy.wait()

    for u in range(share):
        rest(u).wait_recv()

        @pl.when(partner != me)
        def _(u=u):
            zero(u).wait_recv()
            zero(u).wait_send()

        @pl.when(partner == me)
        def _(u=u):
            stay(u).wait()

    own = gathered.at[sharer]
    far = (1 - grp) * 2 + mem
    across = remote(own, own, g_sem.at[0], g_sem.at[1], grp=1 - grp)
    across.start()
    beside = remote(own, own, g_sem.at[2], g_sem.at[3], mem=1 - mem)
    beside.start()
    wait_a(0, arrivals[:AHEAD])
    start_a(1)
    across.wait_recv()
    passed = remote(gathered.at[far], gathered.at[far], g_sem.at[4], g_sem.at[5], mem=1 - mem)
    passed.start()
    beside.wait_recv()
    passed.wait_recv()

    from_lane = lax.broadcasted_iota(jnp.int32, (2 * INNER, lanes), 0)
    to_lane = lax.broadcasted_iota(jnp.int32, (2 * INNER, lanes), 1)
    pick = jnp.where(from_lane == to_lane + jnp.where(to_lane < HALF, 0, HALF), 0.5, 0.0).astype(bf16)
    from_lane, to_lane = from_lane[:INNER], to_lane[:INNER]
    pick_edge = jnp.where((from_lane == HALF) & (to_lane == 0), 0.5, 0.0).astype(bf16)
    mask = (to_lane == 0) & (me == 0)

    def turned(r):
        c, s = turns[r, :, 0:1], turns[r, :, 1:2]
        pc, ps = phase_ref[me, r, 0], phase_ref[me, r, 1]
        return c * pc - s * ps, s * pc + c * ps

    def wave(r):
        re, im = spectra[r, :INNER], spectra[r, INNER:]
        c, s = turned(r)
        high, low = split_value(jnp.concatenate([re * c + im * s, im * c - re * s], axis=0))
        return dot(tables[0], high) + dot(tables[0], low) + dot(tables[1], high)

    def finish(chunk, r, got):
        re, im = got[:INNER], got[INNER:]
        rows = pl.ds(pl.multiple_of(r * INNER, INNER), INNER)
        holder, u = r // share, lax.rem(r, share)
        parts = []
        for c in range(2):
            other = [gathered[holder, u, 2 * chunk + j, :, c * HALF : (c + 1) * HALF] for j in range(2)]
            other = jnp.concatenate(other, axis=1)
            mine = dot(kern[local, c, rows, 2 * chunk * INNER : 2 * (chunk + 1) * INNER], pick)
            parts.append(mine + 0.5 * other if c == 0 else mine - 0.5 * other)
        kr, ki = parts
        if chunk == 0:
            other = lax.rem(RADIX - r, RADIX)
            other_rows = pl.ds(pl.multiple_of(other * INNER, INNER), INNER)
            swap = swapped(r == 0, (INNER, INNER), 0)
            edges = []
            for c in range(2):
                mine = dot(kern[local, c, rows, :INNER], pick_edge)
                flipped = dot(swap, kern[local, c, other_rows, :INNER]).astype(bf16)
                flipped = dot(flipped, pick_edge)
                edges.append(mine + flipped if c == 0 else mine - flipped)
            high, low = split_value(waves[other])
            ore = dot(swap, high[:INNER]) + dot(swap, low[:INNER])
            oim = -(dot(swap, high[INNER:]) + dot(swap, low[INNER:]))
            hr = jnp.where(mask, 0.5 * (kr - edges[0]), 0.0)
            hi = jnp.where(mask, 0.5 * (ki - edges[1]), 0.0)
            kr, ki = kr - hr, ki - hi
            sr = re * kr - im * ki + (ore * hr - oim * hi)
            si = re * ki + im * kr + (ore * hi + oim * hr)
        else:
            sr, si = re * kr - im * ki, re * ki + im * kr
        high, low = split_value(jnp.concatenate([sr, si], axis=0))
        got = dot(tables[2], high) + dot(tables[2], low) + dot(tables[3], high)
        re, im = got[:INNER], got[INNER:]
        c, s = turned(r)
        spectra[r, :INNER] = re * c - im * s
        spectra[r, INNER:] = im * c + re * s

    def columns(chunk):
        def forward(b, carry):
            values = []
            for n in range(RADIX):
                j, begin = divmod(n * INNER, part_rows)
                i, begin = divmod(begin, block)
                at = pl.ds(pl.multiple_of(begin + b * 8, 8), 8)
                ref = sending.at[chunk, 0, i] if j == 0 else landing.at[chunk, pencils - j - 1, i]
                values.append((ref[0, at, :], ref[1, at, :]))
            at = pl.ds(pl.multiple_of(b * 8, 8), 8)
            also = pl.ds(pl.multiple_of(INNER + b * 8, 8), 8)
            for r, (re, im) in enumerate(transform(values, -1)):
                spectra[r, at, :] = re
                spectra[r, also, :] = im
            return carry

        lax.fori_loop(0, INNER // 8, forward, 0)

        def early(i, carry):
            for u in range(UNROLL):
                waves[i * UNROLL + u] = wave(i * UNROLL + u)
            return carry

        def late(i, carry):
            for u in range(UNROLL):
                r = i * UNROLL + u
                finish(chunk, r, waves[r] if chunk == 0 else wave(r))
            return carry

        if chunk == 0:
            lax.fori_loop(0, RADIX // UNROLL, early, 0)
        lax.fori_loop(0, RADIX // UNROLL, late, 0)

        def backward(b, carry):
            at = pl.ds(pl.multiple_of(b * 8, 8), 8)
            also = pl.ds(pl.multiple_of(INNER + b * 8, 8), 8)
            values = [(spectra[r, at, :], spectra[r, also, :]) for r in range(RADIX)]
            for n, (re, im) in enumerate(transform(values, 1)):
                shift_depth, begin = divmod(n * INNER, out_rows)
                shift, depth = divmod(shift_depth, depths)
                put = pl.ds(pl.multiple_of(begin + b * 8, 8), 8)
                slot = jnp.where(deep == depth, 0, 1)
                keep[chunk, slot, shift, 0, put, :] = re
                keep[chunk, slot, shift, 1, put, :] = im
            return carry

        lax.fori_loop(0, INNER // 8, backward, 0)

    out_block = out_rows // PARTS

    def x_copy(chunk, j, i):
        at = pl.ds(i * out_block, out_block)
        return remote(keep.at[chunk, 1, j, :, at], other_keep.at[chunk, j, :, at],
                      x_sem.at[0, chunk, j, i], x_sem.at[1, chunk, j, i], depth=1 - deep)

    def c_copy(chunk, j, i):
        at = pl.ds(i * out_block, out_block)
        return remote(keep.at[chunk, 0, j, :, at], fields.at[chunk, j - 1, :, at],
                      c_sem.at[0, chunk, j - 1, i], c_sem.at[1, chunk, j - 1, i], pencil=toward(j))

    def summed(chunk, j, i):
        x_copy(chunk, j, i).wait_recv()
        at = pl.ds(i * out_block, out_block)
        keep[chunk, 0, j, :, at] += other_keep[chunk, j, :, at]

    def gather_field(chunk, shift, i):
        t = lax.rem(me + pencils - shift, pencils) * chunks + chunk
        at = pl.ds(i * out_block, out_block)
        ref = keep.at[chunk, 0, 0] if shift == 0 else fields.at[chunk, shift - 1]
        high, low = split_value(jnp.concatenate([ref[0, at], ref[1, at]], axis=1))
        for odd in range(2):
            r = 2 * t + odd
            half[slot_at(r), at] += dot(high, back_high[r]) + dot(low, back_high[r]) + dot(high, back_low[r])

    half[...] = jnp.zeros_like(half)
    wait_a(0, arrivals[AHEAD:])
    columns(0)
    pairs = [(i, j) for i in range(PARTS) for j in ORDER]
    for i, j in pairs:
        x_copy(0, j, i).start()
    for i, j in pairs:
        summed(0, j, i)
    wait_a(1, arrivals[:BEFORE])
    for i, j in pairs:
        if j:
            c_copy(0, j, i).start()
    wait_a(1, arrivals[BEFORE:])
    columns(1)
    for i, j in pairs:
        x_copy(1, j, i).start()
    for i in range(PARTS):
        gather_field(0, 0, i)
    for i, j in pairs:
        summed(1, j, i)
        if j:
            c_copy(1, j, i).start()
    for i in range(PARTS):
        gather_field(1, 0, i)
    for i, j in pairs:
        if j:
            c_copy(0, j, i).wait_recv()
            gather_field(0, j, i)
    leaving = []
    for i in range(PARTS):
        for j in ORDER:
            if j:
                c_copy(1, j, i).wait_recv()
                gather_field(1, j, i)
        at = pl.ds(i * out_block, out_block)
        leaving.append(pltpu.make_async_copy(half.at[:, at], out_ref.at[:, at], local_sem.at[i]))
        leaving[-1].start()
    for copy in leaving:
        copy.wait()

    for u in range(share):
        rest(u).wait_send()
    across.wait_send()
    beside.wait_send()
    passed.wait_send()
    for chunk in range(chunks):
        for shift in SHIFTS:
            for i in range(BLOCKS):
                a_copy(chunk, shift, i).wait_send()
        for j in ORDER:
            for i in range(PARTS):
                x_copy(chunk, j, i).wait_send()
                if j:
                    c_copy(chunk, j, i).wait_send()


def last_kernel(in_ref, out_ref, half, done, sem):
    block = half.shape[1] // LAST

    def copies(i):
        at = pl.ds(i * block, block)
        return (pltpu.make_async_copy(in_ref.at[:, at], half.at[:, at], sem.at[0, i]),
                pltpu.make_async_copy(done.at[at], out_ref.at[0, at], sem.at[1, i]))

    def last(b, carry):
        at = pl.ds(pl.multiple_of(b * 8, 8), 8)
        values = [(half[0, at, :INNER], None)]
        for s in range(1, 8):
            values.append((half[s, at, :INNER], half[s, at, INNER:]))
        values.append((half[0, at, INNER:], None))
        for n, value in enumerate(real_inverse(values)):
            done[at, n * INNER : (n + 1) * INNER] = value
        return carry

    for i in range(LAST):
        copies(i)[0].start()
    for i in range(LAST):
        copies(i)[0].wait()
        lax.fori_loop(i * block // 8, (i + 1) * block // 8, last, 0)
        copies(i)[1].start()
    for i in range(LAST):
        copies(i)[1].wait()


LAST = 4
SHIFTS = (2, 1, 3)
ORDER = (2, 1, 3, 0)
UNROLL = 4
AHEAD = 9
BEFORE = 12
PARTS = 1


def params(**more):
    return pltpu.CompilerParams(vmem_limit_bytes=48 * 1024 * 1024, **more)


def wide_body(density, background, member_ids, layer_kernel, kernel_spectra):
    pencils = lax.axis_size("pencil")
    depths = lax.axis_size("depth")
    sharers = lax.axis_size("grp") * lax.axis_size("mem")
    pencil = lax.axis_index("pencil")
    per = RADIX // pencils
    width = min(per, 2)
    chunks = per // width
    lanes = width * HALF
    part_rows = density.shape[2]
    out_rows = part_rows // depths
    vmem = pl.BlockSpec(memory_space=pltpu.VMEM)
    smem = pl.BlockSpec(memory_space=pltpu.SMEM)

    kern_count = kernel_spectra.shape[0]
    local = layer_kernel[0] - lax.axis_index("depth") * kern_count
    share = RADIX // sharers
    first = lax.axis_index(("grp", "mem")) * share
    groups = [1] if per == 1 else [1, per - 1]
    moved = pl.pallas_call(
        functools.partial(mirror_kernel, share),
        grid_spec=pltpu.PrefetchScalarGridSpec(
            num_scalar_prefetch=1,
            grid=(1,),
            in_specs=[
                pl.BlockSpec(
                    (None, 2, INNER, per * INNER),
                    lambda i, w, u=u: (w[0], 0, lax.rem(RADIX - w[1] - u, RADIX), 0),
                )
                for u in range(share)
            ],
            out_specs=[pl.BlockSpec((g, share, INNER, INNER), lambda i, w: (0, 0, 0, 0)) for g in groups],
        ),
        out_shape=[jax.ShapeDtypeStruct((g, share, INNER, INNER), f32) for g in groups],
        compiler_params=params(),
        cost_estimate=pl.CostEstimate(flops=1 << 20, bytes_accessed=2 << 20, transcendentals=0),
    )(jnp.stack([local, first, pencil]), *[kernel_spectra] * share)
    mirrored = lax.ppermute(moved[0], "pencil", [(p, (pencils - p) % pencils) for p in range(pencils)])
    if per > 1:
        rest = lax.ppermute(moved[1], "pencil", [(p, pencils - 1 - p) for p in range(pencils)])

    offset = lax.dynamic_index_in_dim(background[:, 0], member_ids[0], 0, keepdims=True)
    row_high, row_low = halves(row_tables())
    block = min(part_rows, 128)
    sent = pl.pallas_call(
        functools.partial(rows_kernel, pencils, width),
        grid=(part_rows // block,),
        in_specs=[
            smem,
            pl.BlockSpec((None, None, block, LENGTH), lambda i: (0, 0, i, 0)),
            pl.BlockSpec((8, 512, 256), lambda i: (0, 0, 0)),
            pl.BlockSpec((8, 512, 256), lambda i: (0, 0, 0)),
        ],
        out_specs=[pl.BlockSpec((pencils, 2, block, lanes), lambda i: (0, 0, i, 0))] * chunks,
        out_shape=[jax.ShapeDtypeStruct((pencils, 2, part_rows, lanes), f32)] * chunks,
        scratch_shapes=[pltpu.VMEM((8, block, 256), f32)],
        compiler_params=params(),
        cost_estimate=pl.CostEstimate(flops=6 * part_rows * 2 * LENGTH * 512, bytes_accessed=12 << 20, transcendentals=0),
    )(offset, density, row_high, row_low)
    arrived = [lax.all_to_all(part, "pencil", 0, 0, tiled=True) for part in sent]

    sign = jnp.array([0.5, -0.5], f32)
    edge = lax.dynamic_slice(kernel_spectra, (local, 0, 0, HALF), (1, 2, LENGTH, 1))
    edge = edge.reshape(2, RADIX, INNER).astype(f32)
    flipped = jnp.concatenate([edge[:, :1], edge[:, :0:-1]], axis=1)[..., ::-1]
    flipped = jnp.concatenate([jnp.roll(flipped[:, :1], 1, axis=2), flipped[:, 1:]], axis=1)
    edge = 0.5 * edge + sign.reshape(2, 1, 1) * flipped
    edge = jnp.where(lax.broadcasted_iota(jnp.int32, (lanes,), 0) == 0, edge[..., None], 0.0)

    if per > 1:
        mirrored = jnp.concatenate([mirrored, rest], axis=0)
    mirrored, edge, _ = lax.optimization_barrier((mirrored, edge, sent[0]))
    mirrored = lax.all_gather(mirrored, ("grp", "mem"), axis=0)

    column, column_turns = column_tables()
    column_turns = jnp.asarray(column_turns)
    tables = jnp.stack(halves(column) + halves(column.T))
    two = depths == 2
    mine = lax.axis_index("depth") if two else jnp.int32(0)
    where = jnp.stack([mine, local, pencil])
    fields = []
    before = None
    for k in range(chunks):
        special = k == 0
        steps = sharers

        def early(i, special=special):
            return jnp.minimum(i, steps - 1) if special else i

        def late(i, special=special):
            return jnp.maximum(i - steps, 0) if special else i

        here = arrived[k]
        if before is not None:
            here, before = lax.optimization_barrier((here, before))
            fields.append(lax.all_to_all(before, "pencil", 0, 0, tiled=True))
        edge_block = (2, share, INNER, lanes) if special else (2, 1, 8, lanes)
        out = pl.pallas_call(
            functools.partial(columns_kernel, special),
            grid_spec=pltpu.PrefetchScalarGridSpec(
                num_scalar_prefetch=1,
                grid=(2 * steps if special else steps,),
                in_specs=[
                    pl.BlockSpec((pencils, 2, part_rows, lanes), lambda i, w: (0, 0, 0, 0)),
                    pl.BlockSpec(
                        (None, 2, share * INNER, width * INNER), lambda i, w, k=k, late=late: (w[1], 0, late(i), k)
                    ),
                    pl.BlockSpec(
                        (None, width, share, INNER, INNER), lambda i, w, k=k, late=late: (late(i), k, 0, 0, 0)
                    ),
                    pl.BlockSpec(
                        edge_block,
                        (lambda i, w, late=late: (0, late(i), 0, 0)) if special else (lambda i, w: (0, 0, 0, 0)),
                    ),
                ]
                + [pl.BlockSpec((share, INNER, INNER), lambda i, w, early=early: (early(i), 0, 0))]
                + [pl.BlockSpec((share, INNER, INNER), lambda i, w, late=late: (late(i), 0, 0))]
                + [pl.BlockSpec((4, 256, 256), lambda i, w: (0, 0, 0))],
                out_specs=pl.BlockSpec((depths, pencils, 2, out_rows, lanes), lambda i, w: (0, 0, 0, 0, 0)),
                scratch_shapes=[
                    pltpu.VMEM((RADIX, 256, lanes), f32),
                    pltpu.VMEM((RADIX if special else 1, 256, lanes), f32),
                ],
            ),
            out_shape=jax.ShapeDtypeStruct((depths, pencils, 2, out_rows, lanes), f32),
            compiler_params=params(),
            cost_estimate=pl.CostEstimate(
                flops=12 * RADIX * 256 * 256 * lanes, bytes_accessed=16 << 20, transcendentals=0
            ),
        )(where, here, kernel_spectra, mirrored, edge, column_turns, column_turns, tables)
        if two:
            before = out[0] + lax.ppermute(out[1], "depth", [(0, 1), (1, 0)])
        else:
            before = lax.psum_scatter(out, "depth", scatter_dimension=0, tiled=False)
    fields.append(lax.all_to_all(before, "pencil", 0, 0, tiled=True))

    back_high, back_low = halves(inverse_row_tables())
    return pl.pallas_call(
        functools.partial(fields_kernel, pencils, width, [1] * chunks),
        in_specs=[vmem] * (len(fields) + 2),
        out_specs=vmem,
        out_shape=jax.ShapeDtypeStruct((1, out_rows, LENGTH), f32),
        scratch_shapes=[pltpu.VMEM((8, out_rows, 256), f32)],
        compiler_params=params(),
        cost_estimate=pl.CostEstimate(flops=6 * out_rows * 2 * LENGTH * 512, bytes_accessed=8 << 20, transcendentals=0),
    )(*fields, back_high, back_low)


def fused_body(density, background, member_ids, layer_kernel, kernel_spectra):
    pencils = lax.axis_size("pencil")
    depths = lax.axis_size("depth")
    sharers = lax.axis_size("grp") * lax.axis_size("mem")
    per = RADIX // pencils
    chunks = per // 2
    lanes = 2 * HALF
    part_rows = density.shape[2]
    out_rows = part_rows // depths
    share = RADIX // sharers
    smem = pl.BlockSpec(memory_space=pltpu.SMEM)
    anywhere = pl.BlockSpec(memory_space=pl.ANY)

    angles = 2 * np.pi * np.arange(pencils)[:, None] * np.arange(RADIX)[None, :] / pencils
    phases = jnp.asarray(np.stack([np.cos(angles), np.sin(angles)], axis=-1).round(15), f32)
    row_high, row_low = halves(row_tables())
    where = [0 if r == 8 else min(r, RADIX - r) for r in range(RADIX)], [int(r >= 8) for r in range(RADIX)]
    back_high, back_low = halves(inverse_row_tables().reshape(8, 2, 256, 256)[where])
    column, turns = column_tables()
    tables = jnp.stack(halves(column) + halves(column.T))
    turns = jnp.asarray(turns)
    dma = pltpu.SemaphoreType.DMA
    half = pl.pallas_call(
        functools.partial(fused_kernel, pencils, depths),
        in_specs=[smem] * 4 + [anywhere] * 8,
        out_specs=anywhere,
        out_shape=jax.ShapeDtypeStruct((8, out_rows, 256), f32),
        scratch_shapes=[
            pltpu.VMEM((part_rows, LENGTH), f32),
            [pltpu.VMEM((kernel_spectra.shape[0], 2, INNER, per * INNER), bf16)] * share,
            pltpu.VMEM(kernel_spectra.shape, bf16),
            pltpu.VMEM(row_high.shape, bf16),
            pltpu.VMEM(row_low.shape, bf16),
            pltpu.VMEM(back_high.shape, bf16),
            pltpu.VMEM(back_low.shape, bf16),
            pltpu.VMEM(tables.shape, bf16),
            pltpu.VMEM(turns.shape, f32),
            pltpu.VMEM((8, part_rows // BLOCKS, 256), f32),
            pltpu.VMEM((chunks, pencils, BLOCKS, 2, part_rows // BLOCKS, lanes), f32),
            pltpu.VMEM((chunks, pencils - 1, BLOCKS, 2, part_rows // BLOCKS, lanes), f32),
            pltpu.VMEM((share, per, INNER, INNER), f32),
            pltpu.VMEM((sharers, share, per, INNER, INNER), f32),
            pltpu.VMEM((RADIX, 256, lanes), f32),
            pltpu.VMEM((RADIX, 256, lanes), f32),
            pltpu.VMEM((chunks, 2, pencils, 2, out_rows, lanes), f32),
            pltpu.VMEM((chunks, pencils, 2, out_rows, lanes), f32),
            pltpu.VMEM((chunks, pencils - 1, 2, out_rows, lanes), f32),
            pltpu.VMEM((8, out_rows, 256), f32),
            dma((share + BLOCKS + 7,)),
            dma((5, share)),
            dma((6,)),
            dma((chunks, pencils - 1, BLOCKS)),
            dma((chunks, pencils - 1, BLOCKS)),
            dma((2, chunks, pencils, PARTS)),
            dma((2, chunks, pencils - 1, PARTS)),
        ],
        compiler_params=pltpu.CompilerParams(
            vmem_limit_bytes=60 * 1024 * 1024, collective_id=0, has_side_effects=True
        ),
    )(background.reshape(-1), member_ids, layer_kernel, phases, density, kernel_spectra, row_high, row_low, back_high, back_low, tables, turns)
    return pl.pallas_call(
        last_kernel,
        in_specs=[anywhere],
        out_specs=anywhere,
        out_shape=jax.ShapeDtypeStruct((1, out_rows, LENGTH), f32),
        scratch_shapes=[
            pltpu.VMEM((8, out_rows, 256), f32),
            pltpu.VMEM((out_rows, LENGTH), f32),
            dma((2, LAST)),
        ],
        compiler_params=pltpu.CompilerParams(vmem_limit_bytes=60 * 1024 * 1024),
    )(half)


def body(density, background, member_ids, layer_kernel, kernel_spectra):
    sizes = tuple(lax.axis_size(name) for name in ("grp", "pencil", "depth", "mem"))
    plan = fused_body if sizes == (2, 4, 2, 2) else wide_body
    return plan(density, background, member_ids, layer_kernel, kernel_spectra)


def solution(mesh):
    placed = (
        P(("grp", "mem"), "depth", "pencil", None),
        P(None, "depth"),
        P(("grp", "mem")),
        P("depth"),
        P("depth", None, None, "pencil"),
    )
    return jax.shard_map(
        body,
        mesh=mesh,
        in_specs=placed,
        out_specs=P(("grp", "mem"), ("pencil", "depth"), None),
        check_vma=False,
    )
```

```python
import functools
import math

import jax
import jax.numpy as jnp
import numpy as np
from jax import lax
from jax.experimental import pallas as pl
from jax.experimental.pallas import tpu as pltpu
from jax.sharding import PartitionSpec as P

RADIX = 16
INNER = 128
HALF = 64
LENGTH = RADIX * INNER
f32 = jnp.float32
bf16 = jnp.bfloat16


def halves(table):
    table = np.asarray(table, np.float32)
    high = table.astype(bf16)
    low = (table - high.astype(np.float32)).astype(bf16)
    return jnp.asarray(high), jnp.asarray(low)


def residue_rows(r):
    m = np.arange(INNER)[:, None]
    q = np.arange(HALF)[None, :]
    turn = np.exp(-2j * np.pi * (((RADIX * q + r) * m) % LENGTH) / LENGTH)
    re, im = turn.real.copy(), turn.imag.copy()
    if r == 0:
        im[:, 0] = (-1.0) ** m[:, 0]
    out = np.zeros((2 * INNER, 2 * HALF))
    if r == 0:
        out[:INNER, :HALF], out[:INNER, HALF:] = re, im
    elif r == 8:
        out[INNER:, :HALF], out[INNER:, HALF:] = re, im
    else:
        sign = 1.0 if r < 8 else -1.0
        out[:INNER, :HALF], out[:INNER, HALF:] = re, im
        out[INNER:, :HALF], out[INNER:, HALF:] = -sign * im, sign * re
    return out


def slot_of(r):
    return 0 if r in (0, 8) else min(r, RADIX - r)


def row_tables():
    tables = np.zeros((8, 512, 256))
    for t in range(8):
        for odd in range(2):
            block = residue_rows(2 * t + odd)
            rows = slice(256 * odd, 256 * odd + 256)
            tables[t, rows, HALF * odd : HALF * odd + HALF] = block[:, :HALF]
            tables[t, rows, 128 + HALF * odd : 128 + HALF * odd + HALF] = block[:, HALF:]
    return tables


def inverse_row_tables():
    tables = np.zeros((8, 512, 256))
    scale = 1.0 / (LENGTH * LENGTH)
    for s in range(8):
        for place, r in enumerate((s, 8 if s == 0 else RADIX - s)):
            block = residue_rows(r).T.copy() * scale
            weight = np.full((2 * HALF, 1), 2.0 if r in (0, 8) else 1.0)
            if r == 0:
                weight[0] = weight[HALF] = 1.0
            block *= weight
            odd = r % 2
            tables[s, 256 * place + HALF * odd : 256 * place + HALF * odd + HALF] += block[:HALF]
            tables[s, 256 * place + 128 + HALF * odd : 256 * place + 128 + HALF * odd + HALF] += block[HALF:]
    return tables


def column_tables():
    q = np.arange(INNER)[:, None]
    m = np.arange(INNER)[None, :]
    turn = np.exp(-2j * np.pi * ((q * m) % INNER) / INNER)
    table = np.block([[turn.real, -turn.imag], [turn.imag, turn.real]])
    angles = 2 * np.pi * np.arange(RADIX)[:, None] * np.arange(INNER)[None, :] / LENGTH
    turns = np.zeros((RADIX, INNER, INNER), np.float32)
    turns[..., 0] = np.cos(angles)
    turns[..., 1] = np.sin(angles)
    return table, turns


def split_value(value):
    high = value.astype(bf16)
    return high, (value - high.astype(f32)).astype(bf16)


def dot(a, b):
    return jnp.dot(a, b, preferred_element_type=f32)


def rotate(value, count, length, sign):
    re, im = value
    count %= length
    if count == 0:
        return value
    if 4 * count == length:
        return (im, -re) if sign < 0 else (-im, re)
    c = math.cos(2 * math.pi * count / length)
    s = sign * math.sin(2 * math.pi * count / length)
    if 8 * count == length:
        return ((re + im) * c, (im - re) * c) if sign < 0 else ((re - im) * c, (im + re) * c)
    return (re * c - im * s, re * s + im * c)


def plus(a, b):
    return (a[0] + b[0], a[1] + b[1])


def minus(a, b):
    return (a[0] - b[0], a[1] - b[1])


def transform(values, sign):
    length = len(values)
    if length == 1:
        return values
    even, odd = transform(values[0::2], sign), transform(values[1::2], sign)
    turned = [rotate(odd[k], k, length, sign) for k in range(length // 2)]
    return [plus(even[k], turned[k]) for k in range(length // 2)] + [
        minus(even[k], turned[k]) for k in range(length // 2)
    ]


def real_transform(values):
    length = len(values)
    if length == 2:
        return [(values[0] + values[1], None), (values[0] - values[1], None)]
    even, odd = real_transform(values[0::2]), real_transform(values[1::2])
    out = [None] * (length // 2 + 1)
    out[0] = (even[0][0] + odd[0][0], None)
    out[length // 2] = (even[0][0] - odd[0][0], None)
    quarter = length // 4
    for k in range(1, quarter):
        turned = rotate(odd[k], k, length, -1)
        out[k] = plus(even[k], turned)
        low = minus(even[k], turned)
        out[length // 2 - k] = (low[0], -low[1])
    out[quarter] = (even[quarter][0], -odd[quarter][0])
    return out


def real_inverse(values):
    half = len(values) - 1
    length = 2 * half
    if length == 2:
        return [values[0][0] + values[1][0], values[0][0] - values[1][0]]
    even, odd = [], []
    for k in range(half // 2 + 1):
        if k == 0:
            even.append((values[0][0] + values[half][0], None))
            odd.append((values[0][0] - values[half][0], None))
        elif k == half // 2:
            even.append((2.0 * values[k][0], None))
            odd.append((-2.0 * values[k][1], None))
        else:
            other = values[half - k]
            even.append((values[k][0] + other[0], values[k][1] - other[1]))
            odd.append(rotate((values[k][0] - other[0], values[k][1] + other[1]), k, length, 1))
    first, second = real_inverse(even), real_inverse(odd)
    return [x for pair in zip(first, second) for x in pair]


def rows_kernel(pencils, width, offset_ref, in_ref, high_ref, low_ref, *rest):
    outs, pieces = rest[:-1], rest[-1]
    rows = in_ref.shape[0]
    per = RADIX // pencils
    offset = offset_ref[0]

    def step(b, carry):
        at = pl.ds(pl.multiple_of(b * 8, 8), 8)
        values = [in_ref[at, n * INNER : (n + 1) * INNER] - offset for n in range(RADIX)]
        got = real_transform(values)
        pieces[0, at, :INNER] = got[0][0]
        pieces[0, at, INNER:] = got[8][0]
        for s in range(1, 8):
            pieces[s, at, :INNER] = got[s][0]
            pieces[s, at, INNER:] = got[s][1]
        return carry

    lax.fori_loop(0, rows // 8, step, 0)
    for t in range(8):
        total = None
        for odd in range(2):
            high, low = split_value(pieces[slot_of(2 * t + odd)])
            table_high = high_ref[t, 256 * odd : 256 * odd + 256]
            table_low = low_ref[t, 256 * odd : 256 * odd + 256]
            part = dot(high, table_high) + dot(low, table_high) + dot(high, table_low)
            total = part if total is None else total + part
        if width == 2:
            pencil, place = divmod(2 * t, per)
            for c in range(2):
                outs[place // 2][pencil, c] = total[:, c * 128 : (c + 1) * 128]
        else:
            for odd in range(2):
                pencil, place = divmod(2 * t + odd, per)
                for c in range(2):
                    begin = c * 128 + odd * HALF
                    outs[place][pencil, c] = total[:, begin : begin + HALF]


def swapped(zero, shape, axis):
    total = lax.broadcasted_iota(jnp.int32, shape, 0) + lax.broadcasted_iota(jnp.int32, shape, 1)
    wanted = jnp.where(zero, INNER, INNER - 1)
    also = jnp.where(zero, 0, INNER - 1)
    return jnp.where((total == wanted) | (total == also), 1.0, 0.0).astype(bf16)


def mirror_kernel(share, where_ref, *refs):
    ins, zero_ref, rest_refs = refs[:share], refs[share], refs[share + 1 :]
    per = ins[0].shape[2] // INNER
    plain = swapped(where_ref[1] < 0, (INNER, HALF), 1)
    edge = swapped(where_ref[2] == 0, (INNER, HALF), 1)
    for u in range(share):
        swap = swapped(where_ref[1] + u == 0, (INNER, INNER), 0)
        rows = [dot(swap, ins[u][c]).astype(bf16) for c in range(2)]
        for j in range(per):
            turn = edge if j == 0 else plain
            turned = [dot(rows[c][:, j * INNER : (j + 1) * INNER], turn) for c in range(2)]
            value = jnp.concatenate(turned, axis=1)
            if j == 0:
                zero_ref[0, u] = value
            else:
                rest_refs[0][per - 1 - j, u] = value


def columns_kernel(special, where_ref, in_ref, kern_ref, mirror_ref, edge_ref,
                   turns_ref, late_ref, table_ref, out_ref, pieces, waves):
    part_rows = in_ref.shape[2]
    depths, pencils, _, out_rows, lanes = out_ref.shape
    share = mirror_ref.shape[1]
    steps = RADIX // share
    mine = where_ref[0]
    now = pl.program_id(0)
    from_lane = lax.broadcasted_iota(jnp.int32, (kern_ref.shape[2], lanes), 0)
    to_lane = lax.broadcasted_iota(jnp.int32, (kern_ref.shape[2], lanes), 1)
    wanted = to_lane + jnp.where(to_lane < HALF, 0, HALF)
    pick = jnp.where(from_lane == wanted, 0.5, 0.0).astype(bf16)
    zero_swap = swapped(mine >= 0, (INNER, INNER), 0)
    plain_swap = swapped(mine < 0, (INNER, INNER), 0)

    def forward(b, carry):
        values = []
        for n in range(RADIX):
            source, begin = divmod(n * INNER, part_rows)
            at = pl.ds(pl.multiple_of(begin + b * 8, 8), 8)
            values.append((in_ref[source, 0, at, :], in_ref[source, 1, at, :]))
        at = pl.ds(pl.multiple_of(b * 8, 8), 8)
        also = pl.ds(pl.multiple_of(INNER + b * 8, 8), 8)
        for r, (re, im) in enumerate(transform(values, -1)):
            pieces[r, at, :] = re
            pieces[r, also, :] = im
        return carry

    @pl.when(now == 0)
    def _():
        lax.fori_loop(0, INNER // 8, forward, 0)

    def wave(r, u):
        re, im = pieces[r, :INNER], pieces[r, INNER:]
        c, s = turns_ref[u, :, 0:1], turns_ref[u, :, 1:2]
        high, low = split_value(jnp.concatenate([re * c + im * s, im * c - re * s], axis=0))
        return dot(table_ref[0], high) + dot(table_ref[0], low) + dot(table_ref[1], high)

    def finish(r, u, got):
        re, im = got[:INNER], got[INNER:]
        tiles = [mirror_ref[j, u] for j in range(mirror_ref.shape[0])]
        rows = slice(u * INNER, (u + 1) * INNER)
        parts = []
        for c in range(2):
            other = [tile[:, c * HALF : (c + 1) * HALF] for tile in tiles]
            other = jnp.concatenate(other, axis=1) if len(other) > 1 else other[0]
            own = dot(kern_ref[c, rows, :], pick)
            parts.append(own + 0.5 * other if c == 0 else own - 0.5 * other)
        kr, ki = parts
        if special:
            other = lax.rem(RADIX - r, RADIX)
            high, low = split_value(waves[other])
            swap = jnp.where(r == 0, zero_swap.astype(f32), plain_swap.astype(f32)).astype(bf16) if u == 0 else plain_swap
            ore = dot(swap, high[:INNER]) + dot(swap, low[:INNER])
            oim = -(dot(swap, high[INNER:]) + dot(swap, low[INNER:]))
            mask = (lax.broadcasted_iota(jnp.int32, (INNER, lanes), 1) == 0) & (where_ref[2] == 0)
            hr = jnp.where(mask, 0.5 * (kr - edge_ref[0, u]), 0.0)
            hi = jnp.where(mask, 0.5 * (ki - edge_ref[1, u]), 0.0)
            kr, ki = kr - hr, ki - hi
            sr = re * kr - im * ki + (ore * hr - oim * hi)
            si = re * ki + im * kr + (ore * hi + oim * hr)
        else:
            sr, si = re * kr - im * ki, re * ki + im * kr
        spectrum = jnp.concatenate([sr, si], axis=0)
        high, low = split_value(spectrum)
        got = dot(table_ref[2], high) + dot(table_ref[2], low) + dot(table_ref[3], high)
        re, im = got[:INNER], got[INNER:]
        c, s = late_ref[u, :, 0:1], late_ref[u, :, 1:2]
        pieces[r, :INNER] = re * c - im * s
        pieces[r, INNER:] = im * c + re * s

    if special:
        @pl.when(now < steps)
        def _():
            for u in range(share):
                waves[now * share + u] = wave(now * share + u, u)

        @pl.when(now >= steps)
        def _():
            for u in range(share):
                r = (now - steps) * share + u
                finish(r, u, waves[r])
    else:
        for u in range(share):
            r = now * share + u
            finish(r, u, wave(r, u))

    slots = [lax.rem(d - mine + depths, depths) for d in range(depths)]

    def backward(b, carry):
        at = pl.ds(pl.multiple_of(b * 8, 8), 8)
        also = pl.ds(pl.multiple_of(INNER + b * 8, 8), 8)
        values = [(pieces[r, at, :], pieces[r, also, :]) for r in range(RADIX)]
        for n, (re, im) in enumerate(transform(values, 1)):
            if out_rows % INNER == 0:
                part, begin = divmod(n * INNER, out_rows)
                pencil, depth = divmod(part, depths)
                depth = slots[depth]
                put = pl.ds(pl.multiple_of(begin + b * 8, 8), 8)
            else:
                x = n * INNER + b * 8
                pencil = x // (out_rows * depths)
                depth = lax.rem(x // out_rows - mine + depths, depths)
                put = pl.ds(pl.multiple_of(lax.rem(x, out_rows), 8), 8)
            out_ref[depth, pencil, 0, put, :] = re
            out_ref[depth, pencil, 1, put, :] = im
        return carry

    @pl.when(now == pl.num_programs(0) - 1)
    def _():
        lax.fori_loop(0, INNER // 8, backward, 0)


def fields_kernel(pencils, width, counts, *refs):
    ins, at = [], 0
    for count in counts:
        ins.append(refs[at : at + count])
        at += count
    high_ref, low_ref, out_ref, pieces = refs[at:]
    per = RADIX // pencils
    rows = out_ref.shape[1]

    def read(chunk, pencil, c):
        found = [ref[pencil, c] for ref in ins[chunk]]
        return jnp.concatenate(found, axis=0) if len(found) > 1 else found[0]

    def pair(t):
        if width == 2:
            pencil, place = divmod(2 * t, per)
            return jnp.concatenate([read(place // 2, pencil, c) for c in range(2)], axis=1)
        found = []
        for c in range(2):
            for odd in range(2):
                pencil, place = divmod(2 * t + odd, per)
                found.append(read(place, pencil, c))
        return jnp.concatenate(found, axis=1)

    for s in range(8):
        total = None
        for place, r in enumerate((s, 8 if s == 0 else RADIX - s)):
            high, low = split_value(pair(r // 2))
            table_high = high_ref[s, 256 * place : 256 * place + 256]
            table_low = low_ref[s, 256 * place : 256 * place + 256]
            part = dot(high, table_high) + dot(low, table_high) + dot(high, table_low)
            total = part if total is None else total + part
        pieces[s] = total

    def step(b, carry):
        at = pl.ds(pl.multiple_of(b * 8, 8), 8)
        values = [(pieces[0, at, :INNER], None)]
        for s in range(1, 8):
            values.append((pieces[s, at, :INNER], pieces[s, at, INNER:]))
        values.append((pieces[0, at, INNER:], None))
        for n, value in enumerate(real_inverse(values)):
            out_ref[0, at, n * INNER : (n + 1) * INNER] = value
        return carry

    lax.fori_loop(0, rows // 8, step, 0)


def slot_at(r):
    return jnp.where(r == 8, 0, jnp.minimum(r, RADIX - r))


BLOCKS = 4


def fused_kernel(pencils, depths, background_ref, member_ref, layer_ref, phase_ref, density_ref, kern_ref, row_high_ref, row_low_ref,
                 back_high_ref, back_low_ref, table_ref, turns_ref, out_ref,
                 dens, sources, kern, row_high, row_low, back_high, back_low, tables, turns,
                 pieces, sending, landing, moved, gathered, spectra, waves, keep, other_keep, fields, half,
                 local_sem, b_sem, g_sem, a_send_sem, a_recv_sem, x_sem, c_sem):
    per = RADIX // pencils
    chunks = per // 2
    lanes = 2 * HALF
    part_rows = dens.shape[0]
    block = part_rows // BLOCKS
    out_rows = part_rows // depths
    share = moved.shape[0]
    me = lax.axis_index("pencil")
    deep = lax.axis_index("depth")
    grp, mem = lax.axis_index("grp"), lax.axis_index("mem")
    sharer = grp * 2 + mem
    first = sharer * share
    local = jnp.clip(layer_ref[0] - deep * kern.shape[0], 0, kern.shape[0] - 1)

    def remote(src, dst, send, recv, **where):
        return pltpu.make_async_remote_copy(
            src_ref=src, dst_ref=dst, send_sem=send, recv_sem=recv,
            device_id=where, device_id_type=pl.DeviceIdType.MESH,
        )

    def toward(shift):
        return lax.rem(me + shift, pencils)

    loads = []

    def load(src, dst):
        copy = pltpu.make_async_copy(src, dst, local_sem.at[len(loads)])
        copy.start()
        loads.append(copy)
        return copy

    source_loads = [
        load(kern_ref.at[:, :, pl.ds(pl.multiple_of(lax.rem(RADIX - first - u, RADIX) * INNER, INNER), INNER)], sources[u])
        for u in range(share)
    ]
    barrier = pltpu.get_barrier_semaphore()
    peers = [{"pencil": toward(shift)} for shift in range(1, pencils)]
    peers += [{"depth": 1 - deep}, {"grp": 1 - grp}, {"mem": 1 - mem}]
    for peer in peers:
        pl.semaphore_signal(barrier, inc=1, device_id=peer, device_id_type=pl.DeviceIdType.MESH)

    row_loads = [load(row_high_ref, row_high), load(row_low_ref, row_low)]
    dens_loads = [load(density_ref.at[0, 0, pl.ds(i * block, block)], dens.at[pl.ds(i * block, block)]) for i in range(BLOCKS)]
    partner = lax.rem(pencils - me, pencils)

    def rest(u):
        at = pl.ds(1, per - 1)
        return remote(moved.at[u, at], gathered.at[sharer, u, at], b_sem.at[0, u], b_sem.at[1, u], pencil=pencils - 1 - me)

    def zero(u):
        return remote(moved.at[u, 0], gathered.at[sharer, u, 0], b_sem.at[2, u], b_sem.at[3, u], pencil=partner)

    def stay(u):
        return pltpu.make_async_copy(moved.at[u, 0], gathered.at[sharer, u, 0], b_sem.at[4, u])

    plain = swapped(me < 0, (INNER, HALF), 1)
    edge = swapped(me == 0, (INNER, HALF), 1)
    for u in range(share):
        source_loads[u].wait()
        swap = swapped(first + u == 0, (INNER, INNER), 0)
        rows = [dot(swap, sources[u][local, c]).astype(bf16) for c in range(2)]
        for j in range(per):
            turn = edge if j == 0 else plain
            turned = [dot(rows[c][:, j * INNER : (j + 1) * INNER], turn) for c in range(2)]
            moved[u, (per - j) % per] = jnp.concatenate(turned, axis=1)

        if u == 0:
            pl.semaphore_wait(barrier, len(peers))
        rest(u).start()

        @pl.when(partner != me)
        def _(u=u):
            zero(u).start()

        @pl.when(partner == me)
        def _(u=u):
            stay(u).start()

    late_loads = [load(table_ref, tables), load(turns_ref, turns), load(kern_ref, kern),
                  load(back_high_ref, back_high), load(back_low_ref, back_low)]

    for copy in row_loads:
        copy.wait()
    offset = background_ref[member_ref[0]]

    def a_copy(chunk, shift, i):
        return remote(sending.at[chunk, shift, i], landing.at[chunk, shift - 1, i],
                      a_send_sem.at[chunk, shift - 1, i], a_recv_sem.at[chunk, shift - 1, i], pencil=toward(shift))

    for i in range(BLOCKS):
        dens_loads[i].wait()

        def step(b, carry, i=i):
            at = pl.ds(pl.multiple_of(b * 8, 8), 8)
            here = pl.ds(pl.multiple_of(i * block + b * 8, 8), 8)
            got = real_transform([dens[here, n * INNER : (n + 1) * INNER] - offset for n in range(RADIX)])
            pieces[0, at, :INNER] = got[0][0]
            pieces[0, at, INNER:] = got[8][0]
            for s in range(1, 8):
                pieces[s, at, :INNER] = got[s][0]
                pieces[s, at, INNER:] = got[s][1]
            return carry

        lax.fori_loop(0, block // 8, step, 0)

        def part(index, carry, i=i):
            shift, chunk = index // chunks, lax.rem(index, chunks)
            t = lax.rem(me + shift, pencils) * chunks + chunk
            total = None
            for odd in range(2):
                high, low = split_value(pieces[slot_at(2 * t + odd)])
                table_high = row_high[t, 256 * odd : 256 * odd + 256]
                table_low = row_low[t, 256 * odd : 256 * odd + 256]
                term = dot(high, table_high) + dot(low, table_high) + dot(high, table_low)
                total = term if total is None else total + term
            for c in range(2):
                sending[chunk, shift, i, c] = total[:, c * 128 : (c + 1) * 128]
            return carry

        lax.fori_loop(0, pencils * chunks, part, 0)
        for shift in SHIFTS:
            a_copy(0, shift, i).start()

    def start_a(chunk):
        for i in range(BLOCKS):
            for shift in SHIFTS:
                a_copy(chunk, shift, i).start()

    arrivals = [(i, shift) for i in range(BLOCKS) for shift in SHIFTS]

    def wait_a(chunk, which):
        for i, shift in which:
            a_copy(chunk, shift, i).wait_recv()

    for copy in late_loads:
        copy.wait()

    for u in range(share):
        rest(u).wait_recv()

        @pl.when(partner != me)
        def _(u=u):
            zero(u).wait_recv()
            zero(u).wait_send()

        @pl.when(partner == me)
        def _(u=u):
            stay(u).wait()

    own = gathered.at[sharer]
    far = (1 - grp) * 2 + mem
    across = remote(own, own, g_sem.at[0], g_sem.at[1], grp=1 - grp)
    across.start()
    beside = remote(own, own, g_sem.at[2], g_sem.at[3], mem=1 - mem)
    beside.start()
    wait_a(0, arrivals[:AHEAD])
    start_a(1)
    across.wait_recv()
    passed = remote(gathered.at[far], gathered.at[far], g_sem.at[4], g_sem.at[5], mem=1 - mem)
    passed.start()
    beside.wait_recv()
    passed.wait_recv()

    from_lane = lax.broadcasted_iota(jnp.int32, (2 * INNER, lanes), 0)
    to_lane = lax.broadcasted_iota(jnp.int32, (2 * INNER, lanes), 1)
    pick = jnp.where(from_lane == to_lane + jnp.where(to_lane < HALF, 0, HALF), 0.5, 0.0).astype(bf16)
    from_lane, to_lane = from_lane[:INNER], to_lane[:INNER]
    pick_edge = jnp.where((from_lane == HALF) & (to_lane == 0), 0.5, 0.0).astype(bf16)
    mask = (to_lane == 0) & (me == 0)

    def turned(r):
        cos, sin = turns[r, :, 0:1], turns[r, :, 1:2]
        pc, ps = (phase_ref[(me * RADIX + r) * 2 + c] for c in range(2))
        return cos * pc - sin * ps, sin * pc + cos * ps

    def wave(r):
        re, im = spectra[r, :INNER], spectra[r, INNER:]
        c, s = turned(r)
        high, low = split_value(jnp.concatenate([re * c + im * s, im * c - re * s], axis=0))
        return dot(tables[0], high) + dot(tables[0], low) + dot(tables[1], high)

    def finish(chunk, r, got):
        re, im = got[:INNER], got[INNER:]
        rows = pl.ds(pl.multiple_of(r * INNER, INNER), INNER)
        holder, u = r // share, lax.rem(r, share)
        parts = []
        for c in range(2):
            other = [gathered[holder, u, 2 * chunk + j, :, c * HALF : (c + 1) * HALF] for j in range(2)]
            other = jnp.concatenate(other, axis=1)
            mine = dot(kern[local, c, rows, 2 * chunk * INNER : 2 * (chunk + 1) * INNER], pick)
            parts.append(mine + 0.5 * other if c == 0 else mine - 0.5 * other)
        kr, ki = parts
        if chunk == 0:
            other = lax.rem(RADIX - r, RADIX)
            other_rows = pl.ds(pl.multiple_of(other * INNER, INNER), INNER)
            swap = swapped(r == 0, (INNER, INNER), 0)
            edges = []
            for c in range(2):
                mine = dot(kern[local, c, rows, :INNER], pick_edge)
                flipped = dot(swap, kern[local, c, other_rows, :INNER]).astype(bf16)
                flipped = dot(flipped, pick_edge)
                edges.append(mine + flipped if c == 0 else mine - flipped)
            high, low = split_value(waves[other])
            ore = dot(swap, high[:INNER]) + dot(swap, low[:INNER])
            oim = -(dot(swap, high[INNER:]) + dot(swap, low[INNER:]))
            hr = jnp.where(mask, 0.5 * (kr - edges[0]), 0.0)
            hi = jnp.where(mask, 0.5 * (ki - edges[1]), 0.0)
            kr, ki = kr - hr, ki - hi
            sr = re * kr - im * ki + (ore * hr - oim * hi)
            si = re * ki + im * kr + (ore * hi + oim * hr)
        else:
            sr, si = re * kr - im * ki, re * ki + im * kr
        high, low = split_value(jnp.concatenate([sr, si], axis=0))
        got = dot(tables[2], high) + dot(tables[2], low) + dot(tables[3], high)
        re, im = got[:INNER], got[INNER:]
        c, s = turned(r)
        spectra[r, :INNER] = re * c - im * s
        spectra[r, INNER:] = im * c + re * s

    def columns(chunk):
        def forward(b, carry):
            values = []
            for n in range(RADIX):
                j, begin = divmod(n * INNER, part_rows)
                i, begin = divmod(begin, block)
                at = pl.ds(pl.multiple_of(begin + b * 8, 8), 8)
                ref = sending.at[chunk, 0, i] if j == 0 else landing.at[chunk, pencils - j - 1, i]
                values.append((ref[0, at, :], ref[1, at, :]))
            at = pl.ds(pl.multiple_of(b * 8, 8), 8)
            also = pl.ds(pl.multiple_of(INNER + b * 8, 8), 8)
            for r, (re, im) in enumerate(transform(values, -1)):
                spectra[r, at, :] = re
                spectra[r, also, :] = im
            return carry

        lax.fori_loop(0, INNER // 8, forward, 0)

        def early(i, carry):
            for u in range(UNROLL):
                waves[i * UNROLL + u] = wave(i * UNROLL + u)
            return carry

        def late(i, carry):
            for u in range(UNROLL):
                r = i * UNROLL + u
                finish(chunk, r, waves[r] if chunk == 0 else wave(r))
            return carry

        if chunk == 0:
            lax.fori_loop(0, RADIX // UNROLL, early, 0)
        lax.fori_loop(0, RADIX // UNROLL, late, 0)

        def backward(b, carry):
            at = pl.ds(pl.multiple_of(b * 8, 8), 8)
            also = pl.ds(pl.multiple_of(INNER + b * 8, 8), 8)
            values = [(spectra[r, at, :], spectra[r, also, :]) for r in range(RADIX)]
            for n, (re, im) in enumerate(transform(values, 1)):
                shift_depth, begin = divmod(n * INNER, out_rows)
                shift, depth = divmod(shift_depth, depths)
                put = pl.ds(pl.multiple_of(begin + b * 8, 8), 8)
                slot = jnp.where(deep == depth, 0, 1)
                keep[chunk, slot, shift, 0, put, :] = re
                keep[chunk, slot, shift, 1, put, :] = im
            return carry

        lax.fori_loop(0, INNER // 8, backward, 0)

    out_block = out_rows // PARTS

    def x_copy(chunk, j, i):
        at = pl.ds(i * out_block, out_block)
        return remote(keep.at[chunk, 1, j, :, at], other_keep.at[chunk, j, :, at],
                      x_sem.at[0, chunk, j, i], x_sem.at[1, chunk, j, i], depth=1 - deep)

    def c_copy(chunk, j, i):
        at = pl.ds(i * out_block, out_block)
        return remote(keep.at[chunk, 0, j, :, at], fields.at[chunk, j - 1, :, at],
                      c_sem.at[0, chunk, j - 1, i], c_sem.at[1, chunk, j - 1, i], pencil=toward(j))

    def summed(chunk, j, i):
        x_copy(chunk, j, i).wait_recv()
        at = pl.ds(i * out_block, out_block)
        keep[chunk, 0, j, :, at] += other_keep[chunk, j, :, at]

    def gather_field(chunk, shift, i):
        t = lax.rem(me + pencils - shift, pencils) * chunks + chunk
        at = pl.ds(i * out_block, out_block)
        ref = keep.at[chunk, 0, 0] if shift == 0 else fields.at[chunk, shift - 1]
        high, low = split_value(jnp.concatenate([ref[0, at], ref[1, at]], axis=1))
        for odd in range(2):
            r = 2 * t + odd
            half[slot_at(r), at] += dot(high, back_high[r]) + dot(low, back_high[r]) + dot(high, back_low[r])

    half[...] = jnp.zeros_like(half)
    wait_a(0, arrivals[AHEAD:])
    columns(0)
    pairs = [(i, j) for i in range(PARTS) for j in ORDER]
    for i, j in pairs:
        x_copy(0, j, i).start()
    for i, j in pairs:
        summed(0, j, i)
    wait_a(1, arrivals[:BEFORE])
    for i, j in pairs:
        if j:
            c_copy(0, j, i).start()
    wait_a(1, arrivals[BEFORE:])
    columns(1)
    for i, j in pairs:
        x_copy(1, j, i).start()
    for i in range(PARTS):
        gather_field(0, 0, i)
    for i, j in pairs:
        summed(1, j, i)
        if j:
            c_copy(1, j, i).start()
    for i in range(PARTS):
        gather_field(1, 0, i)
    for i, j in pairs:
        if j:
            c_copy(0, j, i).wait_recv()
            gather_field(0, j, i)
    leaving = []
    for i in range(PARTS):
        for j in ORDER:
            if j:
                c_copy(1, j, i).wait_recv()
                gather_field(1, j, i)
        for quarter in range(LEAVE):
            at = pl.ds(i * out_block + quarter * (out_block // LEAVE), out_block // LEAVE)
            leaving.append(pltpu.make_async_copy(half.at[:, at], out_ref.at[:, at], local_sem.at[len(leaving)]))
            leaving[-1].start()
    for copy in leaving:
        copy.wait()

    for u in range(share):
        rest(u).wait_send()
    across.wait_send()
    beside.wait_send()
    passed.wait_send()
    for chunk in range(chunks):
        for shift in SHIFTS:
            for i in range(BLOCKS):
                a_copy(chunk, shift, i).wait_send()
        for j in ORDER:
            for i in range(PARTS):
                x_copy(chunk, j, i).wait_send()
                if j:
                    c_copy(chunk, j, i).wait_send()


def last_kernel(in_ref, out_ref, half, done, sem):
    block = half.shape[1] // LAST

    def copies(i):
        at = pl.ds(i * block, block)
        return (pltpu.make_async_copy(in_ref.at[:, at], half.at[:, at], sem.at[0, i]),
                pltpu.make_async_copy(done.at[at], out_ref.at[0, at], sem.at[1, i]))

    def last(b, carry):
        at = pl.ds(pl.multiple_of(b * STEP, STEP), STEP)
        values = [(half[0, at, :INNER], None)]
        for s in range(1, 8):
            values.append((half[s, at, :INNER], half[s, at, INNER:]))
        values.append((half[0, at, INNER:], None))
        for n, value in enumerate(real_inverse(values)):
            done[at, n * INNER : (n + 1) * INNER] = value
        return carry

    for i in range(LAST):
        copies(i)[0].start()
    for i in range(LAST):
        copies(i)[0].wait()
        lax.fori_loop(i * block // STEP, (i + 1) * block // STEP, last, 0)
        copies(i)[1].start()
    for i in range(LAST):
        copies(i)[1].wait()


STEP = 16
LAST = 8
SHIFTS = (2, 1, 3)
ORDER = (2, 1, 3, 0)
UNROLL = 4
AHEAD = 9
BEFORE = 12
PARTS = 1
LEAVE = 4


def params(**more):
    return pltpu.CompilerParams(vmem_limit_bytes=48 * 1024 * 1024, **more)


def wide_body(density, background, member_ids, layer_kernel, kernel_spectra):
    pencils = lax.axis_size("pencil")
    depths = lax.axis_size("depth")
    sharers = lax.axis_size("grp") * lax.axis_size("mem")
    pencil = lax.axis_index("pencil")
    per = RADIX // pencils
    width = min(per, 2)
    chunks = per // width
    lanes = width * HALF
    part_rows = density.shape[2]
    out_rows = part_rows // depths
    vmem = pl.BlockSpec(memory_space=pltpu.VMEM)
    smem = pl.BlockSpec(memory_space=pltpu.SMEM)

    kern_count = kernel_spectra.shape[0]
    local = layer_kernel[0] - lax.axis_index("depth") * kern_count
    share = RADIX // sharers
    first = lax.axis_index(("grp", "mem")) * share
    groups = [1] if per == 1 else [1, per - 1]
    moved = pl.pallas_call(
        functools.partial(mirror_kernel, share),
        grid_spec=pltpu.PrefetchScalarGridSpec(
            num_scalar_prefetch=1,
            grid=(1,),
            in_specs=[
                pl.BlockSpec(
                    (None, 2, INNER, per * INNER),
                    lambda i, w, u=u: (w[0], 0, lax.rem(RADIX - w[1] - u, RADIX), 0),
                )
                for u in range(share)
            ],
            out_specs=[pl.BlockSpec((g, share, INNER, INNER), lambda i, w: (0, 0, 0, 0)) for g in groups],
        ),
        out_shape=[jax.ShapeDtypeStruct((g, share, INNER, INNER), f32) for g in groups],
        compiler_params=params(),
        cost_estimate=pl.CostEstimate(flops=1 << 20, bytes_accessed=2 << 20, transcendentals=0),
    )(jnp.stack([local, first, pencil]), *[kernel_spectra] * share)
    mirrored = lax.ppermute(moved[0], "pencil", [(p, (pencils - p) % pencils) for p in range(pencils)])
    if per > 1:
        rest = lax.ppermute(moved[1], "pencil", [(p, pencils - 1 - p) for p in range(pencils)])

    offset = lax.dynamic_index_in_dim(background[:, 0], member_ids[0], 0, keepdims=True)
    row_high, row_low = halves(row_tables())
    block = min(part_rows, 128)
    sent = pl.pallas_call(
        functools.partial(rows_kernel, pencils, width),
        grid=(part_rows // block,),
        in_specs=[
            smem,
            pl.BlockSpec((None, None, block, LENGTH), lambda i: (0, 0, i, 0)),
            pl.BlockSpec((8, 512, 256), lambda i: (0, 0, 0)),
            pl.BlockSpec((8, 512, 256), lambda i: (0, 0, 0)),
        ],
        out_specs=[pl.BlockSpec((pencils, 2, block, lanes), lambda i: (0, 0, i, 0))] * chunks,
        out_shape=[jax.ShapeDtypeStruct((pencils, 2, part_rows, lanes), f32)] * chunks,
        scratch_shapes=[pltpu.VMEM((8, block, 256), f32)],
        compiler_params=params(),
        cost_estimate=pl.CostEstimate(flops=6 * part_rows * 2 * LENGTH * 512, bytes_accessed=12 << 20, transcendentals=0),
    )(offset, density, row_high, row_low)
    arrived = [lax.all_to_all(part, "pencil", 0, 0, tiled=True) for part in sent]

    sign = jnp.array([0.5, -0.5], f32)
    edge = lax.dynamic_slice(kernel_spectra, (local, 0, 0, HALF), (1, 2, LENGTH, 1))
    edge = edge.reshape(2, RADIX, INNER).astype(f32)
    flipped = jnp.concatenate([edge[:, :1], edge[:, :0:-1]], axis=1)[..., ::-1]
    flipped = jnp.concatenate([jnp.roll(flipped[:, :1], 1, axis=2), flipped[:, 1:]], axis=1)
    edge = 0.5 * edge + sign.reshape(2, 1, 1) * flipped
    edge = jnp.where(lax.broadcasted_iota(jnp.int32, (lanes,), 0) == 0, edge[..., None], 0.0)

    if per > 1:
        mirrored = jnp.concatenate([mirrored, rest], axis=0)
    mirrored, edge, _ = lax.optimization_barrier((mirrored, edge, sent[0]))
    mirrored = lax.all_gather(mirrored, ("grp", "mem"), axis=0)

    column, column_turns = column_tables()
    column_turns = jnp.asarray(column_turns)
    tables = jnp.stack(halves(column) + halves(column.T))
    two = depths == 2
    mine = lax.axis_index("depth") if two else jnp.int32(0)
    where = jnp.stack([mine, local, pencil])
    fields = []
    before = None
    for k in range(chunks):
        special = k == 0
        steps = sharers

        def early(i, special=special):
            return jnp.minimum(i, steps - 1) if special else i

        def late(i, special=special):
            return jnp.maximum(i - steps, 0) if special else i

        here = arrived[k]
        if before is not None:
            here, before = lax.optimization_barrier((here, before))
            fields.append(lax.all_to_all(before, "pencil", 0, 0, tiled=True))
        edge_block = (2, share, INNER, lanes) if special else (2, 1, 8, lanes)
        out = pl.pallas_call(
            functools.partial(columns_kernel, special),
            grid_spec=pltpu.PrefetchScalarGridSpec(
                num_scalar_prefetch=1,
                grid=(2 * steps if special else steps,),
                in_specs=[
                    pl.BlockSpec((pencils, 2, part_rows, lanes), lambda i, w: (0, 0, 0, 0)),
                    pl.BlockSpec(
                        (None, 2, share * INNER, width * INNER), lambda i, w, k=k, late=late: (w[1], 0, late(i), k)
                    ),
                    pl.BlockSpec(
                        (None, width, share, INNER, INNER), lambda i, w, k=k, late=late: (late(i), k, 0, 0, 0)
                    ),
                    pl.BlockSpec(
                        edge_block,
                        (lambda i, w, late=late: (0, late(i), 0, 0)) if special else (lambda i, w: (0, 0, 0, 0)),
                    ),
                ]
                + [pl.BlockSpec((share, INNER, INNER), lambda i, w, early=early: (early(i), 0, 0))]
                + [pl.BlockSpec((share, INNER, INNER), lambda i, w, late=late: (late(i), 0, 0))]
                + [pl.BlockSpec((4, 256, 256), lambda i, w: (0, 0, 0))],
                out_specs=pl.BlockSpec((depths, pencils, 2, out_rows, lanes), lambda i, w: (0, 0, 0, 0, 0)),
                scratch_shapes=[
                    pltpu.VMEM((RADIX, 256, lanes), f32),
                    pltpu.VMEM((RADIX if special else 1, 256, lanes), f32),
                ],
            ),
            out_shape=jax.ShapeDtypeStruct((depths, pencils, 2, out_rows, lanes), f32),
            compiler_params=params(),
            cost_estimate=pl.CostEstimate(
                flops=12 * RADIX * 256 * 256 * lanes, bytes_accessed=16 << 20, transcendentals=0
            ),
        )(where, here, kernel_spectra, mirrored, edge, column_turns, column_turns, tables)
        if two:
            before = out[0] + lax.ppermute(out[1], "depth", [(0, 1), (1, 0)])
        else:
            before = lax.psum_scatter(out, "depth", scatter_dimension=0, tiled=False)
    fields.append(lax.all_to_all(before, "pencil", 0, 0, tiled=True))

    back_high, back_low = halves(inverse_row_tables())
    return pl.pallas_call(
        functools.partial(fields_kernel, pencils, width, [1] * chunks),
        in_specs=[vmem] * (len(fields) + 2),
        out_specs=vmem,
        out_shape=jax.ShapeDtypeStruct((1, out_rows, LENGTH), f32),
        scratch_shapes=[pltpu.VMEM((8, out_rows, 256), f32)],
        compiler_params=params(),
        cost_estimate=pl.CostEstimate(flops=6 * out_rows * 2 * LENGTH * 512, bytes_accessed=8 << 20, transcendentals=0),
    )(*fields, back_high, back_low)


def fused_body(density, background, member_ids, layer_kernel, kernel_spectra):
    pencils = lax.axis_size("pencil")
    depths = lax.axis_size("depth")
    sharers = lax.axis_size("grp") * lax.axis_size("mem")
    per = RADIX // pencils
    chunks = per // 2
    lanes = 2 * HALF
    part_rows = density.shape[2]
    out_rows = part_rows // depths
    share = RADIX // sharers
    smem = pl.BlockSpec(memory_space=pltpu.SMEM)
    anywhere = pl.BlockSpec(memory_space=pl.ANY)

    angles = 2 * np.pi * np.arange(pencils)[:, None] * np.arange(RADIX)[None, :] / pencils
    phases = jnp.asarray(np.stack([np.cos(angles), np.sin(angles)], axis=-1).round(15).reshape(-1), f32)
    row_high, row_low = halves(row_tables())
    where = [0 if r == 8 else min(r, RADIX - r) for r in range(RADIX)], [int(r >= 8) for r in range(RADIX)]
    back_high, back_low = halves(inverse_row_tables().reshape(8, 2, 256, 256)[where])
    column, turns = column_tables()
    tables = jnp.stack(halves(column) + halves(column.T))
    turns = jnp.asarray(turns)
    dma = pltpu.SemaphoreType.DMA
    half = pl.pallas_call(
        functools.partial(fused_kernel, pencils, depths),
        in_specs=[smem] * 4 + [anywhere] * 8,
        out_specs=anywhere,
        out_shape=jax.ShapeDtypeStruct((8, out_rows, 256), f32),
        scratch_shapes=[
            pltpu.VMEM((part_rows, LENGTH), f32),
            [pltpu.VMEM((kernel_spectra.shape[0], 2, INNER, per * INNER), bf16)] * share,
            pltpu.VMEM(kernel_spectra.shape, bf16),
            pltpu.VMEM(row_high.shape, bf16),
            pltpu.VMEM(row_low.shape, bf16),
            pltpu.VMEM(back_high.shape, bf16),
            pltpu.VMEM(back_low.shape, bf16),
            pltpu.VMEM(tables.shape, bf16),
            pltpu.VMEM(turns.shape, f32),
            pltpu.VMEM((8, part_rows // BLOCKS, 256), f32),
            pltpu.VMEM((chunks, pencils, BLOCKS, 2, part_rows // BLOCKS, lanes), f32),
            pltpu.VMEM((chunks, pencils - 1, BLOCKS, 2, part_rows // BLOCKS, lanes), f32),
            pltpu.VMEM((share, per, INNER, INNER), f32),
            pltpu.VMEM((sharers, share, per, INNER, INNER), f32),
            pltpu.VMEM((RADIX, 256, lanes), f32),
            pltpu.VMEM((RADIX, 256, lanes), f32),
            pltpu.VMEM((chunks, 2, pencils, 2, out_rows, lanes), f32),
            pltpu.VMEM((chunks, pencils, 2, out_rows, lanes), f32),
            pltpu.VMEM((chunks, pencils - 1, 2, out_rows, lanes), f32),
            pltpu.VMEM((8, out_rows, 256), f32),
            dma((share + BLOCKS + 7,)),
            dma((5, share)),
            dma((6,)),
            dma((chunks, pencils - 1, BLOCKS)),
            dma((chunks, pencils - 1, BLOCKS)),
            dma((2, chunks, pencils, PARTS)),
            dma((2, chunks, pencils - 1, PARTS)),
        ],
        compiler_params=pltpu.CompilerParams(
            vmem_limit_bytes=60 * 1024 * 1024, collective_id=0, has_side_effects=True
        ),
    )(background.reshape(-1), member_ids, layer_kernel, phases, density, kernel_spectra, row_high, row_low, back_high, back_low, tables, turns)
    return pl.pallas_call(
        last_kernel,
        in_specs=[anywhere],
        out_specs=anywhere,
        out_shape=jax.ShapeDtypeStruct((1, out_rows, LENGTH), f32),
        scratch_shapes=[
            pltpu.VMEM((8, out_rows, 256), f32),
            pltpu.VMEM((out_rows, LENGTH), f32),
            dma((2, LAST)),
        ],
        compiler_params=pltpu.CompilerParams(vmem_limit_bytes=60 * 1024 * 1024),
    )(half)


def body(density, background, member_ids, layer_kernel, kernel_spectra):
    sizes = tuple(lax.axis_size(name) for name in ("grp", "pencil", "depth", "mem"))
    plan = fused_body if sizes == (2, 4, 2, 2) else wide_body
    return plan(density, background, member_ids, layer_kernel, kernel_spectra)


def solution(mesh):
    placed = (
        P(("grp", "mem"), "depth", "pencil", None),
        P(None, "depth"),
        P(("grp", "mem")),
        P("depth"),
        P("depth", None, None, "pencil"),
    )
    return jax.shard_map(
        body,
        mesh=mesh,
        in_specs=placed,
        out_specs=P(("grp", "mem"), ("pencil", "depth"), None),
        check_vma=False,
    )
```

```python
import functools
import math

import jax
import jax.numpy as jnp
import numpy as np
from jax import lax
from jax.experimental import pallas as pl
from jax.experimental.pallas import tpu as pltpu
from jax.sharding import PartitionSpec as P

RADIX = 16
INNER = 128
HALF = 64
LENGTH = RADIX * INNER
f32 = jnp.float32
bf16 = jnp.bfloat16


def halves(table):
    table = np.asarray(table, np.float32)
    high = table.astype(bf16)
    low = (table - high.astype(np.float32)).astype(bf16)
    return jnp.asarray(high), jnp.asarray(low)


def residue_rows(r):
    m = np.arange(INNER)[:, None]
    q = np.arange(HALF)[None, :]
    turn = np.exp(-2j * np.pi * (((RADIX * q + r) * m) % LENGTH) / LENGTH)
    re, im = turn.real.copy(), turn.imag.copy()
    if r == 0:
        im[:, 0] = (-1.0) ** m[:, 0]
    out = np.zeros((2 * INNER, 2 * HALF))
    if r == 0:
        out[:INNER, :HALF], out[:INNER, HALF:] = re, im
    elif r == 8:
        out[INNER:, :HALF], out[INNER:, HALF:] = re, im
    else:
        sign = 1.0 if r < 8 else -1.0
        out[:INNER, :HALF], out[:INNER, HALF:] = re, im
        out[INNER:, :HALF], out[INNER:, HALF:] = -sign * im, sign * re
    return out


def slot_of(r):
    return 0 if r in (0, 8) else min(r, RADIX - r)


def row_tables():
    tables = np.zeros((8, 512, 256))
    for t in range(8):
        for odd in range(2):
            block = residue_rows(2 * t + odd)
            rows = slice(256 * odd, 256 * odd + 256)
            tables[t, rows, HALF * odd : HALF * odd + HALF] = block[:, :HALF]
            tables[t, rows, 128 + HALF * odd : 128 + HALF * odd + HALF] = block[:, HALF:]
    return tables


def inverse_row_tables():
    tables = np.zeros((8, 512, 256))
    scale = 1.0 / (LENGTH * LENGTH)
    for s in range(8):
        for place, r in enumerate((s, 8 if s == 0 else RADIX - s)):
            block = residue_rows(r).T.copy() * scale
            weight = np.full((2 * HALF, 1), 2.0 if r in (0, 8) else 1.0)
            if r == 0:
                weight[0] = weight[HALF] = 1.0
            block *= weight
            odd = r % 2
            tables[s, 256 * place + HALF * odd : 256 * place + HALF * odd + HALF] += block[:HALF]
            tables[s, 256 * place + 128 + HALF * odd : 256 * place + 128 + HALF * odd + HALF] += block[HALF:]
    return tables


def column_tables():
    q = np.arange(INNER)[:, None]
    m = np.arange(INNER)[None, :]
    turn = np.exp(-2j * np.pi * ((q * m) % INNER) / INNER)
    table = np.block([[turn.real, -turn.imag], [turn.imag, turn.real]])
    angles = 2 * np.pi * np.arange(RADIX)[:, None] * np.arange(INNER)[None, :] / LENGTH
    turns = np.zeros((RADIX, INNER, INNER), np.float32)
    turns[..., 0] = np.cos(angles)
    turns[..., 1] = np.sin(angles)
    return table, turns


def split_value(value):
    high = value.astype(bf16)
    return high, (value - high.astype(f32)).astype(bf16)


def dot(a, b):
    return jnp.dot(a, b, preferred_element_type=f32)


def rotate(value, count, length, sign):
    re, im = value
    count %= length
    if count == 0:
        return value
    if 4 * count == length:
        return (im, -re) if sign < 0 else (-im, re)
    c = math.cos(2 * math.pi * count / length)
    s = sign * math.sin(2 * math.pi * count / length)
    if 8 * count == length:
        return ((re + im) * c, (im - re) * c) if sign < 0 else ((re - im) * c, (im + re) * c)
    return (re * c - im * s, re * s + im * c)


def plus(a, b):
    return (a[0] + b[0], a[1] + b[1])


def minus(a, b):
    return (a[0] - b[0], a[1] - b[1])


def transform(values, sign):
    length = len(values)
    if length == 1:
        return values
    even, odd = transform(values[0::2], sign), transform(values[1::2], sign)
    turned = [rotate(odd[k], k, length, sign) for k in range(length // 2)]
    return [plus(even[k], turned[k]) for k in range(length // 2)] + [
        minus(even[k], turned[k]) for k in range(length // 2)
    ]


def real_transform(values):
    length = len(values)
    if length == 2:
        return [(values[0] + values[1], None), (values[0] - values[1], None)]
    even, odd = real_transform(values[0::2]), real_transform(values[1::2])
    out = [None] * (length // 2 + 1)
    out[0] = (even[0][0] + odd[0][0], None)
    out[length // 2] = (even[0][0] - odd[0][0], None)
    quarter = length // 4
    for k in range(1, quarter):
        turned = rotate(odd[k], k, length, -1)
        out[k] = plus(even[k], turned)
        low = minus(even[k], turned)
        out[length // 2 - k] = (low[0], -low[1])
    out[quarter] = (even[quarter][0], -odd[quarter][0])
    return out


def real_inverse(values):
    half = len(values) - 1
    length = 2 * half
    if length == 2:
        return [values[0][0] + values[1][0], values[0][0] - values[1][0]]
    even, odd = [], []
    for k in range(half // 2 + 1):
        if k == 0:
            even.append((values[0][0] + values[half][0], None))
            odd.append((values[0][0] - values[half][0], None))
        elif k == half // 2:
            even.append((2.0 * values[k][0], None))
            odd.append((-2.0 * values[k][1], None))
        else:
            other = values[half - k]
            even.append((values[k][0] + other[0], values[k][1] - other[1]))
            odd.append(rotate((values[k][0] - other[0], values[k][1] + other[1]), k, length, 1))
    first, second = real_inverse(even), real_inverse(odd)
    return [x for pair in zip(first, second) for x in pair]


def rows_kernel(pencils, width, offset_ref, in_ref, high_ref, low_ref, *rest):
    outs, pieces = rest[:-1], rest[-1]
    rows = in_ref.shape[0]
    per = RADIX // pencils
    offset = offset_ref[0]

    def step(b, carry):
        at = pl.ds(pl.multiple_of(b * 8, 8), 8)
        values = [in_ref[at, n * INNER : (n + 1) * INNER] - offset for n in range(RADIX)]
        got = real_transform(values)
        pieces[0, at, :INNER] = got[0][0]
        pieces[0, at, INNER:] = got[8][0]
        for s in range(1, 8):
            pieces[s, at, :INNER] = got[s][0]
            pieces[s, at, INNER:] = got[s][1]
        return carry

    lax.fori_loop(0, rows // 8, step, 0)
    for t in range(8):
        total = None
        for odd in range(2):
            high, low = split_value(pieces[slot_of(2 * t + odd)])
            table_high = high_ref[t, 256 * odd : 256 * odd + 256]
            table_low = low_ref[t, 256 * odd : 256 * odd + 256]
            part = dot(high, table_high) + dot(low, table_high) + dot(high, table_low)
            total = part if total is None else total + part
        if width == 2:
            pencil, place = divmod(2 * t, per)
            for c in range(2):
                outs[place // 2][pencil, c] = total[:, c * 128 : (c + 1) * 128]
        else:
            for odd in range(2):
                pencil, place = divmod(2 * t + odd, per)
                for c in range(2):
                    begin = c * 128 + odd * HALF
                    outs[place][pencil, c] = total[:, begin : begin + HALF]


def swapped(zero, shape, axis):
    total = lax.broadcasted_iota(jnp.int32, shape, 0) + lax.broadcasted_iota(jnp.int32, shape, 1)
    wanted = jnp.where(zero, INNER, INNER - 1)
    also = jnp.where(zero, 0, INNER - 1)
    return jnp.where((total == wanted) | (total == also), 1.0, 0.0).astype(bf16)


def mirror_kernel(share, where_ref, *refs):
    ins, zero_ref, rest_refs = refs[:share], refs[share], refs[share + 1 :]
    per = ins[0].shape[2] // INNER
    plain = swapped(where_ref[1] < 0, (INNER, HALF), 1)
    edge = swapped(where_ref[2] == 0, (INNER, HALF), 1)
    for u in range(share):
        swap = swapped(where_ref[1] + u == 0, (INNER, INNER), 0)
        rows = [dot(swap, ins[u][c]).astype(bf16) for c in range(2)]
        for j in range(per):
            turn = edge if j == 0 else plain
            turned = [dot(rows[c][:, j * INNER : (j + 1) * INNER], turn) for c in range(2)]
            value = jnp.concatenate(turned, axis=1)
            if j == 0:
                zero_ref[0, u] = value
            else:
                rest_refs[0][per - 1 - j, u] = value


def columns_kernel(special, where_ref, in_ref, kern_ref, mirror_ref, edge_ref,
                   turns_ref, late_ref, table_ref, out_ref, pieces, waves):
    part_rows = in_ref.shape[2]
    depths, pencils, _, out_rows, lanes = out_ref.shape
    share = mirror_ref.shape[1]
    steps = RADIX // share
    mine = where_ref[0]
    now = pl.program_id(0)
    from_lane = lax.broadcasted_iota(jnp.int32, (kern_ref.shape[2], lanes), 0)
    to_lane = lax.broadcasted_iota(jnp.int32, (kern_ref.shape[2], lanes), 1)
    wanted = to_lane + jnp.where(to_lane < HALF, 0, HALF)
    pick = jnp.where(from_lane == wanted, 0.5, 0.0).astype(bf16)
    zero_swap = swapped(mine >= 0, (INNER, INNER), 0)
    plain_swap = swapped(mine < 0, (INNER, INNER), 0)

    def forward(b, carry):
        values = []
        for n in range(RADIX):
            source, begin = divmod(n * INNER, part_rows)
            at = pl.ds(pl.multiple_of(begin + b * 8, 8), 8)
            values.append((in_ref[source, 0, at, :], in_ref[source, 1, at, :]))
        at = pl.ds(pl.multiple_of(b * 8, 8), 8)
        also = pl.ds(pl.multiple_of(INNER + b * 8, 8), 8)
        for r, (re, im) in enumerate(transform(values, -1)):
            pieces[r, at, :] = re
            pieces[r, also, :] = im
        return carry

    @pl.when(now == 0)
    def _():
        lax.fori_loop(0, INNER // 8, forward, 0)

    def wave(r, u):
        re, im = pieces[r, :INNER], pieces[r, INNER:]
        c, s = turns_ref[u, :, 0:1], turns_ref[u, :, 1:2]
        high, low = split_value(jnp.concatenate([re * c + im * s, im * c - re * s], axis=0))
        return dot(table_ref[0], high) + dot(table_ref[0], low) + dot(table_ref[1], high)

    def finish(r, u, got):
        re, im = got[:INNER], got[INNER:]
        tiles = [mirror_ref[j, u] for j in range(mirror_ref.shape[0])]
        rows = slice(u * INNER, (u + 1) * INNER)
        parts = []
        for c in range(2):
            other = [tile[:, c * HALF : (c + 1) * HALF] for tile in tiles]
            other = jnp.concatenate(other, axis=1) if len(other) > 1 else other[0]
            own = dot(kern_ref[c, rows, :], pick)
            parts.append(own + 0.5 * other if c == 0 else own - 0.5 * other)
        kr, ki = parts
        if special:
            other = lax.rem(RADIX - r, RADIX)
            high, low = split_value(waves[other])
            swap = jnp.where(r == 0, zero_swap.astype(f32), plain_swap.astype(f32)).astype(bf16) if u == 0 else plain_swap
            ore = dot(swap, high[:INNER]) + dot(swap, low[:INNER])
            oim = -(dot(swap, high[INNER:]) + dot(swap, low[INNER:]))
            mask = (lax.broadcasted_iota(jnp.int32, (INNER, lanes), 1) == 0) & (where_ref[2] == 0)
            hr = jnp.where(mask, 0.5 * (kr - edge_ref[0, u]), 0.0)
            hi = jnp.where(mask, 0.5 * (ki - edge_ref[1, u]), 0.0)
            kr, ki = kr - hr, ki - hi
            sr = re * kr - im * ki + (ore * hr - oim * hi)
            si = re * ki + im * kr + (ore * hi + oim * hr)
        else:
            sr, si = re * kr - im * ki, re * ki + im * kr
        spectrum = jnp.concatenate([sr, si], axis=0)
        high, low = split_value(spectrum)
        got = dot(table_ref[2], high) + dot(table_ref[2], low) + dot(table_ref[3], high)
        re, im = got[:INNER], got[INNER:]
        c, s = late_ref[u, :, 0:1], late_ref[u, :, 1:2]
        pieces[r, :INNER] = re * c - im * s
        pieces[r, INNER:] = im * c + re * s

    if special:
        @pl.when(now < steps)
        def _():
            for u in range(share):
                waves[now * share + u] = wave(now * share + u, u)

        @pl.when(now >= steps)
        def _():
            for u in range(share):
                r = (now - steps) * share + u
                finish(r, u, waves[r])
    else:
        for u in range(share):
            r = now * share + u
            finish(r, u, wave(r, u))

    slots = [lax.rem(d - mine + depths, depths) for d in range(depths)]

    def backward(b, carry):
        at = pl.ds(pl.multiple_of(b * 8, 8), 8)
        also = pl.ds(pl.multiple_of(INNER + b * 8, 8), 8)
        values = [(pieces[r, at, :], pieces[r, also, :]) for r in range(RADIX)]
        for n, (re, im) in enumerate(transform(values, 1)):
            if out_rows % INNER == 0:
                part, begin = divmod(n * INNER, out_rows)
                pencil, depth = divmod(part, depths)
                depth = slots[depth]
                put = pl.ds(pl.multiple_of(begin + b * 8, 8), 8)
            else:
                x = n * INNER + b * 8
                pencil = x // (out_rows * depths)
                depth = lax.rem(x // out_rows - mine + depths, depths)
                put = pl.ds(pl.multiple_of(lax.rem(x, out_rows), 8), 8)
            out_ref[depth, pencil, 0, put, :] = re
            out_ref[depth, pencil, 1, put, :] = im
        return carry

    @pl.when(now == pl.num_programs(0) - 1)
    def _():
        lax.fori_loop(0, INNER // 8, backward, 0)


def fields_kernel(pencils, width, counts, *refs):
    ins, at = [], 0
    for count in counts:
        ins.append(refs[at : at + count])
        at += count
    high_ref, low_ref, out_ref, pieces = refs[at:]
    per = RADIX // pencils
    rows = out_ref.shape[1]

    def read(chunk, pencil, c):
        found = [ref[pencil, c] for ref in ins[chunk]]
        return jnp.concatenate(found, axis=0) if len(found) > 1 else found[0]

    def pair(t):
        if width == 2:
            pencil, place = divmod(2 * t, per)
            return jnp.concatenate([read(place // 2, pencil, c) for c in range(2)], axis=1)
        found = []
        for c in range(2):
            for odd in range(2):
                pencil, place = divmod(2 * t + odd, per)
                found.append(read(place, pencil, c))
        return jnp.concatenate(found, axis=1)

    for s in range(8):
        total = None
        for place, r in enumerate((s, 8 if s == 0 else RADIX - s)):
            high, low = split_value(pair(r // 2))
            table_high = high_ref[s, 256 * place : 256 * place + 256]
            table_low = low_ref[s, 256 * place : 256 * place + 256]
            part = dot(high, table_high) + dot(low, table_high) + dot(high, table_low)
            total = part if total is None else total + part
        pieces[s] = total

    def step(b, carry):
        at = pl.ds(pl.multiple_of(b * 8, 8), 8)
        values = [(pieces[0, at, :INNER], None)]
        for s in range(1, 8):
            values.append((pieces[s, at, :INNER], pieces[s, at, INNER:]))
        values.append((pieces[0, at, INNER:], None))
        for n, value in enumerate(real_inverse(values)):
            out_ref[0, at, n * INNER : (n + 1) * INNER] = value
        return carry

    lax.fori_loop(0, rows // 8, step, 0)


def slot_at(r):
    return jnp.where(r == 8, 0, jnp.minimum(r, RADIX - r))


BLOCKS = 4


def fused_kernel(pencils, depths, background_ref, member_ref, layer_ref, phase_ref, density_ref, kern_ref, row_high_ref, row_low_ref,
                 back_high_ref, back_low_ref, table_ref, turns_ref, out_ref,
                 dens, sources, kern, row_high, row_low, back_high, back_low, tables, turns,
                 pieces, sending, landing, moved, gathered, spectra, waves, keep, other_keep, fields, half,
                 local_sem, b_sem, g_sem, a_send_sem, a_recv_sem, x_sem, c_sem):
    per = RADIX // pencils
    chunks = per // 2
    lanes = 2 * HALF
    part_rows = dens.shape[0]
    block = part_rows // BLOCKS
    out_rows = part_rows // depths
    share = moved.shape[0]
    me = lax.axis_index("pencil")
    deep = lax.axis_index("depth")
    grp, mem = lax.axis_index("grp"), lax.axis_index("mem")
    sharer = grp * 2 + mem
    first = sharer * share
    local = jnp.clip(layer_ref[0] - deep * kern.shape[0], 0, kern.shape[0] - 1)

    def remote(src, dst, send, recv, **where):
        return pltpu.make_async_remote_copy(
            src_ref=src, dst_ref=dst, send_sem=send, recv_sem=recv,
            device_id=where, device_id_type=pl.DeviceIdType.MESH,
        )

    def toward(shift):
        return lax.rem(me + shift, pencils)

    loads = []

    def load(src, dst):
        copy = pltpu.make_async_copy(src, dst, local_sem.at[len(loads)])
        copy.start()
        loads.append(copy)
        return copy

    source_loads = [
        load(kern_ref.at[:, :, pl.ds(pl.multiple_of(lax.rem(RADIX - first - u, RADIX) * INNER, INNER), INNER)], sources[u])
        for u in range(share)
    ]
    barrier = pltpu.get_barrier_semaphore()
    peers = [{"pencil": toward(shift)} for shift in range(1, pencils)]
    peers += [{"depth": 1 - deep}, {"grp": 1 - grp}, {"mem": 1 - mem}]
    for peer in peers:
        pl.semaphore_signal(barrier, inc=1, device_id=peer, device_id_type=pl.DeviceIdType.MESH)

    row_loads = [load(row_high_ref, row_high), load(row_low_ref, row_low)]
    dens_loads = [load(density_ref.at[0, 0, pl.ds(i * block, block)], dens.at[pl.ds(i * block, block)]) for i in range(BLOCKS)]
    partner = lax.rem(pencils - me, pencils)

    def rest(u):
        at = pl.ds(1, per - 1)
        return remote(moved.at[u, at], gathered.at[sharer, u, at], b_sem.at[0, u], b_sem.at[1, u], pencil=pencils - 1 - me)

    def zero(u):
        return remote(moved.at[u, 0], gathered.at[sharer, u, 0], b_sem.at[2, u], b_sem.at[3, u], pencil=partner)

    def stay(u):
        return pltpu.make_async_copy(moved.at[u, 0], gathered.at[sharer, u, 0], b_sem.at[4, u])

    plain = swapped(me < 0, (INNER, HALF), 1)
    edge = swapped(me == 0, (INNER, HALF), 1)
    for u in range(share):
        source_loads[u].wait()
        swap = swapped(first + u == 0, (INNER, INNER), 0)
        rows = [dot(swap, sources[u][local, c]).astype(bf16) for c in range(2)]
        for j in range(per):
            turn = edge if j == 0 else plain
            turned = [dot(rows[c][:, j * INNER : (j + 1) * INNER], turn) for c in range(2)]
            moved[u, (per - j) % per] = jnp.concatenate(turned, axis=1)

        if u == 0:
            pl.semaphore_wait(barrier, len(peers))
        rest(u).start()

        @pl.when(partner != me)
        def _(u=u):
            zero(u).start()

        @pl.when(partner == me)
        def _(u=u):
            stay(u).start()

    late_loads = [load(table_ref, tables), load(turns_ref, turns), load(kern_ref, kern),
                  load(back_high_ref, back_high), load(back_low_ref, back_low)]

    for copy in row_loads:
        copy.wait()
    offset = background_ref[member_ref[0]]

    def a_copy(chunk, shift, i):
        return remote(sending.at[chunk, shift, i], landing.at[chunk, shift - 1, i],
                      a_send_sem.at[chunk, shift - 1, i], a_recv_sem.at[chunk, shift - 1, i], pencil=toward(shift))

    for i in range(BLOCKS):
        dens_loads[i].wait()

        def step(b, carry, i=i):
            at = pl.ds(pl.multiple_of(b * 8, 8), 8)
            here = pl.ds(pl.multiple_of(i * block + b * 8, 8), 8)
            got = real_transform([dens[here, n * INNER : (n + 1) * INNER] - offset for n in range(RADIX)])
            pieces[0, at, :INNER] = got[0][0]
            pieces[0, at, INNER:] = got[8][0]
            for s in range(1, 8):
                pieces[s, at, :INNER] = got[s][0]
                pieces[s, at, INNER:] = got[s][1]
            return carry

        lax.fori_loop(0, block // 8, step, 0)

        def part(index, carry, i=i):
            shift, chunk = index // chunks, lax.rem(index, chunks)
            t = lax.rem(me + shift, pencils) * chunks + chunk
            total = None
            for odd in range(2):
                high, low = split_value(pieces[slot_at(2 * t + odd)])
                table_high = row_high[t, 256 * odd : 256 * odd + 256]
                table_low = row_low[t, 256 * odd : 256 * odd + 256]
                term = dot(high, table_high) + dot(low, table_high) + dot(high, table_low)
                total = term if total is None else total + term
            for c in range(2):
                sending[chunk, shift, i, c] = total[:, c * 128 : (c + 1) * 128]
            return carry

        lax.fori_loop(0, pencils * chunks, part, 0)
        for shift in SHIFTS:
            a_copy(0, shift, i).start()

    def start_a(chunk):
        for i in range(BLOCKS):
            for shift in SHIFTS:
                a_copy(chunk, shift, i).start()

    arrivals = [(i, shift) for i in range(BLOCKS) for shift in SHIFTS]

    def wait_a(chunk, which):
        for i, shift in which:
            a_copy(chunk, shift, i).wait_recv()

    for copy in late_loads:
        copy.wait()

    for u in range(share):
        rest(u).wait_recv()

        @pl.when(partner != me)
        def _(u=u):
            zero(u).wait_recv()
            zero(u).wait_send()

        @pl.when(partner == me)
        def _(u=u):
            stay(u).wait()

    own = gathered.at[sharer]
    far = (1 - grp) * 2 + mem
    across = remote(own, own, g_sem.at[0], g_sem.at[1], grp=1 - grp)
    across.start()
    beside = remote(own, own, g_sem.at[2], g_sem.at[3], mem=1 - mem)
    beside.start()
    wait_a(0, arrivals[:AHEAD])
    start_a(1)
    across.wait_recv()
    passed = remote(gathered.at[far], gathered.at[far], g_sem.at[4], g_sem.at[5], mem=1 - mem)
    passed.start()
    beside.wait_recv()
    passed.wait_recv()

    from_lane = lax.broadcasted_iota(jnp.int32, (2 * INNER, lanes), 0)
    to_lane = lax.broadcasted_iota(jnp.int32, (2 * INNER, lanes), 1)
    pick = jnp.where(from_lane == to_lane + jnp.where(to_lane < HALF, 0, HALF), 0.5, 0.0).astype(bf16)
    from_lane, to_lane = from_lane[:INNER], to_lane[:INNER]
    pick_edge = jnp.where((from_lane == HALF) & (to_lane == 0), 0.5, 0.0).astype(bf16)
    mask = (to_lane == 0) & (me == 0)

    def turned(r):
        cos, sin = turns[r, :, 0:1], turns[r, :, 1:2]
        pc, ps = (phase_ref[(me * RADIX + r) * 2 + c] for c in range(2))
        return cos * pc - sin * ps, sin * pc + cos * ps

    def wave(r):
        re, im = spectra[r, :INNER], spectra[r, INNER:]
        c, s = turned(r)
        high, low = split_value(jnp.concatenate([re * c + im * s, im * c - re * s], axis=0))
        return dot(tables[0], high) + dot(tables[0], low) + dot(tables[1], high)

    def finish(chunk, r, got):
        re, im = got[:INNER], got[INNER:]
        rows = pl.ds(pl.multiple_of(r * INNER, INNER), INNER)
        holder, u = r // share, lax.rem(r, share)
        parts = []
        for c in range(2):
            other = [gathered[holder, u, 2 * chunk + j, :, c * HALF : (c + 1) * HALF] for j in range(2)]
            other = jnp.concatenate(other, axis=1)
            mine = dot(kern[local, c, rows, 2 * chunk * INNER : 2 * (chunk + 1) * INNER], pick)
            parts.append(mine + 0.5 * other if c == 0 else mine - 0.5 * other)
        kr, ki = parts
        if chunk == 0:
            other = lax.rem(RADIX - r, RADIX)
            other_rows = pl.ds(pl.multiple_of(other * INNER, INNER), INNER)
            swap = swapped(r == 0, (INNER, INNER), 0)
            edges = []
            for c in range(2):
                mine = dot(kern[local, c, rows, :INNER], pick_edge)
                flipped = dot(swap, kern[local, c, other_rows, :INNER]).astype(bf16)
                flipped = dot(flipped, pick_edge)
                edges.append(mine + flipped if c == 0 else mine - flipped)
            high, low = split_value(waves[other])
            ore = dot(swap, high[:INNER]) + dot(swap, low[:INNER])
            oim = -(dot(swap, high[INNER:]) + dot(swap, low[INNER:]))
            hr = jnp.where(mask, 0.5 * (kr - edges[0]), 0.0)
            hi = jnp.where(mask, 0.5 * (ki - edges[1]), 0.0)
            kr, ki = kr - hr, ki - hi
            sr = re * kr - im * ki + (ore * hr - oim * hi)
            si = re * ki + im * kr + (ore * hi + oim * hr)
        else:
            sr, si = re * kr - im * ki, re * ki + im * kr
        high, low = split_value(jnp.concatenate([sr, si], axis=0))
        got = dot(tables[2], high) + dot(tables[2], low) + dot(tables[3], high)
        re, im = got[:INNER], got[INNER:]
        c, s = turned(r)
        spectra[r, :INNER] = re * c - im * s
        spectra[r, INNER:] = im * c + re * s

    def columns(chunk):
        def forward(b, carry):
            values = []
            for n in range(RADIX):
                j, begin = divmod(n * INNER, part_rows)
                i, begin = divmod(begin, block)
                at = pl.ds(pl.multiple_of(begin + b * 8, 8), 8)
                ref = sending.at[chunk, 0, i] if j == 0 else landing.at[chunk, pencils - j - 1, i]
                values.append((ref[0, at, :], ref[1, at, :]))
            at = pl.ds(pl.multiple_of(b * 8, 8), 8)
            also = pl.ds(pl.multiple_of(INNER + b * 8, 8), 8)
            for r, (re, im) in enumerate(transform(values, -1)):
                spectra[r, at, :] = re
                spectra[r, also, :] = im
            return carry

        lax.fori_loop(0, INNER // 8, forward, 0)

        def early(i, carry):
            for u in range(UNROLL):
                waves[i * UNROLL + u] = wave(i * UNROLL + u)
            return carry

        def late(i, carry):
            for u in range(UNROLL):
                r = i * UNROLL + u
                finish(chunk, r, waves[r] if chunk == 0 else wave(r))
            return carry

        if chunk == 0:
            lax.fori_loop(0, RADIX // UNROLL, early, 0)
        lax.fori_loop(0, RADIX // UNROLL, late, 0)

        def backward(b, carry):
            at = pl.ds(pl.multiple_of(b * 8, 8), 8)
            also = pl.ds(pl.multiple_of(INNER + b * 8, 8), 8)
            values = [(spectra[r, at, :], spectra[r, also, :]) for r in range(RADIX)]
            for n, (re, im) in enumerate(transform(values, 1)):
                shift_depth, begin = divmod(n * INNER, out_rows)
                shift, depth = divmod(shift_depth, depths)
                put = pl.ds(pl.multiple_of(begin + b * 8, 8), 8)
                slot = jnp.where(deep == depth, 0, 1)
                keep[chunk, slot, shift, 0, put, :] = re
                keep[chunk, slot, shift, 1, put, :] = im
            return carry

        lax.fori_loop(0, INNER // 8, backward, 0)

    out_block = out_rows // PARTS

    def x_copy(chunk, j, i):
        at = pl.ds(i * out_block, out_block)
        return remote(keep.at[chunk, 1, j, :, at], other_keep.at[chunk, j, :, at],
                      x_sem.at[0, chunk, j, i], x_sem.at[1, chunk, j, i], depth=1 - deep)

    def c_copy(chunk, j, i):
        at = pl.ds(i * out_block, out_block)
        return remote(keep.at[chunk, 0, j, :, at], fields.at[chunk, j - 1, :, at],
                      c_sem.at[0, chunk, j - 1, i], c_sem.at[1, chunk, j - 1, i], pencil=toward(j))

    def summed(chunk, j, i):
        x_copy(chunk, j, i).wait_recv()
        at = pl.ds(i * out_block, out_block)
        keep[chunk, 0, j, :, at] += other_keep[chunk, j, :, at]

    def gather_field(chunk, shift, i, size=None):
        t = lax.rem(me + pencils - shift, pencils) * chunks + chunk
        size = size or out_block
        at = pl.ds(i * size, size)
        ref = keep.at[chunk, 0, 0] if shift == 0 else fields.at[chunk, shift - 1]
        high, low = split_value(jnp.concatenate([ref[0, at], ref[1, at]], axis=1))
        for odd in range(2):
            r = 2 * t + odd
            half[slot_at(r), at] += dot(high, back_high[r]) + dot(low, back_high[r]) + dot(high, back_low[r])

    half[...] = jnp.zeros_like(half)
    wait_a(0, arrivals[AHEAD:])
    columns(0)
    pairs = [(i, j) for i in range(PARTS) for j in ORDER]
    for i, j in pairs:
        x_copy(0, j, i).start()
    for i, j in pairs:
        summed(0, j, i)
    wait_a(1, arrivals[:BEFORE])
    for i, j in pairs:
        if j:
            c_copy(0, j, i).start()
    wait_a(1, arrivals[BEFORE:])
    columns(1)
    for i, j in pairs:
        x_copy(1, j, i).start()
    for i in range(PARTS):
        gather_field(0, 0, i)
    for i, j in pairs:
        summed(1, j, i)
        if j:
            c_copy(1, j, i).start()
    for i in range(PARTS):
        gather_field(1, 0, i)
    for i, j in pairs:
        if j:
            c_copy(0, j, i).wait_recv()
            gather_field(0, j, i)
    leaving = []
    *ahead, final = [j for j in ORDER if j]
    for i in range(PARTS):
        for j in ahead:
            c_copy(1, j, i).wait_recv()
            gather_field(1, j, i)
        c_copy(1, final, i).wait_recv()
        size = out_block // LEAVE
        for piece in range(i * LEAVE, (i + 1) * LEAVE):
            gather_field(1, final, piece, size)
            at = pl.ds(piece * size, size)
            leaving.append(pltpu.make_async_copy(half.at[:, at], out_ref.at[:, at], local_sem.at[piece]))
            leaving[-1].start()
    for copy in leaving:
        copy.wait()

    for u in range(share):
        rest(u).wait_send()
    across.wait_send()
    beside.wait_send()
    passed.wait_send()
    for chunk in range(chunks):
        for shift in SHIFTS:
            for i in range(BLOCKS):
                a_copy(chunk, shift, i).wait_send()
        for j in ORDER:
            for i in range(PARTS):
                x_copy(chunk, j, i).wait_send()
                if j:
                    c_copy(chunk, j, i).wait_send()


def last_kernel(in_ref, out_ref, half, done, sem):
    block = half.shape[1] // LAST

    def copies(i):
        at = pl.ds(i * block, block)
        return (pltpu.make_async_copy(in_ref.at[:, at], half.at[:, at], sem.at[0, i]),
                pltpu.make_async_copy(done.at[at], out_ref.at[0, at], sem.at[1, i]))

    def last(b, carry):
        at = pl.ds(pl.multiple_of(b * STEP, STEP), STEP)
        values = [(half[0, at, :INNER], None)]
        for s in range(1, 8):
            values.append((half[s, at, :INNER], half[s, at, INNER:]))
        values.append((half[0, at, INNER:], None))
        for n, value in enumerate(real_inverse(values)):
            done[at, n * INNER : (n + 1) * INNER] = value
        return carry

    for i in range(LAST):
        copies(i)[0].start()
    for i in range(LAST):
        copies(i)[0].wait()
        lax.fori_loop(i * block // STEP, (i + 1) * block // STEP, last, 0)
        copies(i)[1].start()
    for i in range(LAST):
        copies(i)[1].wait()


STEP = 16
LAST = 8
SHIFTS = (2, 1, 3)
ORDER = (2, 1, 0, 3)
UNROLL = 4
AHEAD = 9
BEFORE = 12
PARTS = 1
LEAVE = 4


def params(**more):
    return pltpu.CompilerParams(vmem_limit_bytes=48 * 1024 * 1024, **more)


def wide_body(density, background, member_ids, layer_kernel, kernel_spectra):
    pencils = lax.axis_size("pencil")
    depths = lax.axis_size("depth")
    sharers = lax.axis_size("grp") * lax.axis_size("mem")
    pencil = lax.axis_index("pencil")
    per = RADIX // pencils
    width = min(per, 2)
    chunks = per // width
    lanes = width * HALF
    part_rows = density.shape[2]
    out_rows = part_rows // depths
    vmem = pl.BlockSpec(memory_space=pltpu.VMEM)
    smem = pl.BlockSpec(memory_space=pltpu.SMEM)

    kern_count = kernel_spectra.shape[0]
    local = layer_kernel[0] - lax.axis_index("depth") * kern_count
    share = RADIX // sharers
    first = lax.axis_index(("grp", "mem")) * share
    groups = [1] if per == 1 else [1, per - 1]
    moved = pl.pallas_call(
        functools.partial(mirror_kernel, share),
        grid_spec=pltpu.PrefetchScalarGridSpec(
            num_scalar_prefetch=1,
            grid=(1,),
            in_specs=[
                pl.BlockSpec(
                    (None, 2, INNER, per * INNER),
                    lambda i, w, u=u: (w[0], 0, lax.rem(RADIX - w[1] - u, RADIX), 0),
                )
                for u in range(share)
            ],
            out_specs=[pl.BlockSpec((g, share, INNER, INNER), lambda i, w: (0, 0, 0, 0)) for g in groups],
        ),
        out_shape=[jax.ShapeDtypeStruct((g, share, INNER, INNER), f32) for g in groups],
        compiler_params=params(),
        cost_estimate=pl.CostEstimate(flops=1 << 20, bytes_accessed=2 << 20, transcendentals=0),
    )(jnp.stack([local, first, pencil]), *[kernel_spectra] * share)
    mirrored = lax.ppermute(moved[0], "pencil", [(p, (pencils - p) % pencils) for p in range(pencils)])
    if per > 1:
        rest = lax.ppermute(moved[1], "pencil", [(p, pencils - 1 - p) for p in range(pencils)])

    offset = lax.dynamic_index_in_dim(background[:, 0], member_ids[0], 0, keepdims=True)
    row_high, row_low = halves(row_tables())
    block = min(part_rows, 128)
    sent = pl.pallas_call(
        functools.partial(rows_kernel, pencils, width),
        grid=(part_rows // block,),
        in_specs=[
            smem,
            pl.BlockSpec((None, None, block, LENGTH), lambda i: (0, 0, i, 0)),
            pl.BlockSpec((8, 512, 256), lambda i: (0, 0, 0)),
            pl.BlockSpec((8, 512, 256), lambda i: (0, 0, 0)),
        ],
        out_specs=[pl.BlockSpec((pencils, 2, block, lanes), lambda i: (0, 0, i, 0))] * chunks,
        out_shape=[jax.ShapeDtypeStruct((pencils, 2, part_rows, lanes), f32)] * chunks,
        scratch_shapes=[pltpu.VMEM((8, block, 256), f32)],
        compiler_params=params(),
        cost_estimate=pl.CostEstimate(flops=6 * part_rows * 2 * LENGTH * 512, bytes_accessed=12 << 20, transcendentals=0),
    )(offset, density, row_high, row_low)
    arrived = [lax.all_to_all(part, "pencil", 0, 0, tiled=True) for part in sent]

    sign = jnp.array([0.5, -0.5], f32)
    edge = lax.dynamic_slice(kernel_spectra, (local, 0, 0, HALF), (1, 2, LENGTH, 1))
    edge = edge.reshape(2, RADIX, INNER).astype(f32)
    flipped = jnp.concatenate([edge[:, :1], edge[:, :0:-1]], axis=1)[..., ::-1]
    flipped = jnp.concatenate([jnp.roll(flipped[:, :1], 1, axis=2), flipped[:, 1:]], axis=1)
    edge = 0.5 * edge + sign.reshape(2, 1, 1) * flipped
    edge = jnp.where(lax.broadcasted_iota(jnp.int32, (lanes,), 0) == 0, edge[..., None], 0.0)

    if per > 1:
        mirrored = jnp.concatenate([mirrored, rest], axis=0)
    mirrored, edge, _ = lax.optimization_barrier((mirrored, edge, sent[0]))
    mirrored = lax.all_gather(mirrored, ("grp", "mem"), axis=0)

    column, column_turns = column_tables()
    column_turns = jnp.asarray(column_turns)
    tables = jnp.stack(halves(column) + halves(column.T))
    two = depths == 2
    mine = lax.axis_index("depth") if two else jnp.int32(0)
    where = jnp.stack([mine, local, pencil])
    fields = []
    before = None
    for k in range(chunks):
        special = k == 0
        steps = sharers

        def early(i, special=special):
            return jnp.minimum(i, steps - 1) if special else i

        def late(i, special=special):
            return jnp.maximum(i - steps, 0) if special else i

        here = arrived[k]
        if before is not None:
            here, before = lax.optimization_barrier((here, before))
            fields.append(lax.all_to_all(before, "pencil", 0, 0, tiled=True))
        edge_block = (2, share, INNER, lanes) if special else (2, 1, 8, lanes)
        out = pl.pallas_call(
            functools.partial(columns_kernel, special),
            grid_spec=pltpu.PrefetchScalarGridSpec(
                num_scalar_prefetch=1,
                grid=(2 * steps if special else steps,),
                in_specs=[
                    pl.BlockSpec((pencils, 2, part_rows, lanes), lambda i, w: (0, 0, 0, 0)),
                    pl.BlockSpec(
                        (None, 2, share * INNER, width * INNER), lambda i, w, k=k, late=late: (w[1], 0, late(i), k)
                    ),
                    pl.BlockSpec(
                        (None, width, share, INNER, INNER), lambda i, w, k=k, late=late: (late(i), k, 0, 0, 0)
                    ),
                    pl.BlockSpec(
                        edge_block,
                        (lambda i, w, late=late: (0, late(i), 0, 0)) if special else (lambda i, w: (0, 0, 0, 0)),
                    ),
                ]
                + [pl.BlockSpec((share, INNER, INNER), lambda i, w, early=early: (early(i), 0, 0))]
                + [pl.BlockSpec((share, INNER, INNER), lambda i, w, late=late: (late(i), 0, 0))]
                + [pl.BlockSpec((4, 256, 256), lambda i, w: (0, 0, 0))],
                out_specs=pl.BlockSpec((depths, pencils, 2, out_rows, lanes), lambda i, w: (0, 0, 0, 0, 0)),
                scratch_shapes=[
                    pltpu.VMEM((RADIX, 256, lanes), f32),
                    pltpu.VMEM((RADIX if special else 1, 256, lanes), f32),
                ],
            ),
            out_shape=jax.ShapeDtypeStruct((depths, pencils, 2, out_rows, lanes), f32),
            compiler_params=params(),
            cost_estimate=pl.CostEstimate(
                flops=12 * RADIX * 256 * 256 * lanes, bytes_accessed=16 << 20, transcendentals=0
            ),
        )(where, here, kernel_spectra, mirrored, edge, column_turns, column_turns, tables)
        if two:
            before = out[0] + lax.ppermute(out[1], "depth", [(0, 1), (1, 0)])
        else:
            before = lax.psum_scatter(out, "depth", scatter_dimension=0, tiled=False)
    fields.append(lax.all_to_all(before, "pencil", 0, 0, tiled=True))

    back_high, back_low = halves(inverse_row_tables())
    return pl.pallas_call(
        functools.partial(fields_kernel, pencils, width, [1] * chunks),
        in_specs=[vmem] * (len(fields) + 2),
        out_specs=vmem,
        out_shape=jax.ShapeDtypeStruct((1, out_rows, LENGTH), f32),
        scratch_shapes=[pltpu.VMEM((8, out_rows, 256), f32)],
        compiler_params=params(),
        cost_estimate=pl.CostEstimate(flops=6 * out_rows * 2 * LENGTH * 512, bytes_accessed=8 << 20, transcendentals=0),
    )(*fields, back_high, back_low)


def fused_body(density, background, member_ids, layer_kernel, kernel_spectra):
    pencils = lax.axis_size("pencil")
    depths = lax.axis_size("depth")
    sharers = lax.axis_size("grp") * lax.axis_size("mem")
    per = RADIX // pencils
    chunks = per // 2
    lanes = 2 * HALF
    part_rows = density.shape[2]
    out_rows = part_rows // depths
    share = RADIX // sharers
    smem = pl.BlockSpec(memory_space=pltpu.SMEM)
    anywhere = pl.BlockSpec(memory_space=pl.ANY)

    angles = 2 * np.pi * np.arange(pencils)[:, None] * np.arange(RADIX)[None, :] / pencils
    phases = jnp.asarray(np.stack([np.cos(angles), np.sin(angles)], axis=-1).round(15).reshape(-1), f32)
    row_high, row_low = halves(row_tables())
    where = [0 if r == 8 else min(r, RADIX - r) for r in range(RADIX)], [int(r >= 8) for r in range(RADIX)]
    back_high, back_low = halves(inverse_row_tables().reshape(8, 2, 256, 256)[where])
    column, turns = column_tables()
    tables = jnp.stack(halves(column) + halves(column.T))
    turns = jnp.asarray(turns)
    dma = pltpu.SemaphoreType.DMA
    half = pl.pallas_call(
        functools.partial(fused_kernel, pencils, depths),
        in_specs=[smem] * 4 + [anywhere] * 8,
        out_specs=anywhere,
        out_shape=jax.ShapeDtypeStruct((8, out_rows, 256), f32),
        scratch_shapes=[
            pltpu.VMEM((part_rows, LENGTH), f32),
            [pltpu.VMEM((kernel_spectra.shape[0], 2, INNER, per * INNER), bf16)] * share,
            pltpu.VMEM(kernel_spectra.shape, bf16),
            pltpu.VMEM(row_high.shape, bf16),
            pltpu.VMEM(row_low.shape, bf16),
            pltpu.VMEM(back_high.shape, bf16),
            pltpu.VMEM(back_low.shape, bf16),
            pltpu.VMEM(tables.shape, bf16),
            pltpu.VMEM(turns.shape, f32),
            pltpu.VMEM((8, part_rows // BLOCKS, 256), f32),
            pltpu.VMEM((chunks, pencils, BLOCKS, 2, part_rows // BLOCKS, lanes), f32),
            pltpu.VMEM((chunks, pencils - 1, BLOCKS, 2, part_rows // BLOCKS, lanes), f32),
            pltpu.VMEM((share, per, INNER, INNER), f32),
            pltpu.VMEM((sharers, share, per, INNER, INNER), f32),
            pltpu.VMEM((RADIX, 256, lanes), f32),
            pltpu.VMEM((RADIX, 256, lanes), f32),
            pltpu.VMEM((chunks, 2, pencils, 2, out_rows, lanes), f32),
            pltpu.VMEM((chunks, pencils, 2, out_rows, lanes), f32),
            pltpu.VMEM((chunks, pencils - 1, 2, out_rows, lanes), f32),
            pltpu.VMEM((8, out_rows, 256), f32),
            dma((share + BLOCKS + 7,)),
            dma((5, share)),
            dma((6,)),
            dma((chunks, pencils - 1, BLOCKS)),
            dma((chunks, pencils - 1, BLOCKS)),
            dma((2, chunks, pencils, PARTS)),
            dma((2, chunks, pencils - 1, PARTS)),
        ],
        compiler_params=pltpu.CompilerParams(
            vmem_limit_bytes=60 * 1024 * 1024, collective_id=0, has_side_effects=True
        ),
    )(background.reshape(-1), member_ids, layer_kernel, phases, density, kernel_spectra, row_high, row_low, back_high, back_low, tables, turns)
    return pl.pallas_call(
        last_kernel,
        in_specs=[anywhere],
        out_specs=anywhere,
        out_shape=jax.ShapeDtypeStruct((1, out_rows, LENGTH), f32),
        scratch_shapes=[
            pltpu.VMEM((8, out_rows, 256), f32),
            pltpu.VMEM((out_rows, LENGTH), f32),
            dma((2, LAST)),
        ],
        compiler_params=pltpu.CompilerParams(vmem_limit_bytes=60 * 1024 * 1024),
    )(half)


def body(density, background, member_ids, layer_kernel, kernel_spectra):
    sizes = tuple(lax.axis_size(name) for name in ("grp", "pencil", "depth", "mem"))
    plan = fused_body if sizes == (2, 4, 2, 2) else wide_body
    return plan(density, background, member_ids, layer_kernel, kernel_spectra)


def solution(mesh):
    placed = (
        P(("grp", "mem"), "depth", "pencil", None),
        P(None, "depth"),
        P(("grp", "mem")),
        P("depth"),
        P("depth", None, None, "pencil"),
    )
    return jax.shard_map(
        body,
        mesh=mesh,
        in_specs=placed,
        out_specs=P(("grp", "mem"), ("pencil", "depth"), None),
        check_vma=False,
    )
```
